32 devices in a mesh: fsdp: 32 (over z, y, x, core).
Axes of the slice: x: 2, y: 2, z: 4, core: 2. Of those that a mesh axis runs over, the one named last changes fastest.
Arguments:
- tokens: bfloat16 [8192, 768], P('fsdp'), may hold values from -6 to 6
- w_qkv: bfloat16 [768, 2304], P(None, 'fsdp'), may hold values from -0.21875 to 0.21875
- w_out: bfloat16 [768, 768], P(None, 'fsdp'), may hold values from -0.625 to 0.625
- w_up: bfloat16 [768, 2304], P(None, 'fsdp'), may hold values from -0.21875 to 0.21875
- w_down: bfloat16 [1152, 768], P(None, 'fsdp'), may hold values from -0.1875 to 0.1875
- gain_attn: bfloat16 [768], P('fsdp'), may hold values from 0.5 to 1.5
- gain_mlp: bfloat16 [768], P('fsdp'), may hold values from 0.5 to 1.5
- cotangent: bfloat16 [8192, 768], P('fsdp'), may hold values from -6 to 6
- block_counts: int32 [32], replicated, may hold values from 1 to 2, as said below
- seq_lengths: int32 [4], replicated, may hold values from 1024 to 2048, as said below
Outputs:
- block_out: bfloat16 [8192, 768], P('fsdp')
- tokens_grad: float32 [8192, 768], P('fsdp')
- w_qkv_grad: float32 [768, 2304], P(None, 'fsdp')
- w_out_grad: float32 [768, 768], P(None, 'fsdp')
- w_up_grad: float32 [768, 2304], P(None, 'fsdp')
- w_down_grad: float32 [1152, 768], P(None, 'fsdp')
- gain_attn_grad: float32 [768], P('fsdp')
- gain_mlp_grad: float32 [768], P('fsdp')
The draws below stay inside these ranges and needn't reach their ends.
Inputs may be any that keep to these rules, and one draw needn't show every extreme that they name: `block_counts`: each device holds 1 to 2 blocks, 48 in all; some device holds 2. `seq_lengths`: the lengths add up to 6144; both 1024 and 2048 occur.
All inputs are finite; a program needn't handle non-finite values.
Results may differ from the reference program's by a relative error of at most 0.015.
Values may be sent and summed in bfloat16 or wider, within the bound.
No kernel may reach another device: no remote copies, remote signals or barrier semaphores. Data moves between devices by JAX's collectives and lax.ppermute only.
A program may use at most 128 MiB of HBM per device.

```python
import math
import jax
import jax.numpy as jnp
from jax import lax

D = 768
HEADS = 12
HD = 64
FF = 1152
BLK = 128
WIN = 64
SEQ_MIN = 1024
CAP = 2
NPAIR = 2
NSEQ = 4
NBLK = 48
TOTAL = 6144
SLOTS = 8192
N_FSDP = 32


def draw_block_counts(key, part):
    key = jax.random.fold_in(key, 11)
    ranking = jax.random.permutation(key, N_FSDP).astype(jnp.int32)
    extra = NBLK - N_FSDP
    return (1 + jnp.clip(extra - ranking * (CAP - 1), 0, CAP - 1)).astype(jnp.int32)


def draw_seq_lengths(key, part):
    key = jax.random.fold_in(key, 23)
    key_shift, key_order = jax.random.split(key)
    shifts = jax.random.randint(key_shift, (NPAIR,), 0, SEQ_MIN + 1)
    shifts = shifts.at[0].set(SEQ_MIN)
    paired = jnp.stack([SEQ_MIN + shifts, 2 * SEQ_MIN - shifts], axis=1).reshape(NSEQ)
    return jax.random.permutation(key_order, paired).astype(jnp.int32)


def spiked(array, key, source, target, blocks, factor):
    def block_of(dim):
        return (jnp.arange(array.shape[dim]) // (array.shape[dim] // blocks)).reshape((-1,) + (1,) * (array.ndim - 1 - dim))

    one_side = jax.random.permutation(key, blocks)[block_of(target)]
    far = (block_of(target) + blocks // 2) % blocks
    return jnp.where((block_of(source) == one_side) | (block_of(source) == far), factor * array, array)


def steps_of(own_key, shape, cuts, low, largest):
    level, own = 1.0, jax.random.fold_in(own_key, 6)
    for dim, shards_of in cuts:
        heights = jnp.exp(jax.random.uniform(jax.random.fold_in(own, dim), (shards_of,), jnp.float32, low / len(cuts), largest / len(cuts)))
        level = level * jnp.repeat(heights, shape[dim] // shards_of).reshape([-1 if axis == dim else 1 for axis in range(len(shape))])
    return level


def noise(key, dims, scale, limit, cuts=(), kind=jnp.bfloat16):
    level = steps_of(key, dims, cuts, -0.22, 0.18) if cuts else 1.0
    values = jax.random.normal(key, dims, jnp.float32) * scale * level
    return jnp.minimum(jnp.maximum(values, -limit), limit).astype(kind)


def gaussian_with(rng, extent, scale, bound, cuts, heavy, held_as=jnp.bfloat16):
    values = scale * jax.random.normal(rng, extent, jnp.float32)
    if cuts:
        values = values * steps_of(rng, extent, cuts, -0.22, 0.18)
    return jnp.clip(spiked(values, jax.random.fold_in(rng, 3), *heavy), -bound, bound).astype(held_as)


def setup_inputs(seed: int = 0) -> dict:
    splits = jax.random.split(jax.random.key(seed), 11)
    tokens = noise(splits[0], (SLOTS, D), 1.0, 6.0, ((0, 32),))
    w_qkv = noise(splits[1], (D, 3 * D), D ** -0.5, 0.21875, ((1, 32),))
    w_out = noise(splits[2], (D, D), (D // 8) ** -0.5, 0.625, ((1, 32),))
    w_up = noise(splits[3], (D, 2 * FF), D ** -0.5, 0.21875, ((1, 32),))
    w_down = noise(splits[4], (FF, D), FF ** -0.5, 0.1875, ((1, 32),))
    gain_attn = jnp.clip(1.0 + 0.1 * jax.random.normal(splits[5], (D,), jnp.float32), 0.5, 1.5).astype(jnp.bfloat16)
    gain_mlp = jnp.clip(1.0 + 0.1 * jax.random.normal(splits[6], (D,), jnp.float32), 0.5, 1.5).astype(jnp.bfloat16)
    cotangent = gaussian_with(splits[7], (SLOTS, D), 1.0, 6.0, ((0, 32),), (0, 1, 32, 2.75))
    block_counts = draw_block_counts(jax.random.fold_in(splits[10], 71), 0)
    seq_lengths = draw_seq_lengths(jax.random.fold_in(splits[10], 71), 0)
    return {"tokens": tokens, "w_qkv": w_qkv, "w_out": w_out, "w_up": w_up, "w_down": w_down, "gain_attn": gain_attn, "gain_mlp": gain_mlp, "cotangent": cotangent, "block_counts": block_counts, "seq_lengths": seq_lengths}


EPSILON = 1e-05
MASKED = -1e+30
HIGHEST = lax.Precision.HIGHEST

@jax.custom_vjp
def low(v):
    return lax.optimization_barrier(v.astype(jnp.bfloat16)).astype(jnp.float32)

@jax.custom_vjp
def low_back(v):
    return v

def low_keep(v):
    return (low(v), None)

def low_pass(kept, grad):
    return (grad,)

def back_keep(v):
    return (v, None)

def back_low(kept, grad):
    return (low(grad),)
low.defvjp(low_keep, low_pass)
low_back.defvjp(back_keep, back_low)

def exact_product(left, right):
    return jnp.dot(left, right, precision=HIGHEST, preferred_element_type=jnp.float32)

def normalized(values, gain):
    center = values - lax.optimization_barrier(jnp.mean(values, axis=-1, keepdims=True))
    spread = lax.optimization_barrier(jnp.mean(center * center, axis=-1, keepdims=True))
    return center * lax.rsqrt(spread + EPSILON) * gain

def sequence_places(places, lengths):
    ends = jnp.cumsum(lengths).astype(jnp.int32)
    starts = ends - lengths
    segment = lax.optimization_barrier(jnp.sum((places[:, None] >= ends[None, :]).astype(jnp.int32), axis=1))
    picked = segment[:, None] == jnp.arange(lengths.shape[0], dtype=jnp.int32)[None, :]
    start = lax.optimization_barrier(jnp.sum(jnp.where(picked, starts[None, :], 0), axis=1)).astype(jnp.int32)
    return (segment, places - start)

def rotary_tables(position):
    half = HD // 2
    freq = jnp.power(10000.0, -(jnp.arange(half, dtype=jnp.float32) * (2.0 / HD)))
    angle = position.astype(jnp.float32)[:, None] * freq[None, :]
    angle = jnp.concatenate([angle, angle], axis=1)[:, None, :]
    return (jnp.cos(angle), jnp.sin(angle))

def rotate_heads(values, cosine, sine):
    half = HD // 2
    turned = jnp.concatenate([-values[..., half:], values[..., :half]], axis=-1)
    return values * cosine + turned * sine

def make_slabs(values, blocks):
    tiles = values.reshape(blocks, SEQ_MIN, values.shape[1])
    zeros = jnp.zeros((1, WIN, values.shape[1]), values.dtype)
    left = jnp.concatenate([zeros, tiles[:-1, SEQ_MIN - WIN:]], axis=0)
    right = jnp.concatenate([tiles[1:, :WIN], zeros], axis=0)
    return jnp.concatenate([left, tiles, right], axis=1)

def attend_block(pieces):
    query, keys, values, query_seg, query_place, key_seg, key_place, key_valid = pieces
    rows = query.shape[0]
    query_heads = query.reshape(rows, HEADS, HD)
    key_heads = keys.reshape(-1, HEADS, HD)
    value_heads = values.reshape(-1, HEADS, HD)
    scores = jnp.einsum('qhd,khd->hqk', query_heads, key_heads, precision=HIGHEST) * (1.0 / math.sqrt(HD))
    allowed = key_valid[None, :] & (query_seg[:, None] == key_seg[None, :]) & (jnp.abs(query_place[:, None] - key_place[None, :]) <= WIN)
    scores = low_back(jnp.where(allowed[None], scores, MASKED))
    row_top = lax.optimization_barrier(jnp.max(scores, axis=-1, keepdims=True))
    expos = jnp.exp(scores - row_top)
    probs = expos / lax.optimization_barrier(jnp.sum(expos, axis=-1, keepdims=True))
    mixed = jnp.einsum('hqk,khd->qhd', low(probs), value_heads, precision=HIGHEST)
    return mixed.reshape(rows, D)

def reference(tokens, w_qkv, w_out, w_up, w_down, gain_attn, gain_mlp, cotangent, block_counts, seq_lengths):
    slot_count = CAP * BLK
    flat = jnp.arange(N_FSDP * slot_count, dtype=jnp.int32)
    owner = flat // slot_count
    within = flat - owner * slot_count
    firsts = (jnp.cumsum(block_counts) - block_counts).astype(jnp.int32)
    live_slots = within < block_counts[owner] * BLK
    place = firsts[owner] * BLK + within
    target = jnp.where(live_slots, place, TOTAL)
    source = jnp.zeros((TOTAL,), jnp.int32).at[target].set(flat, mode='drop')
    stream_tokens = tokens.astype(jnp.float32)[source]
    stream_grad = cotangent.astype(jnp.float32)[source]
    places = jnp.arange(TOTAL, dtype=jnp.int32)
    segment, position = sequence_places(places, seq_lengths)
    cosine, sine = rotary_tables(position)
    blocks = TOTAL // SEQ_MIN
    span = SEQ_MIN + 2 * WIN
    key_place = jnp.arange(blocks, dtype=jnp.int32)[:, None] * SEQ_MIN - WIN + jnp.arange(span, dtype=jnp.int32)[None, :]
    key_seg, unused = sequence_places(key_place.reshape(-1), seq_lengths)
    key_seg = key_seg.reshape(blocks, span)
    key_valid = (key_place >= 0) & (key_place < TOTAL)
    query_seg = segment.reshape(blocks, SEQ_MIN)
    query_place = places.reshape(blocks, SEQ_MIN)

    def forward(stream, weight_qkv, weight_out, weight_up, weight_down, norm_attn, norm_mlp):
        first_in = low(normalized(stream, norm_attn))
        joined = low_back(exact_product(first_in, weight_qkv))
        query = joined[:, :D].reshape(-1, HEADS, HD)
        keys = joined[:, D:2 * D].reshape(-1, HEADS, HD)
        query = low(rotate_heads(query, cosine, sine)).reshape(-1, D)
        keys = low(rotate_heads(keys, cosine, sine)).reshape(-1, D)
        values = low(joined[:, 2 * D:])
        mixed = lax.map(jax.checkpoint(attend_block), (query.reshape(blocks, SEQ_MIN, D), make_slabs(keys, blocks), make_slabs(values, blocks), query_seg, query_place, key_seg, key_place, key_valid))
        mixed = low(low_back(mixed.reshape(-1, D)))
        after_attn = stream + low_back(exact_product(mixed, weight_out))
        second_in = low(normalized(after_attn, norm_mlp))
        projected = low_back(exact_product(second_in, weight_up))
        hidden = low(jax.nn.gelu(projected[:, :FF], approximate=False) * projected[:, FF:])
        return after_attn + low_back(exact_product(hidden, weight_down))
    params = tuple((item.astype(jnp.float32) for item in (w_qkv, w_out, w_up, w_down, gain_attn, gain_mlp)))
    result, pull = jax.vjp(forward, stream_tokens, *params)
    grads = pull(stream_grad)
    back_place = jnp.minimum(place, TOTAL - 1)
    block_out = jnp.where(live_slots[:, None], result[back_place], 0.0).astype(jnp.bfloat16)
    tokens_grad = jnp.where(live_slots[:, None], grads[0][back_place], 0.0).astype(jnp.float32)
    return (block_out, tokens_grad, grads[1], grads[2], grads[3], grads[4], grads[5], grads[6])
```

```python
import math

import jax
import jax.numpy as jnp
from jax import lax
from jax.sharding import PartitionSpec as P

D = 768
HEADS = 12
HD = 64
FF = 1152
BLK = 128
WIN = 64


EPSILON = 1e-05
MASKED = -1e30


def with_halo(shard, sides, width):
    for axis, dim in sides:
        peers, length = (lax.axis_size(axis), shard.shape[dim])
        up = [(i, (i + 1) % peers) for i in range(peers - 1)]
        down = [(j, i) for i, j in up]
        last = lax.slice_in_dim(shard, length - width, length, axis=dim)
        initial = lax.slice_in_dim(shard, 0, width, axis=dim)
        before = lax.ppermute(last, axis, up)
        after = lax.ppermute(initial, axis, down)
        shard = jnp.concatenate([before, shard, after], axis=dim)
    return shard


def norm_parts(values):
    center = values - jnp.mean(values, axis=-1, keepdims=True)
    factor = lax.rsqrt(jnp.mean(center * center, axis=-1, keepdims=True) + EPSILON)
    return (center * factor, factor)


def norm_back(grad_normed, normed, factor):
    return factor * (
        grad_normed
        - jnp.mean(grad_normed, axis=-1, keepdims=True)
        - normed * jnp.mean(grad_normed * normed, axis=-1, keepdims=True)
    )


def sequence_places(places, lengths):
    ends = jnp.cumsum(lengths)
    starts = ends - lengths
    segment = jnp.sum((places[:, None] >= ends[None, :]).astype(jnp.int32), axis=1)
    picked = segment[:, None] == jnp.arange(lengths.shape[0], dtype=jnp.int32)[None, :]
    start = jnp.sum(jnp.where(picked, starts[None, :], 0), axis=1)
    return (segment, places - start)


def rotary_tables(position):
    half = HD // 2
    freq = jnp.power(10000.0, -(jnp.arange(half, dtype=jnp.float32) * (2.0 / HD)))
    angle = position.astype(jnp.float32)[:, None] * freq[None, :]
    angle = jnp.concatenate([angle, angle], axis=1)[:, None, :]
    return (jnp.cos(angle), jnp.sin(angle))


def rotate_heads(values, cosine, sine):
    half = HD // 2
    turned = jnp.concatenate([-values[..., half:], values[..., :half]], axis=-1)
    return values * cosine + turned * sine


def rotate_back(grads, cosine, sine):
    half = HD // 2
    spun = grads * sine
    return grads * cosine + jnp.concatenate([spun[..., half:], -spun[..., :half]], axis=-1)


def rows_product(left, right):
    return lax.dot_general(
        left, right, (((0,), (0,)), ((), ())), preferred_element_type=jnp.float32
    )


def cols_product(left, right):
    return lax.dot_general(
        left, right, (((1,), (1,)), ((), ())), preferred_element_type=jnp.float32
    )


def exact_gelu(values):
    return jax.nn.gelu(values, approximate=False)


def masked_scores(query, key_heads, allowed, score_scale):
    raw_scores = (
        jnp.einsum("qhd,khd->hqk", query, key_heads, preferred_element_type=jnp.float32)
        * score_scale
    )
    return jnp.where(allowed[None], raw_scores, MASKED)


def column_term(grad_side, data_side):
    return rows_product(grad_side, data_side)


def permute(values, pairs):
    return lax.ppermute(values, "fsdp", pairs)


def links():
    sibling = [(i, i ^ 1) for i in range(32)]
    near = [(i, i ^ (2 if i & 1 else 4)) for i in range(32)]
    far = [(i, i ^ (4 if i & 1 else 2)) for i in range(32)]
    line = [[(i, (i + 8 * k) % 32) for i in range(32)] for k in range(4)]
    return (sibling, near, far, line)


def chip_place():
    me = lax.axis_index("fsdp")
    return (me // 8, (me // 4) % 2, (me // 2) % 2, me % 2)


def gather_slots(stream):
    z, y, x, core = chip_place()
    slots = []
    for chip in range(16):
        zr = (z - chip // 4) % 4
        yr = (y + (chip // 2) % 2) % 2
        xr = (x + chip % 2) % 2
        first, second = (yr, xr) if stream == 0 else (xr, yr)
        slots.append(second * 8 + first * 4 + zr)
    return slots


def gather_rows(rows):
    size = lax.axis_size("fsdp")
    if size != 32:
        return lax.all_gather(rows, "fsdp", axis=0, tiled=False)
    half = rows.shape[1] // 2
    count = rows.shape[0]
    sibling, near, far, line = links()
    core = lax.axis_index("fsdp") % 2
    low, high = rows[:, :half], rows[:, half:]
    keep = jnp.where(core == 0, low, high)
    got = permute(jnp.where(core == 0, high, low), sibling)
    block = jnp.where(
        core == 0, jnp.concatenate([keep, got]), jnp.concatenate([got, keep])
    )[None]
    held = jnp.concatenate([block] + [permute(block, line[k]) for k in (1, 2, 3)])
    held = jnp.concatenate([held, permute(held, near)])
    held = jnp.concatenate([held, permute(held, far)])
    other = permute(held, sibling)
    streams = (jnp.where(core == 0, held, other), jnp.where(core == 0, other, held))
    sides = []
    for stream in (0, 1):
        picked = [
            lax.dynamic_slice_in_dim(streams[stream], slot, 1, 0)
            for slot in gather_slots(stream)
        ]
        sides.append(jnp.concatenate(picked))
    return jnp.concatenate(sides, axis=-1).reshape(32, count, 2 * half)


def scatter_order(stream):
    z, y, x, core = chip_place()
    order = []
    for slot in range(16):
        first, second = 1 - slot // 8, 1 - (slot // 4) % 2
        yr, xr = (first, second) if stream == 0 else (second, first)
        zz = (z + slot % 4 + 1) % 4
        order.append(zz * 4 + ((y + yr) % 2) * 2 + (x + xr) % 2)
    return order


def scatter_rows(terms):
    size = lax.axis_size("fsdp")
    if size != 32:
        return lax.psum_scatter(terms, "fsdp", scatter_dimension=0, tiled=False).astype(
            jnp.float32
        )
    half = terms.shape[2] // 2
    count = terms.shape[1]
    sibling, near, far, line = links()
    core = lax.axis_index("fsdp") % 2
    chips = terms.reshape(16, 2 * count, 2 * half)

    def stream_terms(stream):
        lanes = chips[:, :, stream * half : (stream + 1) * half]
        return jnp.concatenate(
            [lax.dynamic_slice_in_dim(lanes, chip, 1, 0) for chip in scatter_order(stream)]
        )

    low, high = stream_terms(0), stream_terms(1)
    keep = jnp.where(core == 0, low, high)
    total = keep + permute(jnp.where(core == 0, high, low), sibling)
    total = total[8:] + permute(total[:8], near)
    total = total[4:] + permute(total[:4], far)
    share = total[3].astype(jnp.float32)
    for k in range(3):
        share = share + permute(total[k], line[k + 1]).astype(jnp.float32)
    mine = jnp.where(core == 0, share[:count], share[count:])
    got = permute(jnp.where(core == 0, share[count:], share[:count]), sibling)
    return jnp.where(
        core == 0, jnp.concatenate([mine, got], axis=1), jnp.concatenate([got, mine], axis=1)
    )


def fold_pad(shard):
    count = shard.shape[-2]
    rest = shard[..., D:]
    half = (count + 1) // 2
    left, right = rest[..., :half, :], rest[..., half:, :]
    spare = [(0, 0)] * (shard.ndim - 2) + [(0, 2 * half - count), (0, 0)]
    rest = jnp.concatenate([left, jnp.pad(right, spare)], axis=-1)
    return jnp.concatenate([shard[..., :D], rest], axis=-2)


def unfold_pad(packed, count):
    half, lanes = (count + 1) // 2, FF - D
    rest = packed[..., count : count + half, :]
    rest = jnp.concatenate([rest[..., :lanes], rest[..., lanes:]], axis=-2)[..., :count, :]
    return jnp.concatenate([packed[..., :count, :], rest], axis=-1)


def body(
    tokens, w_qkv, w_out, w_up, w_down, gain_attn, gain_mlp, cotangent, block_counts, seq_lengths
):
    slot_total = tokens.shape[0]
    score_scale = 1.0 / math.sqrt(HD)
    device_index = lax.axis_index("fsdp")
    block_count = lax.dynamic_index_in_dim(block_counts, device_index, keepdims=False)
    device_ids = jnp.arange(block_counts.shape[0], dtype=jnp.int32)
    first_place = jnp.sum(jnp.where(device_ids < device_index, block_counts, 0)) * BLK
    live_rows = block_count * BLK
    stream_total = jnp.sum(block_counts) * BLK
    slot_index = jnp.arange(slot_total, dtype=jnp.int32)
    live_slots = slot_index < live_rows
    rim_offsets = jnp.arange(WIN, dtype=jnp.int32)
    query_place = first_place + slot_index
    before_place = first_place - WIN + rim_offsets
    after_place = first_place + live_rows + rim_offsets
    key_place = jnp.concatenate([before_place, query_place, after_place])
    key_live = jnp.concatenate([before_place >= 0, live_slots, after_place < stream_total])
    key_slot = jnp.concatenate([rim_offsets * 0 - 1, slot_index, rim_offsets * 0 - 1])
    query_seg, query_pos = sequence_places(query_place, seq_lengths)
    key_seg, unused = sequence_places(key_place, seq_lengths)
    in_window = jnp.abs(query_place[:, None] - key_place[None, :]) <= WIN
    allowed = live_slots[:, None] & key_live[None, :] & (
        query_seg[:, None] == key_seg[None, :]
    ) & in_window | jnp.logical_not(live_slots)[:, None] & (
        key_slot[None, :] == slot_index[:, None]
    )
    cosine, sine = rotary_tables(query_pos)
    peers = lax.axis_size("fsdp")
    columns = D // peers
    gains = jnp.zeros((8, D), jnp.bfloat16)
    gains = gains.at[0, :columns].set(gain_attn).at[1, :columns].set(gain_mlp)
    first_rows = gather_rows(jnp.concatenate([w_qkv.T, gains]))
    qkv_full = first_rows[:, : 3 * columns].reshape(3 * D, D)
    gain_a_full = first_rows[:, 3 * columns, :columns].reshape(D)
    gain_m_full = first_rows[:, 3 * columns + 1, :columns].reshape(D)
    up_columns = w_up.shape[1]
    later = jnp.concatenate([w_up.T, w_out.T, fold_pad(w_down.T)])
    later_rows = gather_rows(later)
    up_full = later_rows[:, :up_columns].reshape(2 * FF, D)
    out_full = later_rows[:, up_columns : up_columns + columns].reshape(D, D)
    down_full = unfold_pad(later_rows[:, up_columns + columns :], columns).reshape(D, FF)
    stream = tokens.astype(jnp.float32)
    normed_one, factor_one = norm_parts(stream)
    first_in = (normed_one * gain_a_full.astype(jnp.float32)).astype(jnp.bfloat16)
    joined = cols_product(first_in, qkv_full)
    query = rotate_heads(joined[:, :D].reshape(slot_total, HEADS, HD), cosine, sine).astype(
        jnp.bfloat16
    )
    keys_own = rotate_heads(
        joined[:, D : 2 * D].reshape(slot_total, HEADS, HD), cosine, sine
    ).astype(jnp.bfloat16)
    values_own = joined[:, 2 * D :].astype(jnp.bfloat16)
    pairs = jnp.concatenate([keys_own.reshape(slot_total, D), values_own], axis=1)
    edges = jnp.concatenate(
        [pairs[:WIN], lax.dynamic_slice_in_dim(pairs, live_rows - WIN, WIN, 0)], axis=0
    )
    framed = with_halo(edges, (("fsdp", 0),), WIN)
    all_pairs = jnp.concatenate([framed[:WIN], pairs, framed[3 * WIN :]], axis=0)
    key_heads = all_pairs[:, :D].reshape(-1, HEADS, HD)
    value_heads = all_pairs[:, D:].reshape(-1, HEADS, HD)
    scores = masked_scores(query, key_heads, allowed, score_scale)
    row_top = jnp.max(scores, axis=-1, keepdims=True)
    log_total = row_top + jnp.log(jnp.sum(jnp.exp(scores - row_top), axis=-1, keepdims=True))
    probs_low = jnp.exp(scores - log_total).astype(jnp.bfloat16)
    mixed = (
        jnp.einsum("hqk,khd->qhd", probs_low, value_heads, preferred_element_type=jnp.float32)
        .reshape(slot_total, D)
        .astype(jnp.bfloat16)
    )
    after_attn = stream + cols_product(mixed, out_full)
    normed_two, factor_two = norm_parts(after_attn)
    second_in = (normed_two * gain_m_full.astype(jnp.float32)).astype(jnp.bfloat16)
    projected = cols_product(second_in, up_full)
    gate_half = projected[:, FF:]
    activated, gelu_pull = jax.vjp(exact_gelu, projected[:, :FF])
    hidden = (activated * gate_half).astype(jnp.bfloat16)
    down_out = cols_product(hidden, down_full)
    block_out = jnp.where(live_slots[:, None], after_attn + down_out, 0.0).astype(jnp.bfloat16)
    out_grad = jnp.where(live_slots[:, None], cotangent, jnp.zeros_like(cotangent))
    d_hidden = jnp.dot(out_grad, down_full, preferred_element_type=jnp.float32)
    d_inputs = gelu_pull(d_hidden * gate_half)[0]
    d_projected = jnp.concatenate([d_inputs, d_hidden * activated], axis=1).astype(jnp.bfloat16)
    d_second = jnp.dot(d_projected, up_full, preferred_element_type=jnp.float32)
    grad_gain_m = jnp.sum(normed_two * d_second, axis=0)
    d_after = out_grad.astype(jnp.float32) + norm_back(
        d_second * gain_m_full.astype(jnp.float32), normed_two, factor_two
    )
    d_attn = d_after.astype(jnp.bfloat16)
    d_mixed = jnp.dot(d_attn, out_full, preferred_element_type=jnp.float32).astype(jnp.bfloat16).reshape(slot_total, HEADS, HD)
    scores = masked_scores(query, key_heads, allowed, score_scale)
    probs = jnp.exp(scores - log_total)
    d_probs = jnp.einsum("qhd,khd->hqk", d_mixed, value_heads, preferred_element_type=jnp.float32)
    d_scores = (probs * (d_probs - jnp.sum(probs * d_probs, axis=-1, keepdims=True))).astype(
        jnp.bfloat16
    )
    d_query = (
        jnp.einsum("hqk,khd->qhd", d_scores, key_heads, preferred_element_type=jnp.float32)
        * score_scale
    )
    d_keys = (
        jnp.einsum("hqk,qhd->khd", d_scores, query, preferred_element_type=jnp.float32)
        * score_scale
    )
    d_values = jnp.einsum(
        "hqk,qhd->khd", probs.astype(jnp.bfloat16), d_mixed, preferred_element_type=jnp.float32
    )
    d_pairs = jnp.concatenate([d_keys.reshape(-1, D), d_values.reshape(-1, D)], axis=1)
    grad_edges = jnp.concatenate([d_pairs[:WIN], d_pairs[WIN + slot_total :]], axis=0)
    returned = with_halo(grad_edges.astype(jnp.bfloat16), (("fsdp", 0),), WIN).astype(
        grad_edges.dtype
    )
    own_pairs = d_pairs[WIN : WIN + slot_total]
    own_pairs = own_pairs.at[:WIN].add(returned[:WIN])
    tail_rows = lax.dynamic_slice_in_dim(own_pairs, live_rows - WIN, WIN, 0) + returned[3 * WIN :]
    own_pairs = lax.dynamic_update_slice_in_dim(own_pairs, tail_rows, live_rows - WIN, 0)
    d_query_raw = rotate_back(d_query, cosine, sine).reshape(slot_total, D)
    d_keys_raw = rotate_back(own_pairs[:, :D].reshape(slot_total, HEADS, HD), cosine, sine).reshape(
        slot_total, D
    )
    d_joined = jnp.concatenate([d_query_raw, d_keys_raw, own_pairs[:, D:]], axis=1).astype(
        jnp.bfloat16
    )
    d_first = jnp.dot(d_joined, qkv_full, preferred_element_type=jnp.float32)
    grad_gain_a = jnp.sum(normed_one * d_first, axis=0)
    d_stream = d_after + norm_back(
        d_first * gain_a_full.astype(jnp.float32), normed_one, factor_one
    )
    tokens_grad = jnp.where(live_slots[:, None], d_stream, 0.0)
    down_terms = column_term(out_grad, hidden).astype(jnp.bfloat16).reshape(peers, columns, FF)
    up_terms = column_term(d_projected, second_in).astype(jnp.bfloat16)
    mlp_sum = scatter_rows(
        jnp.concatenate([up_terms.reshape(peers, up_columns, D), fold_pad(down_terms)], axis=1)
    )
    up_sum = mlp_sum[:up_columns].T
    down_sum = unfold_pad(mlp_sum[up_columns:], columns).T
    qkv_terms = column_term(d_joined, first_in).astype(jnp.bfloat16).reshape(peers, 3 * columns, D)
    out_terms = column_term(d_attn, mixed).astype(jnp.bfloat16).reshape(peers, columns, D)
    gain_terms = jnp.stack([grad_gain_a.reshape(peers, columns), grad_gain_m.reshape(peers, columns)], axis=1)
    gain_terms = jnp.pad(gain_terms.astype(jnp.bfloat16), ((0, 0), (0, 6), (0, D - columns)))
    attn_sum = scatter_rows(jnp.concatenate([qkv_terms, out_terms, gain_terms], axis=1))
    qkv_sum = attn_sum[: 3 * columns].T
    out_sum = attn_sum[3 * columns : 4 * columns].T
    gain_a_sum = attn_sum[4 * columns, :columns]
    gain_m_sum = attn_sum[4 * columns + 1, :columns]
    return (block_out, tokens_grad, qkv_sum, out_sum, up_sum, down_sum, gain_a_sum, gain_m_sum)


def solution(mesh):
    placed = (
        P("fsdp", None),
        P(None, "fsdp"),
        P(None, "fsdp"),
        P(None, "fsdp"),
        P(None, "fsdp"),
        P("fsdp"),
        P("fsdp"),
        P("fsdp", None),
        P(),
        P(),
    )
    return jax.shard_map(
        body,
        mesh=mesh,
        in_specs=placed,
        out_specs=(
            P("fsdp", None),
            P("fsdp", None),
            P(None, "fsdp"),
            P(None, "fsdp"),
            P(None, "fsdp"),
            P(None, "fsdp"),
            P("fsdp"),
            P("fsdp"),
        ),
        check_vma=False,
    )
```

```python
import math

import jax
import jax.numpy as jnp
from jax import lax
from jax.experimental import pallas as pl
from jax.experimental.pallas import tpu as pltpu
from jax.sharding import PartitionSpec as P

D = 768
HEADS = 12
HD = 64
FF = 1152
BLK = 128
WIN = 64


EPSILON = 1e-05
MASKED = -1e30


def with_halo(shard, sides, width):
    for axis, dim in sides:
        peers, length = (lax.axis_size(axis), shard.shape[dim])
        up = [(i, (i + 1) % peers) for i in range(peers - 1)]
        down = [(j, i) for i, j in up]
        last = lax.slice_in_dim(shard, length - width, length, axis=dim)
        initial = lax.slice_in_dim(shard, 0, width, axis=dim)
        before = lax.ppermute(last, axis, up)
        after = lax.ppermute(initial, axis, down)
        shard = jnp.concatenate([before, shard, after], axis=dim)
    return shard


def norm_parts(values):
    center = values - jnp.mean(values, axis=-1, keepdims=True)
    factor = lax.rsqrt(jnp.mean(center * center, axis=-1, keepdims=True) + EPSILON)
    return (center * factor, factor)


def norm_back(grad_normed, normed, factor):
    return factor * (
        grad_normed
        - jnp.mean(grad_normed, axis=-1, keepdims=True)
        - normed * jnp.mean(grad_normed * normed, axis=-1, keepdims=True)
    )


def sequence_places(places, lengths):
    ends = jnp.cumsum(lengths)
    starts = ends - lengths
    segment = jnp.sum((places[:, None] >= ends[None, :]).astype(jnp.int32), axis=1)
    picked = segment[:, None] == jnp.arange(lengths.shape[0], dtype=jnp.int32)[None, :]
    start = jnp.sum(jnp.where(picked, starts[None, :], 0), axis=1)
    return (segment, places - start)


def rotary_tables(position):
    half = HD // 2
    freq = jnp.power(10000.0, -(jnp.arange(half, dtype=jnp.float32) * (2.0 / HD)))
    angle = position.astype(jnp.float32)[:, None] * freq[None, :]
    angle = jnp.concatenate([angle, angle], axis=1)[:, None, :]
    return (jnp.cos(angle), jnp.sin(angle))


def rotate_heads(values, cosine, sine):
    half = HD // 2
    turned = jnp.concatenate([-values[..., half:], values[..., :half]], axis=-1)
    return values * cosine + turned * sine


def rotate_back(grads, cosine, sine):
    half = HD // 2
    spun = grads * sine
    return grads * cosine + jnp.concatenate([spun[..., half:], -spun[..., :half]], axis=-1)


def rows_product(left, right):
    return lax.dot_general(
        left, right, (((0,), (0,)), ((), ())), preferred_element_type=jnp.float32
    )


def cols_product(left, right):
    return lax.dot_general(
        left, right, (((1,), (1,)), ((), ())), preferred_element_type=jnp.float32
    )


def exact_gelu(values):
    return jax.nn.gelu(values, approximate=False)


def masked_scores(query, key_heads, allowed, score_scale):
    raw_scores = (
        jnp.einsum("qhd,khd->hqk", query, key_heads, preferred_element_type=jnp.float32)
        * score_scale
    )
    return jnp.where(allowed[None], raw_scores, MASKED)


def column_term(grad_side, data_side):
    return rows_product(grad_side, data_side)


def permute(values, pairs):
    return lax.ppermute(values, "fsdp", pairs)


def links():
    sibling = [(i, i ^ 1) for i in range(32)]
    near = [(i, i ^ (2 if i & 1 else 4)) for i in range(32)]
    far = [(i, i ^ (4 if i & 1 else 2)) for i in range(32)]
    line = [[(i, (i + 8 * k) % 32) for i in range(32)] for k in range(4)]
    return (sibling, near, far, line)


def chip_place():
    me = lax.axis_index("fsdp")
    return (me // 8, (me // 4) % 2, (me // 2) % 2, me % 2)


def gather_rows(rows):
    return lax.all_gather(rows, "fsdp", axis=0, tiled=False)


def scatter_rows(terms):
    return lax.psum_scatter(terms, "fsdp", scatter_dimension=0, tiled=False).astype(jnp.float32)


def fold_pad(shard):
    count = shard.shape[-2]
    rest = shard[..., D:]
    half = (count + 1) // 2
    left, right = rest[..., :half, :], rest[..., half:, :]
    spare = [(0, 0)] * (shard.ndim - 2) + [(0, 2 * half - count), (0, 0)]
    rest = jnp.concatenate([left, jnp.pad(right, spare)], axis=-1)
    return jnp.concatenate([shard[..., :D], rest], axis=-2)


def unfold_pad(packed, count):
    half, lanes = (count + 1) // 2, FF - D
    rest = packed[..., count : count + half, :]
    rest = jnp.concatenate([rest[..., :lanes], rest[..., lanes:]], axis=-2)[..., :count, :]
    return jnp.concatenate([packed[..., :count, :], rest], axis=-1)


def body(
    tokens, w_qkv, w_out, w_up, w_down, gain_attn, gain_mlp, cotangent, block_counts, seq_lengths
):
    slot_total = tokens.shape[0]
    score_scale = 1.0 / math.sqrt(HD)
    device_index = lax.axis_index("fsdp")
    block_count = lax.dynamic_index_in_dim(block_counts, device_index, keepdims=False)
    device_ids = jnp.arange(block_counts.shape[0], dtype=jnp.int32)
    first_place = jnp.sum(jnp.where(device_ids < device_index, block_counts, 0)) * BLK
    live_rows = block_count * BLK
    stream_total = jnp.sum(block_counts) * BLK
    slot_index = jnp.arange(slot_total, dtype=jnp.int32)
    live_slots = slot_index < live_rows
    rim_offsets = jnp.arange(WIN, dtype=jnp.int32)
    query_place = first_place + slot_index
    before_place = first_place - WIN + rim_offsets
    after_place = first_place + live_rows + rim_offsets
    key_place = jnp.concatenate([before_place, query_place, after_place])
    key_live = jnp.concatenate([before_place >= 0, live_slots, after_place < stream_total])
    key_slot = jnp.concatenate([rim_offsets * 0 - 1, slot_index, rim_offsets * 0 - 1])
    query_seg, query_pos = sequence_places(query_place, seq_lengths)
    key_seg, unused = sequence_places(key_place, seq_lengths)
    in_window = jnp.abs(query_place[:, None] - key_place[None, :]) <= WIN
    allowed = live_slots[:, None] & key_live[None, :] & (
        query_seg[:, None] == key_seg[None, :]
    ) & in_window | jnp.logical_not(live_slots)[:, None] & (
        key_slot[None, :] == slot_index[:, None]
    )
    cosine, sine = rotary_tables(query_pos)
    peers = lax.axis_size("fsdp")
    columns = D // peers
    gains = jnp.zeros((8, D), jnp.bfloat16)
    gains = gains.at[0, :columns].set(gain_attn).at[1, :columns].set(gain_mlp)
    first_rows = gather_rows(jnp.concatenate([w_qkv.T, gains]))
    qkv_full = first_rows[:, : 3 * columns].reshape(3 * D, D)
    gain_a_full = first_rows[:, 3 * columns, :columns].reshape(D)
    gain_m_full = first_rows[:, 3 * columns + 1, :columns].reshape(D)
    up_columns = w_up.shape[1]
    later = jnp.concatenate([w_up.T, w_out.T, fold_pad(w_down.T)])
    later_rows = gather_rows(later)
    up_full = later_rows[:, :up_columns].reshape(2 * FF, D)
    out_full = later_rows[:, up_columns : up_columns + columns].reshape(D, D)
    down_full = unfold_pad(later_rows[:, up_columns + columns :], columns).reshape(D, FF)
    stream = tokens.astype(jnp.float32)
    normed_one, factor_one = norm_parts(stream)
    first_in = (normed_one * gain_a_full.astype(jnp.float32)).astype(jnp.bfloat16)
    joined = cols_product(first_in, qkv_full)
    query = rotate_heads(joined[:, :D].reshape(slot_total, HEADS, HD), cosine, sine).astype(
        jnp.bfloat16
    )
    keys_own = rotate_heads(
        joined[:, D : 2 * D].reshape(slot_total, HEADS, HD), cosine, sine
    ).astype(jnp.bfloat16)
    values_own = joined[:, 2 * D :].astype(jnp.bfloat16)
    pairs = jnp.concatenate([keys_own.reshape(slot_total, D), values_own], axis=1)
    edges = jnp.concatenate(
        [pairs[:WIN], lax.dynamic_slice_in_dim(pairs, live_rows - WIN, WIN, 0)], axis=0
    )
    framed = with_halo(edges, (("fsdp", 0),), WIN)
    all_pairs = jnp.concatenate([framed[:WIN], pairs, framed[3 * WIN :]], axis=0)
    key_heads = all_pairs[:, :D].reshape(-1, HEADS, HD)
    value_heads = all_pairs[:, D:].reshape(-1, HEADS, HD)
    scores = masked_scores(query, key_heads, allowed, score_scale)
    row_top = jnp.max(scores, axis=-1, keepdims=True)
    log_total = row_top + jnp.log(jnp.sum(jnp.exp(scores - row_top), axis=-1, keepdims=True))
    probs_low = jnp.exp(scores - log_total).astype(jnp.bfloat16)
    mixed = (
        jnp.einsum("hqk,khd->qhd", probs_low, value_heads, preferred_element_type=jnp.float32)
        .reshape(slot_total, D)
        .astype(jnp.bfloat16)
    )
    after_attn = stream + cols_product(mixed, out_full)
    normed_two, factor_two = norm_parts(after_attn)
    second_in = (normed_two * gain_m_full.astype(jnp.float32)).astype(jnp.bfloat16)
    projected = cols_product(second_in, up_full)
    gate_half = projected[:, FF:]
    activated, gelu_pull = jax.vjp(exact_gelu, projected[:, :FF])
    hidden = (activated * gate_half).astype(jnp.bfloat16)
    down_out = cols_product(hidden, down_full)
    block_out = jnp.where(live_slots[:, None], after_attn + down_out, 0.0).astype(jnp.bfloat16)
    out_grad = jnp.where(live_slots[:, None], cotangent, jnp.zeros_like(cotangent))
    d_hidden = jnp.dot(out_grad, down_full, preferred_element_type=jnp.float32)
    d_inputs = gelu_pull(d_hidden * gate_half)[0]
    d_projected = jnp.concatenate([d_inputs, d_hidden * activated], axis=1).astype(jnp.bfloat16)
    d_second = jnp.dot(d_projected, up_full, preferred_element_type=jnp.float32)
    grad_gain_m = jnp.sum(normed_two * d_second, axis=0)
    d_after = out_grad.astype(jnp.float32) + norm_back(
        d_second * gain_m_full.astype(jnp.float32), normed_two, factor_two
    )
    d_attn = d_after.astype(jnp.bfloat16)
    d_mixed = jnp.dot(d_attn, out_full, preferred_element_type=jnp.float32).astype(jnp.bfloat16).reshape(slot_total, HEADS, HD)
    scores = masked_scores(query, key_heads, allowed, score_scale)
    probs = jnp.exp(scores - log_total)
    d_probs = jnp.einsum("qhd,khd->hqk", d_mixed, value_heads, preferred_element_type=jnp.float32)
    d_scores = (probs * (d_probs - jnp.sum(probs * d_probs, axis=-1, keepdims=True))).astype(
        jnp.bfloat16
    )
    d_query = (
        jnp.einsum("hqk,khd->qhd", d_scores, key_heads, preferred_element_type=jnp.float32)
        * score_scale
    )
    d_keys = (
        jnp.einsum("hqk,qhd->khd", d_scores, query, preferred_element_type=jnp.float32)
        * score_scale
    )
    d_values = jnp.einsum(
        "hqk,qhd->khd", probs.astype(jnp.bfloat16), d_mixed, preferred_element_type=jnp.float32
    )
    d_pairs = jnp.concatenate([d_keys.reshape(-1, D), d_values.reshape(-1, D)], axis=1)
    grad_edges = jnp.concatenate([d_pairs[:WIN], d_pairs[WIN + slot_total :]], axis=0)
    returned = with_halo(grad_edges.astype(jnp.bfloat16), (("fsdp", 0),), WIN).astype(
        grad_edges.dtype
    )
    own_pairs = d_pairs[WIN : WIN + slot_total]
    own_pairs = own_pairs.at[:WIN].add(returned[:WIN])
    tail_rows = lax.dynamic_slice_in_dim(own_pairs, live_rows - WIN, WIN, 0) + returned[3 * WIN :]
    own_pairs = lax.dynamic_update_slice_in_dim(own_pairs, tail_rows, live_rows - WIN, 0)
    d_query_raw = rotate_back(d_query, cosine, sine).reshape(slot_total, D)
    d_keys_raw = rotate_back(own_pairs[:, :D].reshape(slot_total, HEADS, HD), cosine, sine).reshape(
        slot_total, D
    )
    d_joined = jnp.concatenate([d_query_raw, d_keys_raw, own_pairs[:, D:]], axis=1).astype(
        jnp.bfloat16
    )
    d_first = jnp.dot(d_joined, qkv_full, preferred_element_type=jnp.float32)
    grad_gain_a = jnp.sum(normed_one * d_first, axis=0)
    d_stream = d_after + norm_back(
        d_first * gain_a_full.astype(jnp.float32), normed_one, factor_one
    )
    tokens_grad = jnp.where(live_slots[:, None], d_stream, 0.0)
    down_terms = column_term(out_grad, hidden).astype(jnp.bfloat16).reshape(peers, columns, FF)
    up_terms = column_term(d_projected, second_in).astype(jnp.bfloat16)
    mlp_sum = scatter_rows(
        jnp.concatenate([up_terms.reshape(peers, up_columns, D), fold_pad(down_terms)], axis=1)
    )
    up_sum = mlp_sum[:up_columns].T
    down_sum = unfold_pad(mlp_sum[up_columns:], columns).T
    qkv_terms = column_term(d_joined, first_in).astype(jnp.bfloat16).reshape(peers, 3 * columns, D)
    out_terms = column_term(d_attn, mixed).astype(jnp.bfloat16).reshape(peers, columns, D)
    gain_terms = jnp.stack([grad_gain_a.reshape(peers, columns), grad_gain_m.reshape(peers, columns)], axis=1)
    gain_terms = jnp.pad(gain_terms.astype(jnp.bfloat16), ((0, 0), (0, 6), (0, D - columns)))
    attn_sum = scatter_rows(jnp.concatenate([qkv_terms, out_terms, gain_terms], axis=1))
    qkv_sum = attn_sum[: 3 * columns].T
    out_sum = attn_sum[3 * columns : 4 * columns].T
    gain_a_sum = attn_sum[4 * columns, :columns]
    gain_m_sum = attn_sum[4 * columns + 1, :columns]
    return (block_out, tokens_grad, qkv_sum, out_sum, up_sum, down_sum, gain_a_sum, gain_m_sum)


CHIPS = 16
HALF = 384
ROWS1 = 160
ROWS2 = 272
SLOTS = 256
SPAN = SLOTS + 2 * WIN
PAIR = 2 * HD
PAIRS = HEADS // 2
LIMIT = 48 * 1024 * 1024
AT_LIVE, AT_CORE, AT_TAKE, AT_PUT = 0, 1, 2, 34
VMEM = pltpu.MemorySpace.VMEM
SMEM = pltpu.MemorySpace.SMEM


def nt_dot(left, right):
    return lax.dot_general(left, right, (((1,), (1,)), ((), ())), preferred_element_type=jnp.float32)


def nn_dot(left, right):
    return jnp.dot(left, right, preferred_element_type=jnp.float32)


def tn_dot(left, right):
    return lax.dot_general(left, right, (((0,), (0,)), ((), ())), preferred_element_type=jnp.float32)


def call(kernel, outs, scratch, args, flops):
    spaces = [pl.BlockSpec(memory_space=SMEM)] + [pl.BlockSpec(memory_space=VMEM)] * (len(args) - 1)
    return pl.pallas_call(
        kernel,
        out_shape=[jax.ShapeDtypeStruct(shape, kind) for shape, kind in outs],
        in_specs=spaces,
        out_specs=[pl.BlockSpec(memory_space=VMEM)] * len(outs),
        scratch_shapes=[pltpu.VMEM(shape, kind) for shape, kind in scratch],
        compiler_params=pltpu.CompilerParams(vmem_limit_bytes=LIMIT),
        cost_estimate=pl.CostEstimate(flops=flops, bytes_accessed=16_000_000, transcendentals=1_000_000),
    )(*args)


def take_blocks(place, mine, other, copy):
    for stream in (0, 1):
        for held, ref in ((stream, mine), (1 - stream, other)):

            @pl.when(place[AT_CORE] == held)
            def _(stream=stream, ref=ref):
                for chip in range(CHIPS):
                    copy(stream, chip, ref, place[AT_TAKE + 16 * stream + chip])


def put_rows(place, send, keep, stream, start, value, chips):
    count = value.shape[0] // len(chips)
    value = value.astype(jnp.bfloat16)

    def store(ref):
        for i, chip in enumerate(chips):
            slot = place[AT_PUT + 16 * stream + chip]
            ref[slot, start : start + count, :] = value[i * count : (i + 1) * count]

    pl.when(place[AT_CORE] == stream)(lambda: store(keep))
    pl.when(place[AT_CORE] != stream)(lambda: store(send))


def gain_rows(vector, chip):
    start = min(48 * chip // 128 * 128, D - HALF)
    return jnp.broadcast_to(vector[:, start : start + HALF], (16, HALF))


def project_kernel(place, tokens, gain, mine, other, cos, sin_a, sin_b, query, pairs, first, weight):
    def copy(stream, chip, ref, slot):
        weight[144 * chip : 144 * chip + 144, HALF * stream : HALF * (stream + 1)] = ref[slot, 0:144, :]

    take_blocks(place, mine, other, copy)
    normed, _ = norm_parts(tokens[...].astype(jnp.float32))
    a1 = (normed * gain[...]).astype(jnp.bfloat16)
    first[...] = a1
    c, sa, sb = cos[...], sin_a[...], sin_b[...]
    for part in range(3):
        for j in range(2):
            base = part * D + HALF * j
            joined = nt_dot(a1, weight[base : base + HALF, :])
            for p in range(3):
                lanes = slice(HALF * j + PAIR * p, HALF * j + PAIR * (p + 1))
                v = joined[:, PAIR * p : PAIR * (p + 1)]
                if part < 2:
                    v = v * c + pltpu.roll(v, 96, 1) * sa + pltpu.roll(v, 32, 1) * sb
                if part == 0:
                    query[:, lanes] = v.astype(jnp.bfloat16)
                else:
                    where = slice((part - 1) * D + lanes.start, (part - 1) * D + lanes.stop)
                    pairs[:, where] = v.astype(jnp.bfloat16)


def frame_pairs(place, pairs, before, after, framed):
    framed[0:WIN, :] = before[...]
    framed[WIN : WIN + SLOTS, :] = pairs[...]
    framed[WIN + SLOTS : SPAN, :] = jnp.zeros((WIN, 2 * D), jnp.bfloat16)
    framed[pl.ds(pl.multiple_of(WIN + place[AT_LIVE], 64), WIN), :] = after[...]


def stack_heads(values, low, high):
    return jnp.concatenate([values * low, values * high], axis=0)


def head_masks():
    lane = lax.broadcasted_iota(jnp.int32, (1, PAIR), 1)
    low = jnp.where(lane < HD, 1.0, 0.0).astype(jnp.bfloat16)
    return (lane < HD, low, 1.0 - low)


def probabilities(query, keys, bias):
    scores = nt_dot(query, keys) * (1.0 / math.sqrt(HD)) + bias
    expos = jnp.exp(scores - jnp.max(scores, axis=-1, keepdims=True))
    return expos * (1.0 / jnp.sum(expos, axis=-1, keepdims=True))


def middle_kernel(
    place, tokens, query, pairs, before, after, bias, mine, other, gain, cotangent,
    block_out, d_after_out, d_mixed, send, keep,
    framed, w_up, w_out, w_down, mixed, d_proj, hidden,
):
    def copy(stream, chip, ref, slot):
        lanes = slice(HALF * stream, HALF * (stream + 1))
        w_up[144 * chip : 144 * chip + 144, lanes] = ref[slot, 0:144, :]
        w_out[48 * chip : 48 * chip + 48, lanes] = ref[slot, 144:192, :]
        w_down[48 * chip : 48 * chip + 48, lanes] = ref[slot, 192:240, :]
        if stream == 0:
            w_down[48 * chip : 48 * chip + 32, 2 * HALF :] = ref[slot, 240:272, :]
        else:
            w_down[48 * chip + 32 : 48 * chip + 48, 2 * HALF :] = ref[slot, 240:256, :]

    take_blocks(place, mine, other, copy)
    frame_pairs(place, pairs, before, after, framed)
    is_low, low, high = head_masks()
    for block in range(2):
        rows, keys = slice(128 * block, 128 * block + 128), slice(128 * block, 128 * block + 256)
        both = jnp.concatenate([bias[rows, :], bias[rows, :]], axis=0)
        for p in range(PAIRS):
            lanes, vlanes = slice(PAIR * p, PAIR * (p + 1)), slice(D + PAIR * p, D + PAIR * (p + 1))
            probs = probabilities(stack_heads(query[rows, lanes], low, high), framed[keys, lanes], both)
            out = nn_dot(probs.astype(jnp.bfloat16), framed[keys, vlanes])
            mixed[rows, lanes] = jnp.where(is_low, out[:128], out[128:]).astype(jnp.bfloat16)
    after_attn = tokens[...].astype(jnp.float32) + nt_dot(mixed[...], w_out[...])
    normed, factor = norm_parts(after_attn)
    gains = gain[...]
    a2 = (normed * gains).astype(jnp.bfloat16)
    live = lax.broadcasted_iota(jnp.int32, (SLOTS, 1), 0) < place[AT_LIVE]
    grad = jnp.where(live, cotangent[...].astype(jnp.float32), 0.0)
    out_grad = grad.astype(jnp.bfloat16)
    down = jnp.zeros((SLOTS, D), jnp.float32)
    for j in range(3):
        lanes = slice(HALF * j, HALF * (j + 1))
        inputs = nt_dot(a2, w_up[lanes, :])
        gate = nt_dot(a2, w_up[FF + HALF * j : FF + HALF * (j + 1), :])
        cdf = 0.5 * (1.0 + lax.erf(inputs * (1.0 / math.sqrt(2.0))))
        slope = cdf + inputs * (jnp.exp(-0.5 * inputs * inputs) * (1.0 / math.sqrt(2.0 * math.pi)))
        active = inputs * cdf
        low_hidden = (active * gate).astype(jnp.bfloat16)
        hidden[:, lanes] = low_hidden
        down = down + nt_dot(low_hidden, w_down[:, lanes])
        d_hidden = nn_dot(out_grad, w_down[:, lanes])
        d_proj[:, lanes] = (d_hidden * gate * slope).astype(jnp.bfloat16)
        d_proj[:, FF + HALF * j : FF + HALF * (j + 1)] = (d_hidden * active).astype(jnp.bfloat16)
    block_out[...] = jnp.where(live, after_attn + down, 0.0).astype(jnp.bfloat16)
    everyone = list(range(CHIPS))
    d_second = nn_dot(d_proj[...], w_up[...])
    gain_grad = jnp.sum(normed * d_second, axis=0, keepdims=True)
    d_after = grad + norm_back(d_second * gains, normed, factor)
    d_after_out[...] = d_after
    d_attn = d_after.astype(jnp.bfloat16)
    d_mixed[...] = nn_dot(d_attn, w_out[...]).astype(jnp.bfloat16)
    for stream in (0, 1):
        lanes = slice(HALF * stream, HALF * (stream + 1))
        for j in range(2):
            up = tn_dot(d_proj[:, FF * j : FF * (j + 1)], a2[:, lanes])
            put_rows(place, send, keep, stream, 0, up, everyone[8 * j : 8 * j + 8])
        put_rows(place, send, keep, stream, 144, tn_dot(d_attn, mixed[:, lanes]), everyone)
        put_rows(place, send, keep, stream, 192, tn_dot(out_grad, hidden[:, lanes]), everyone)
    rest = tn_dot(out_grad, hidden[:, 2 * HALF :])
    for chip in everyone:
        put_rows(place, send, keep, 0, 240, rest[48 * chip : 48 * chip + 32], [chip])
        put_rows(place, send, keep, 1, 240, rest[48 * chip + 32 : 48 * chip + 48], [chip])
        put_rows(place, send, keep, 1, 256, gain_rows(gain_grad, chip), [chip])


def attend_back_kernel(
    place, query, pairs, before, after, bias, d_mixed,
    d_query, d_own, rim_before, rim_after, framed, d_framed,
):
    frame_pairs(place, pairs, before, after, framed)
    is_low, low, high = head_masks()
    d_framed[256:SPAN, :] = jnp.zeros((SPAN - 256, 2 * D), jnp.float32)
    scale = 1.0 / math.sqrt(HD)
    for block in range(2):
        rows, keys = slice(128 * block, 128 * block + 128), slice(128 * block, 128 * block + 256)
        both = jnp.concatenate([bias[rows, :], bias[rows, :]], axis=0)
        for p in range(PAIRS):
            lanes, vlanes = slice(PAIR * p, PAIR * (p + 1)), slice(D + PAIR * p, D + PAIR * (p + 1))
            q2 = stack_heads(query[rows, lanes], low, high)
            o2 = stack_heads(d_mixed[rows, lanes], low, high)
            k2 = framed[keys, lanes]
            probs = probabilities(q2, k2, both)
            d_probs = nt_dot(o2, framed[keys, vlanes])
            spread = jnp.sum(probs * d_probs, axis=-1, keepdims=True)
            d_scores = (probs * (d_probs - spread)).astype(jnp.bfloat16)
            d_q = nn_dot(d_scores, k2) * scale
            d_query[rows, lanes] = jnp.where(is_low, d_q[:128], d_q[128:])
            d_k = tn_dot(d_scores, q2) * scale
            d_v = tn_dot(probs.astype(jnp.bfloat16), o2)
            if block == 0:
                d_framed[keys, lanes] = d_k
                d_framed[keys, vlanes] = d_v
            else:
                d_framed[keys, lanes] += d_k
                d_framed[keys, vlanes] += d_v
    rim_before[...] = d_framed[0:WIN, :].astype(jnp.bfloat16)
    tail = pl.ds(pl.multiple_of(WIN + place[AT_LIVE], 64), WIN)
    rim_after[...] = d_framed[tail, :].astype(jnp.bfloat16)
    d_own[...] = d_framed[WIN : WIN + SLOTS, :]


def finish_kernel(
    place, tokens, first, gain, weight, d_query, d_own, from_before, from_after, cos, sin_a, sin_b, d_after,
    tokens_grad, send, keep, d_joined, d_pairs,
):
    live = lax.broadcasted_iota(jnp.int32, (SLOTS, 1), 0) < place[AT_LIVE]
    d_pairs[...] = jnp.where(live, d_own[...], 0.0)
    d_pairs[0:WIN, :] += from_before[...].astype(jnp.float32)
    tail = pl.ds(pl.multiple_of(place[AT_LIVE] - WIN, 64), WIN)
    d_pairs[tail, :] += from_after[...].astype(jnp.float32)
    c, sa, sb = cos[...], sin_a[...], sin_b[...]
    for part in range(2):
        source = d_query if part == 0 else d_pairs
        for p in range(PAIRS):
            v = source[:, PAIR * p : PAIR * (p + 1)]
            v = v * c - pltpu.roll(v, 96, 1) * sa - pltpu.roll(v, 32, 1) * sb
            d_joined[:, part * D + PAIR * p : part * D + PAIR * (p + 1)] = v.astype(jnp.bfloat16)
    d_joined[:, 2 * D :] = d_pairs[:, D:].astype(jnp.bfloat16)
    d_first = nn_dot(d_joined[...], weight[...])
    normed, factor = norm_parts(tokens[...].astype(jnp.float32))
    gain_grad = jnp.sum(normed * d_first, axis=0, keepdims=True)
    d_stream = d_after[...] + norm_back(d_first * gain[...], normed, factor)
    tokens_grad[...] = jnp.where(live, d_stream, 0.0)
    everyone = list(range(CHIPS))
    for stream in (0, 1):
        lanes = slice(HALF * stream, HALF * (stream + 1))
        for j in range(2):
            up = tn_dot(d_joined[:, 1152 * j : 1152 * (j + 1)], first[:, lanes])
            put_rows(place, send, keep, stream, 0, up, everyone[8 * j : 8 * j + 8])
        for chip in everyone:
            put_rows(place, send, keep, stream, 144, gain_rows(gain_grad, chip), [chip])


def swap_halves(shard, core, sibling):
    low, high = shard[:, :HALF], shard[:, HALF:]
    own = jnp.where(core == 0, low, high)
    return own, permute(jnp.where(core == 0, high, low), sibling)


def interleave(own, got, core, cuts):
    parts, start = [], 0
    for count in cuts:
        mine, theirs = own[start : start + count], got[start : start + count]
        parts += [jnp.where(core == 0, mine, theirs), jnp.where(core == 0, theirs, mine)]
        start += count
    return parts


def spread_line(block, line):
    return jnp.stack([block] + [permute(block, line[k]) for k in (1, 2, 3)])


def widen(held, pairs):
    return jnp.concatenate([held, permute(held, pairs)])


def reduce_stage(send, keep, links_of):
    sibling, near, far, line = links_of
    total = keep + permute(send, sibling)
    total = total[8:] + permute(total[:8], near)
    total = total[4:] + permute(total[:4], far)
    share = total[3].astype(jnp.float32)
    for k in range(3):
        share = share + permute(total[k], line[k + 1]).astype(jnp.float32)
    return share


def place_table(live_rows):
    z, y, x, core = chip_place()
    chips = jnp.arange(CHIPS, dtype=jnp.int32)
    zz, yy, xx = chips // 4, (chips // 2) % 2, chips % 2
    yr, xr = y ^ yy, x ^ xx
    take, put = [], []
    for near, far in ((yr, xr), (xr, yr)):
        take.append(far * 8 + near * 4 + (z - zz) % 4)
        put.append((1 - near) * 8 + (1 - far) * 4 + (zz - z + 3) % 4)
    head = jnp.stack([live_rows, core]).astype(jnp.int32)
    return jnp.concatenate([head] + take + put).astype(jnp.int32)


def fused_body(
    tokens, w_qkv, w_out, w_up, w_down, gain_attn, gain_mlp, cotangent, block_counts, seq_lengths
):
    bf16, f32 = jnp.bfloat16, jnp.float32
    device_index = lax.axis_index("fsdp")
    core = device_index % 2
    wires = links()
    sibling, near, far, line = wires
    gains = jnp.zeros((8, D), bf16)
    gain_pair = jnp.pad(jnp.stack([gain_attn, gain_mlp]), ((0, 6), (0, HALF - 24)))
    gains = jnp.concatenate([gain_pair, gain_pair], axis=1)
    own, got = swap_halves(jnp.concatenate([w_qkv.T, gains]), core, sibling)
    block = jnp.concatenate(interleave(own, got, core, (72, 8)))
    held = spread_line(block, line)
    held = widen(held, near)
    mine_one = widen(held, far)
    other_one = permute(mine_one, sibling)
    block_count = lax.dynamic_index_in_dim(block_counts, device_index, keepdims=False)
    device_ids = jnp.arange(block_counts.shape[0], dtype=jnp.int32)
    first_place = jnp.sum(jnp.where(device_ids < device_index, block_counts, 0)) * BLK
    live_rows = block_count * BLK
    stream_total = jnp.sum(block_counts) * BLK
    place = place_table(live_rows)
    slot_index = jnp.arange(SLOTS, dtype=jnp.int32)
    live_slots = slot_index < live_rows
    query_place = first_place + slot_index
    query_seg, query_pos = sequence_places(query_place, seq_lengths)
    key_slot = (slot_index // BLK * BLK)[:, None] + jnp.arange(256, dtype=jnp.int32)[None, :] - WIN
    key_place = first_place + key_slot
    ends = jnp.cumsum(seq_lengths)
    key_seg = jnp.sum((key_place[:, :, None] >= ends).astype(jnp.int32), axis=2)
    allowed = (
        live_slots[:, None]
        & (key_place >= 0)
        & (key_place < stream_total)
        & (query_seg[:, None] == key_seg)
        & (jnp.abs(query_place[:, None] - key_place) <= WIN)
    ) | (jnp.logical_not(live_slots)[:, None] & (key_slot == slot_index[:, None]))
    bias = jnp.where(allowed, 0.0, MASKED).astype(f32)
    cosine, sine = rotary_tables(query_pos)
    cosine, sine = (jnp.concatenate([t[:, 0], t[:, 0]], axis=1) for t in (cosine, sine))
    front = (jnp.arange(PAIR) % HD < HD // 2)[None, :]
    sin_a, sin_b = jnp.where(front, -sine, 0.0), jnp.where(front, 0.0, sine)
    zz, yy, xx = (jnp.arange(CHIPS, dtype=jnp.int32) // 4, jnp.arange(CHIPS) // 2 % 2, jnp.arange(CHIPS) % 2)
    taken = jnp.where(core == 0, place[AT_TAKE : AT_TAKE + 16], place[AT_TAKE + 16 : AT_TAKE + 32])
    chosen = (taken[:, None] == jnp.arange(CHIPS)[None, :]).astype(f32)
    flat = jnp.concatenate(
        [mine_one[:, 144, :24], mine_one[:, 152, :24], mine_one[:, 145, :24], mine_one[:, 153, :24]], axis=1
    ).astype(f32)
    flat = jnp.sum(chosen[:, :, None] * flat[None], axis=1)
    gain_a, gain_m = flat[:, :48].reshape(1, D), flat[:, 48:].reshape(1, D)
    query, pairs, first, weight = call(
        project_kernel,
        [((SLOTS, D), bf16), ((SLOTS, 2 * D), bf16), ((SLOTS, D), bf16), ((3 * D, D), bf16)],
        [],
        [place, tokens, gain_a, mine_one, other_one, cosine, sin_a, sin_b],
        900_000_000,
    )
    shard = jnp.concatenate([w_up.T, w_out.T, w_down.T[:, :D]])
    rest = w_down.T[:, D:]
    low, high = shard[:, :HALF], shard[:, HALF:]
    own = jnp.concatenate([jnp.where(core == 0, low, high), rest[:8]])
    got = permute(jnp.concatenate([jnp.where(core == 0, high, low), rest[:8]]), sibling)
    tail = jnp.where(
        core == 0,
        jnp.concatenate([rest, got[120:128]]),
        jnp.concatenate([rest[8:], jnp.zeros((16, HALF), bf16)]),
    )
    block = jnp.concatenate(interleave(own, got, core, (72, 24, 24)) + [tail])
    held, block_done = spread_line(block, line), mine_one
    held, block_done = lax.optimization_barrier((held, block_done))
    held = widen(held, near)
    mine_two = widen(held, far)
    other_two = permute(mine_two, sibling)
    up = [(i, i + 1) for i in range(31)]
    down = [(i + 1, i) for i in range(31)]
    before = permute(lax.dynamic_slice_in_dim(pairs, live_rows - WIN, WIN, 0), up)
    after = permute(pairs[:WIN], down)
    block_out, d_after, d_mixed, send, keep = call(
        middle_kernel,
        [((SLOTS, D), bf16), ((SLOTS, D), f32), ((SLOTS, D), bf16), ((CHIPS, ROWS2, HALF), bf16), ((CHIPS, ROWS2, HALF), bf16)],
        [((SPAN, 2 * D), bf16), ((2 * FF, D), bf16), ((D, D), bf16), ((D, FF), bf16), ((SLOTS, D), bf16), ((SLOTS, 2 * FF), bf16), ((SLOTS, FF), bf16)],
        [place, tokens, query, pairs, before, after, bias, mine_two, other_two, gain_m, cotangent],
        6_000_000_000,
    )
    d_query, d_own, rim_before, rim_after = call(
        attend_back_kernel,
        [((SLOTS, D), f32), ((SLOTS, 2 * D), f32), ((WIN, 2 * D), bf16), ((WIN, 2 * D), bf16)],
        [((SPAN, 2 * D), bf16), ((SPAN, 2 * D), f32)],
        [place, query, pairs, before, after, bias, d_mixed],
        3_000_000_000,
    )
    from_after = permute(rim_before, down)
    from_before = permute(rim_after, up)
    tokens_grad, send_qkv, keep_qkv = call(
        finish_kernel,
        [((SLOTS, D), f32), ((CHIPS, ROWS1, HALF), bf16), ((CHIPS, ROWS1, HALF), bf16)],
        [((SLOTS, 3 * D), bf16), ((SLOTS, 2 * D), f32)],
        [place, tokens, first, gain_a, weight, d_query, d_own, from_before, from_after, cosine, sin_a, sin_b, d_after],
        3_000_000_000,
    )
    share = reduce_stage(send, keep, wires)
    chip = device_index // 2
    lane = 48 * chip - jnp.minimum(48 * chip // 128 * 128, D - HALF) + 24 * core

    def part(block, start, count, whose):
        return lax.dynamic_slice_in_dim(block, start + count * whose, count, 0)

    gain_row = lax.dynamic_slice_in_dim(share[256:264], lane - 24 * core, 48, 1)
    gain_row = jnp.pad(gain_row, ((0, 0), (0, HALF - 48)))
    cuts = ((0, 72), (144, 24), (192, 24))
    theirs = jnp.concatenate(
        [part(share, s, n, 1 - core) for s, n in cuts] + [jnp.where(core == 0, share[264:272], gain_row)]
    )
    own = jnp.concatenate([part(share, s, n, core) for s, n in cuts])
    got = permute(theirs, sibling)
    both = jnp.concatenate(
        [jnp.where(core == 0, own, got[:120]), jnp.where(core == 0, got[:120], own)], axis=1
    )
    last = jnp.where(
        core == 0, share[240:264], jnp.concatenate([got[120:128], share[240:256]])
    )
    up_sum, out_sum = both[:72].T, both[72:96].T
    down_sum = jnp.concatenate([both[96:], last], axis=1).T
    gain_m_sum = jnp.where(core == 0, got[120, :24], gain_row[0, 24:48])
    share = reduce_stage(send_qkv, keep_qkv, wires)
    got = permute(part(share, 0, 72, 1 - core), sibling)
    own = part(share, 0, 72, core)
    qkv_sum = jnp.concatenate([jnp.where(core == 0, own, got), jnp.where(core == 0, got, own)], axis=1).T
    gain_a_sum = lax.dynamic_slice(share, (144, lane), (1, 24))[0]
    return (block_out, tokens_grad, qkv_sum, out_sum, up_sum, down_sum, gain_a_sum, gain_m_sum)


def solution(mesh):
    plan = fused_body if mesh.shape["fsdp"] == 32 else body
    placed = (
        P("fsdp", None),
        P(None, "fsdp"),
        P(None, "fsdp"),
        P(None, "fsdp"),
        P(None, "fsdp"),
        P("fsdp"),
        P("fsdp"),
        P("fsdp", None),
        P(),
        P(),
    )
    return jax.shard_map(
        plan,
        mesh=mesh,
        in_specs=placed,
        out_specs=(
            P("fsdp", None),
            P("fsdp", None),
            P(None, "fsdp"),
            P(None, "fsdp"),
            P(None, "fsdp"),
            P(None, "fsdp"),
            P("fsdp"),
            P("fsdp"),
        ),
        check_vma=False,
    )
```

```python
import math

import jax
import jax.numpy as jnp
from jax import lax
from jax.experimental import pallas as pl
from jax.experimental.pallas import tpu as pltpu
from jax.sharding import PartitionSpec as P

D = 768
HEADS = 12
HD = 64
FF = 1152
BLK = 128
WIN = 64


EPSILON = 1e-05
MASKED = -1e30


def with_halo(shard, sides, width):
    for axis, dim in sides:
        peers, length = (lax.axis_size(axis), shard.shape[dim])
        up = [(i, (i + 1) % peers) for i in range(peers - 1)]
        down = [(j, i) for i, j in up]
        last = lax.slice_in_dim(shard, length - width, length, axis=dim)
        initial = lax.slice_in_dim(shard, 0, width, axis=dim)
        before = lax.ppermute(last, axis, up)
        after = lax.ppermute(initial, axis, down)
        shard = jnp.concatenate([before, shard, after], axis=dim)
    return shard


def norm_parts(values):
    center = values - jnp.mean(values, axis=-1, keepdims=True)
    factor = lax.rsqrt(jnp.mean(center * center, axis=-1, keepdims=True) + EPSILON)
    return (center * factor, factor)


def norm_back(grad_normed, normed, factor):
    return factor * (
        grad_normed
        - jnp.mean(grad_normed, axis=-1, keepdims=True)
        - normed * jnp.mean(grad_normed * normed, axis=-1, keepdims=True)
    )


def sequence_places(places, lengths):
    ends = jnp.cumsum(lengths)
    starts = ends - lengths
    segment = jnp.sum((places[:, None] >= ends[None, :]).astype(jnp.int32), axis=1)
    picked = segment[:, None] == jnp.arange(lengths.shape[0], dtype=jnp.int32)[None, :]
    start = jnp.sum(jnp.where(picked, starts[None, :], 0), axis=1)
    return (segment, places - start)


def rotary_tables(position):
    half = HD // 2
    freq = jnp.power(10000.0, -(jnp.arange(half, dtype=jnp.float32) * (2.0 / HD)))
    angle = position.astype(jnp.float32)[:, None] * freq[None, :]
    angle = jnp.concatenate([angle, angle], axis=1)[:, None, :]
    return (jnp.cos(angle), jnp.sin(angle))


def rotate_heads(values, cosine, sine):
    half = HD // 2
    turned = jnp.concatenate([-values[..., half:], values[..., :half]], axis=-1)
    return values * cosine + turned * sine


def rotate_back(grads, cosine, sine):
    half = HD // 2
    spun = grads * sine
    return grads * cosine + jnp.concatenate([spun[..., half:], -spun[..., :half]], axis=-1)


def rows_product(left, right):
    return lax.dot_general(
        left, right, (((0,), (0,)), ((), ())), preferred_element_type=jnp.float32
    )


def cols_product(left, right):
    return lax.dot_general(
        left, right, (((1,), (1,)), ((), ())), preferred_element_type=jnp.float32
    )


def exact_gelu(values):
    return jax.nn.gelu(values, approximate=False)


def masked_scores(query, key_heads, allowed, score_scale):
    raw_scores = (
        jnp.einsum("qhd,khd->hqk", query, key_heads, preferred_element_type=jnp.float32)
        * score_scale
    )
    return jnp.where(allowed[None], raw_scores, MASKED)


def column_term(grad_side, data_side):
    return rows_product(grad_side, data_side)


def permute(values, pairs):
    return lax.ppermute(values, "fsdp", pairs)


def links():
    sibling = [(i, i ^ 1) for i in range(32)]
    near = [(i, i ^ (2 if i & 1 else 4)) for i in range(32)]
    far = [(i, i ^ (4 if i & 1 else 2)) for i in range(32)]
    line = [[(i, (i + 8 * k) % 32) for i in range(32)] for k in range(4)]
    return (sibling, near, far, line)


def chip_place():
    me = lax.axis_index("fsdp")
    return (me // 8, (me // 4) % 2, (me // 2) % 2, me % 2)


def gather_rows(rows):
    return lax.all_gather(rows, "fsdp", axis=0, tiled=False)


def scatter_rows(terms):
    return lax.psum_scatter(terms, "fsdp", scatter_dimension=0, tiled=False).astype(jnp.float32)


def fold_pad(shard):
    count = shard.shape[-2]
    rest = shard[..., D:]
    half = (count + 1) // 2
    left, right = rest[..., :half, :], rest[..., half:, :]
    spare = [(0, 0)] * (shard.ndim - 2) + [(0, 2 * half - count), (0, 0)]
    rest = jnp.concatenate([left, jnp.pad(right, spare)], axis=-1)
    return jnp.concatenate([shard[..., :D], rest], axis=-2)


def unfold_pad(packed, count):
    half, lanes = (count + 1) // 2, FF - D
    rest = packed[..., count : count + half, :]
    rest = jnp.concatenate([rest[..., :lanes], rest[..., lanes:]], axis=-2)[..., :count, :]
    return jnp.concatenate([packed[..., :count, :], rest], axis=-1)


def body(
    tokens, w_qkv, w_out, w_up, w_down, gain_attn, gain_mlp, cotangent, block_counts, seq_lengths
):
    slot_total = tokens.shape[0]
    score_scale = 1.0 / math.sqrt(HD)
    device_index = lax.axis_index("fsdp")
    block_count = lax.dynamic_index_in_dim(block_counts, device_index, keepdims=False)
    device_ids = jnp.arange(block_counts.shape[0], dtype=jnp.int32)
    first_place = jnp.sum(jnp.where(device_ids < device_index, block_counts, 0)) * BLK
    live_rows = block_count * BLK
    stream_total = jnp.sum(block_counts) * BLK
    slot_index = jnp.arange(slot_total, dtype=jnp.int32)
    live_slots = slot_index < live_rows
    rim_offsets = jnp.arange(WIN, dtype=jnp.int32)
    query_place = first_place + slot_index
    before_place = first_place - WIN + rim_offsets
    after_place = first_place + live_rows + rim_offsets
    key_place = jnp.concatenate([before_place, query_place, after_place])
    key_live = jnp.concatenate([before_place >= 0, live_slots, after_place < stream_total])
    key_slot = jnp.concatenate([rim_offsets * 0 - 1, slot_index, rim_offsets * 0 - 1])
    query_seg, query_pos = sequence_places(query_place, seq_lengths)
    key_seg, unused = sequence_places(key_place, seq_lengths)
    in_window = jnp.abs(query_place[:, None] - key_place[None, :]) <= WIN
    allowed = live_slots[:, None] & key_live[None, :] & (
        query_seg[:, None] == key_seg[None, :]
    ) & in_window | jnp.logical_not(live_slots)[:, None] & (
        key_slot[None, :] == slot_index[:, None]
    )
    cosine, sine = rotary_tables(query_pos)
    peers = lax.axis_size("fsdp")
    columns = D // peers
    gains = jnp.zeros((8, D), jnp.bfloat16)
    gains = gains.at[0, :columns].set(gain_attn).at[1, :columns].set(gain_mlp)
    first_rows = gather_rows(jnp.concatenate([w_qkv.T, gains]))
    qkv_full = first_rows[:, : 3 * columns].reshape(3 * D, D)
    gain_a_full = first_rows[:, 3 * columns, :columns].reshape(D)
    gain_m_full = first_rows[:, 3 * columns + 1, :columns].reshape(D)
    up_columns = w_up.shape[1]
    later = jnp.concatenate([w_up.T, w_out.T, fold_pad(w_down.T)])
    later_rows = gather_rows(later)
    up_full = later_rows[:, :up_columns].reshape(2 * FF, D)
    out_full = later_rows[:, up_columns : up_columns + columns].reshape(D, D)
    down_full = unfold_pad(later_rows[:, up_columns + columns :], columns).reshape(D, FF)
    stream = tokens.astype(jnp.float32)
    normed_one, factor_one = norm_parts(stream)
    first_in = (normed_one * gain_a_full.astype(jnp.float32)).astype(jnp.bfloat16)
    joined = cols_product(first_in, qkv_full)
    query = rotate_heads(joined[:, :D].reshape(slot_total, HEADS, HD), cosine, sine).astype(
        jnp.bfloat16
    )
    keys_own = rotate_heads(
        joined[:, D : 2 * D].reshape(slot_total, HEADS, HD), cosine, sine
    ).astype(jnp.bfloat16)
    values_own = joined[:, 2 * D :].astype(jnp.bfloat16)
    pairs = jnp.concatenate([keys_own.reshape(slot_total, D), values_own], axis=1)
    edges = jnp.concatenate(
        [pairs[:WIN], lax.dynamic_slice_in_dim(pairs, live_rows - WIN, WIN, 0)], axis=0
    )
    framed = with_halo(edges, (("fsdp", 0),), WIN)
    all_pairs = jnp.concatenate([framed[:WIN], pairs, framed[3 * WIN :]], axis=0)
    key_heads = all_pairs[:, :D].reshape(-1, HEADS, HD)
    value_heads = all_pairs[:, D:].reshape(-1, HEADS, HD)
    scores = masked_scores(query, key_heads, allowed, score_scale)
    row_top = jnp.max(scores, axis=-1, keepdims=True)
    log_total = row_top + jnp.log(jnp.sum(jnp.exp(scores - row_top), axis=-1, keepdims=True))
    probs_low = jnp.exp(scores - log_total).astype(jnp.bfloat16)
    mixed = (
        jnp.einsum("hqk,khd->qhd", probs_low, value_heads, preferred_element_type=jnp.float32)
        .reshape(slot_total, D)
        .astype(jnp.bfloat16)
    )
    after_attn = stream + cols_product(mixed, out_full)
    normed_two, factor_two = norm_parts(after_attn)
    second_in = (normed_two * gain_m_full.astype(jnp.float32)).astype(jnp.bfloat16)
    projected = cols_product(second_in, up_full)
    gate_half = projected[:, FF:]
    activated, gelu_pull = jax.vjp(exact_gelu, projected[:, :FF])
    hidden = (activated * gate_half).astype(jnp.bfloat16)
    down_out = cols_product(hidden, down_full)
    block_out = jnp.where(live_slots[:, None], after_attn + down_out, 0.0).astype(jnp.bfloat16)
    out_grad = jnp.where(live_slots[:, None], cotangent, jnp.zeros_like(cotangent))
    d_hidden = jnp.dot(out_grad, down_full, preferred_element_type=jnp.float32)
    d_inputs = gelu_pull(d_hidden * gate_half)[0]
    d_projected = jnp.concatenate([d_inputs, d_hidden * activated], axis=1).astype(jnp.bfloat16)
    d_second = jnp.dot(d_projected, up_full, preferred_element_type=jnp.float32)
    grad_gain_m = jnp.sum(normed_two * d_second, axis=0)
    d_after = out_grad.astype(jnp.float32) + norm_back(
        d_second * gain_m_full.astype(jnp.float32), normed_two, factor_two
    )
    d_attn = d_after.astype(jnp.bfloat16)
    d_mixed = jnp.dot(d_attn, out_full, preferred_element_type=jnp.float32).astype(jnp.bfloat16).reshape(slot_total, HEADS, HD)
    scores = masked_scores(query, key_heads, allowed, score_scale)
    probs = jnp.exp(scores - log_total)
    d_probs = jnp.einsum("qhd,khd->hqk", d_mixed, value_heads, preferred_element_type=jnp.float32)
    d_scores = (probs * (d_probs - jnp.sum(probs * d_probs, axis=-1, keepdims=True))).astype(
        jnp.bfloat16
    )
    d_query = (
        jnp.einsum("hqk,khd->qhd", d_scores, key_heads, preferred_element_type=jnp.float32)
        * score_scale
    )
    d_keys = (
        jnp.einsum("hqk,qhd->khd", d_scores, query, preferred_element_type=jnp.float32)
        * score_scale
    )
    d_values = jnp.einsum(
        "hqk,qhd->khd", probs.astype(jnp.bfloat16), d_mixed, preferred_element_type=jnp.float32
    )
    d_pairs = jnp.concatenate([d_keys.reshape(-1, D), d_values.reshape(-1, D)], axis=1)
    grad_edges = jnp.concatenate([d_pairs[:WIN], d_pairs[WIN + slot_total :]], axis=0)
    returned = with_halo(grad_edges.astype(jnp.bfloat16), (("fsdp", 0),), WIN).astype(
        grad_edges.dtype
    )
    own_pairs = d_pairs[WIN : WIN + slot_total]
    own_pairs = own_pairs.at[:WIN].add(returned[:WIN])
    tail_rows = lax.dynamic_slice_in_dim(own_pairs, live_rows - WIN, WIN, 0) + returned[3 * WIN :]
    own_pairs = lax.dynamic_update_slice_in_dim(own_pairs, tail_rows, live_rows - WIN, 0)
    d_query_raw = rotate_back(d_query, cosine, sine).reshape(slot_total, D)
    d_keys_raw = rotate_back(own_pairs[:, :D].reshape(slot_total, HEADS, HD), cosine, sine).reshape(
        slot_total, D
    )
    d_joined = jnp.concatenate([d_query_raw, d_keys_raw, own_pairs[:, D:]], axis=1).astype(
        jnp.bfloat16
    )
    d_first = jnp.dot(d_joined, qkv_full, preferred_element_type=jnp.float32)
    grad_gain_a = jnp.sum(normed_one * d_first, axis=0)
    d_stream = d_after + norm_back(
        d_first * gain_a_full.astype(jnp.float32), normed_one, factor_one
    )
    tokens_grad = jnp.where(live_slots[:, None], d_stream, 0.0)
    down_terms = column_term(out_grad, hidden).astype(jnp.bfloat16).reshape(peers, columns, FF)
    up_terms = column_term(d_projected, second_in).astype(jnp.bfloat16)
    mlp_sum = scatter_rows(
        jnp.concatenate([up_terms.reshape(peers, up_columns, D), fold_pad(down_terms)], axis=1)
    )
    up_sum = mlp_sum[:up_columns].T
    down_sum = unfold_pad(mlp_sum[up_columns:], columns).T
    qkv_terms = column_term(d_joined, first_in).astype(jnp.bfloat16).reshape(peers, 3 * columns, D)
    out_terms = column_term(d_attn, mixed).astype(jnp.bfloat16).reshape(peers, columns, D)
    gain_terms = jnp.stack([grad_gain_a.reshape(peers, columns), grad_gain_m.reshape(peers, columns)], axis=1)
    gain_terms = jnp.pad(gain_terms.astype(jnp.bfloat16), ((0, 0), (0, 6), (0, D - columns)))
    attn_sum = scatter_rows(jnp.concatenate([qkv_terms, out_terms, gain_terms], axis=1))
    qkv_sum = attn_sum[: 3 * columns].T
    out_sum = attn_sum[3 * columns : 4 * columns].T
    gain_a_sum = attn_sum[4 * columns, :columns]
    gain_m_sum = attn_sum[4 * columns + 1, :columns]
    return (block_out, tokens_grad, qkv_sum, out_sum, up_sum, down_sum, gain_a_sum, gain_m_sum)


CHIPS = 16
HALF = 384
ROWS1 = 160
ROWS2 = 272
SLOTS = 256
SPAN = SLOTS + 2 * WIN
PAIR = 2 * HD
PAIRS = HEADS // 2
LIMIT = 48 * 1024 * 1024
AT_LIVE, AT_CORE, AT_TAKE, AT_PUT = 0, 1, 2, 34
VMEM = pltpu.MemorySpace.VMEM
SMEM = pltpu.MemorySpace.SMEM


def nt_dot(left, right):
    return lax.dot_general(left, right, (((1,), (1,)), ((), ())), preferred_element_type=jnp.float32)


def nn_dot(left, right):
    return jnp.dot(left, right, preferred_element_type=jnp.float32)


def tn_dot(left, right):
    return lax.dot_general(left, right, (((0,), (0,)), ((), ())), preferred_element_type=jnp.float32)


def call(kernel, outs, scratch, args, micros):
    spaces = [pl.BlockSpec(memory_space=SMEM)] + [pl.BlockSpec(memory_space=VMEM)] * (len(args) - 1)
    return pl.pallas_call(
        kernel,
        out_shape=[jax.ShapeDtypeStruct(shape, kind) for shape, kind in outs],
        in_specs=spaces,
        out_specs=[pl.BlockSpec(memory_space=VMEM)] * len(outs),
        scratch_shapes=[pltpu.VMEM(shape, kind) for shape, kind in scratch],
        compiler_params=pltpu.CompilerParams(vmem_limit_bytes=LIMIT),
        cost_estimate=pl.CostEstimate(flops=0, bytes_accessed=3_690_000 * micros, transcendentals=0),
    )(*args)


def take_blocks(place, mine, other, copy):
    for stream in (0, 1):
        for held, refs in ((stream, mine), (1 - stream, other)):

            @pl.when(place[AT_CORE] == held)
            def _(stream=stream, refs=refs):
                for chip in range(CHIPS):
                    slot = place[AT_TAKE + 16 * stream + chip]
                    pl.when(slot < 8)(lambda: copy(stream, chip, refs[0], slot))
                    pl.when(slot >= 8)(lambda: copy(stream, chip, refs[1], slot - 8))


def put_rows(place, send, keep, stream, start, value, chips):
    count = value.shape[0] // len(chips)
    value = value.astype(jnp.bfloat16)

    def store(ref):
        for i, chip in enumerate(chips):
            slot = place[AT_PUT + 16 * stream + chip]
            ref[slot, start : start + count, :] = value[i * count : (i + 1) * count]

    pl.when(place[AT_CORE] == stream)(lambda: store(keep))
    pl.when(place[AT_CORE] != stream)(lambda: store(send))


def gain_rows(vector, chip):
    start = min(48 * chip // 128 * 128, D - HALF)
    return jnp.broadcast_to(vector[:, start : start + HALF], (16, HALF))


def project_kernel(place, tokens, gain, mine_a, mine_b, other_a, other_b, cos, sin_a, sin_b, query, pairs, first, weight):
    def copy(stream, chip, ref, slot):
        weight[144 * chip : 144 * chip + 144, HALF * stream : HALF * (stream + 1)] = ref[slot, 0:144, :]

    take_blocks(place, (mine_a, mine_b), (other_a, other_b), copy)
    normed, _ = norm_parts(tokens[...].astype(jnp.float32))
    a1 = (normed * gain[...]).astype(jnp.bfloat16)
    first[...] = a1
    c, sa, sb = cos[...], sin_a[...], sin_b[...]
    for part in range(3):
        for j in range(2):
            base = part * D + HALF * j
            joined = nt_dot(a1, weight[base : base + HALF, :])
            for p in range(3):
                lanes = slice(HALF * j + PAIR * p, HALF * j + PAIR * (p + 1))
                v = joined[:, PAIR * p : PAIR * (p + 1)]
                if part < 2:
                    v = v * c + pltpu.roll(v, 96, 1) * sa + pltpu.roll(v, 32, 1) * sb
                if part == 0:
                    query[:, lanes] = v.astype(jnp.bfloat16)
                else:
                    where = slice((part - 1) * D + lanes.start, (part - 1) * D + lanes.stop)
                    pairs[:, where] = v.astype(jnp.bfloat16)


def frame_pairs(place, pairs, before, after, framed):
    framed[0:WIN, :] = before[...]
    framed[WIN : WIN + SLOTS, :] = pairs[...]
    framed[WIN + SLOTS : SPAN, :] = jnp.zeros((WIN, 2 * D), jnp.bfloat16)
    framed[pl.ds(pl.multiple_of(WIN + place[AT_LIVE], 64), WIN), :] = after[...]


def stack_heads(values, low, high):
    return jnp.concatenate([values * low, values * high], axis=0)


def head_masks():
    lane = lax.broadcasted_iota(jnp.int32, (1, PAIR), 1)
    low = jnp.where(lane < HD, 1.0, 0.0).astype(jnp.bfloat16)
    return (lane < HD, low, 1.0 - low)


def probabilities(query, keys, bias):
    scores = nt_dot(query, keys) * (1.0 / math.sqrt(HD)) + bias
    expos = jnp.exp(scores - jnp.max(scores, axis=-1, keepdims=True))
    return expos * (1.0 / jnp.sum(expos, axis=-1, keepdims=True))


def attend_kernel(place, query, pairs, before, after, bias, mixed, framed):
    frame_pairs(place, pairs, before, after, framed)
    is_low, low, high = head_masks()
    for block in range(2):
        rows, keys = slice(128 * block, 128 * block + 128), slice(128 * block, 128 * block + 256)
        both = jnp.concatenate([bias[rows, :], bias[rows, :]], axis=0)
        for p in range(PAIRS):
            lanes, vlanes = slice(PAIR * p, PAIR * (p + 1)), slice(D + PAIR * p, D + PAIR * (p + 1))
            probs = probabilities(stack_heads(query[rows, lanes], low, high), framed[keys, lanes], both)
            out = nn_dot(probs.astype(jnp.bfloat16), framed[keys, vlanes])
            mixed[rows, lanes] = jnp.where(is_low, out[:128], out[128:]).astype(jnp.bfloat16)


def middle_kernel(
    place, tokens, mixed, mine_a, mine_b, other_a, other_b, gain, cotangent,
    block_out, d_after_out, d_mixed, send, keep,
    w_up, w_out, w_down, d_proj, hidden,
):
    def copy(stream, chip, ref, slot):
        lanes = slice(HALF * stream, HALF * (stream + 1))
        w_up[144 * chip : 144 * chip + 144, lanes] = ref[slot, 0:144, :]
        w_out[48 * chip : 48 * chip + 48, lanes] = ref[slot, 144:192, :]
        w_down[48 * chip : 48 * chip + 48, lanes] = ref[slot, 192:240, :]
        if stream == 0:
            w_down[48 * chip : 48 * chip + 32, 2 * HALF :] = ref[slot, 240:272, :]
        else:
            w_down[48 * chip + 32 : 48 * chip + 48, 2 * HALF :] = ref[slot, 240:256, :]

    take_blocks(place, (mine_a, mine_b), (other_a, other_b), copy)
    after_attn = tokens[...].astype(jnp.float32) + nt_dot(mixed[...], w_out[...])
    normed, factor = norm_parts(after_attn)
    gains = gain[...]
    a2 = (normed * gains).astype(jnp.bfloat16)
    live = lax.broadcasted_iota(jnp.int32, (SLOTS, 1), 0) < place[AT_LIVE]
    grad = jnp.where(live, cotangent[...].astype(jnp.float32), 0.0)
    out_grad = grad.astype(jnp.bfloat16)
    down = jnp.zeros((SLOTS, D), jnp.float32)
    for j in range(3):
        lanes = slice(HALF * j, HALF * (j + 1))
        inputs = nt_dot(a2, w_up[lanes, :])
        gate = nt_dot(a2, w_up[FF + HALF * j : FF + HALF * (j + 1), :])
        cdf = 0.5 * (1.0 + lax.erf(inputs * (1.0 / math.sqrt(2.0))))
        slope = cdf + inputs * (jnp.exp(-0.5 * inputs * inputs) * (1.0 / math.sqrt(2.0 * math.pi)))
        active = inputs * cdf
        low_hidden = (active * gate).astype(jnp.bfloat16)
        hidden[:, lanes] = low_hidden
        down = down + nt_dot(low_hidden, w_down[:, lanes])
        d_hidden = nn_dot(out_grad, w_down[:, lanes])
        d_proj[:, lanes] = (d_hidden * gate * slope).astype(jnp.bfloat16)
        d_proj[:, FF + HALF * j : FF + HALF * (j + 1)] = (d_hidden * active).astype(jnp.bfloat16)
    block_out[...] = jnp.where(live, after_attn + down, 0.0).astype(jnp.bfloat16)
    everyone = list(range(CHIPS))
    d_second = nn_dot(d_proj[...], w_up[...])
    gain_grad = jnp.sum(normed * d_second, axis=0, keepdims=True)
    d_after = grad + norm_back(d_second * gains, normed, factor)
    d_after_out[...] = d_after
    d_attn = d_after.astype(jnp.bfloat16)
    d_mixed[...] = nn_dot(d_attn, w_out[...]).astype(jnp.bfloat16)
    for stream in (0, 1):
        lanes = slice(HALF * stream, HALF * (stream + 1))
        for j in range(2):
            up = tn_dot(d_proj[:, FF * j : FF * (j + 1)], a2[:, lanes])
            put_rows(place, send, keep, stream, 0, up, everyone[8 * j : 8 * j + 8])
        put_rows(place, send, keep, stream, 144, tn_dot(d_attn, mixed[:, lanes]), everyone)
        put_rows(place, send, keep, stream, 192, tn_dot(out_grad, hidden[:, lanes]), everyone)
    rest = tn_dot(out_grad, hidden[:, 2 * HALF :])
    for chip in everyone:
        put_rows(place, send, keep, 0, 240, rest[48 * chip : 48 * chip + 32], [chip])
        put_rows(place, send, keep, 1, 240, rest[48 * chip + 32 : 48 * chip + 48], [chip])
        put_rows(place, send, keep, 1, 256, gain_rows(gain_grad, chip), [chip])


def attend_back_kernel(
    place, query, pairs, before, after, bias, d_mixed,
    d_query, d_own, rim_before, rim_after, framed, d_framed,
):
    frame_pairs(place, pairs, before, after, framed)
    is_low, low, high = head_masks()
    d_framed[256:SPAN, :] = jnp.zeros((SPAN - 256, 2 * D), jnp.float32)
    scale = 1.0 / math.sqrt(HD)
    for block in range(2):
        rows, keys = slice(128 * block, 128 * block + 128), slice(128 * block, 128 * block + 256)
        both = jnp.concatenate([bias[rows, :], bias[rows, :]], axis=0)
        for p in range(PAIRS):
            lanes, vlanes = slice(PAIR * p, PAIR * (p + 1)), slice(D + PAIR * p, D + PAIR * (p + 1))
            q2 = stack_heads(query[rows, lanes], low, high)
            o2 = stack_heads(d_mixed[rows, lanes], low, high)
            k2 = framed[keys, lanes]
            probs = probabilities(q2, k2, both)
            d_probs = nt_dot(o2, framed[keys, vlanes])
            spread = jnp.sum(probs * d_probs, axis=-1, keepdims=True)
            d_scores = (probs * (d_probs - spread)).astype(jnp.bfloat16)
            d_q = nn_dot(d_scores, k2) * scale
            d_query[rows, lanes] = jnp.where(is_low, d_q[:128], d_q[128:])
            d_k = tn_dot(d_scores, q2) * scale
            d_v = tn_dot(probs.astype(jnp.bfloat16), o2)
            if block == 0:
                d_framed[keys, lanes] = d_k
                d_framed[keys, vlanes] = d_v
            else:
                d_framed[keys, lanes] += d_k
                d_framed[keys, vlanes] += d_v
    rim_before[...] = d_framed[0:WIN, :].astype(jnp.bfloat16)
    tail = pl.ds(pl.multiple_of(WIN + place[AT_LIVE], 64), WIN)
    rim_after[...] = d_framed[tail, :].astype(jnp.bfloat16)
    d_own[...] = d_framed[WIN : WIN + SLOTS, :]


def finish_kernel(
    place, tokens, first, gain, weight, d_query, d_own, from_before, from_after, cos, sin_a, sin_b, d_after,
    tokens_grad, send, keep, d_joined, d_pairs,
):
    live = lax.broadcasted_iota(jnp.int32, (SLOTS, 1), 0) < place[AT_LIVE]
    d_pairs[...] = jnp.where(live, d_own[...], 0.0)
    d_pairs[0:WIN, :] += from_before[...].astype(jnp.float32)
    tail = pl.ds(pl.multiple_of(place[AT_LIVE] - WIN, 64), WIN)
    d_pairs[tail, :] += from_after[...].astype(jnp.float32)
    c, sa, sb = cos[...], sin_a[...], sin_b[...]
    for part in range(2):
        source = d_query if part == 0 else d_pairs
        for p in range(PAIRS):
            v = source[:, PAIR * p : PAIR * (p + 1)]
            v = v * c - pltpu.roll(v, 96, 1) * sa - pltpu.roll(v, 32, 1) * sb
            d_joined[:, part * D + PAIR * p : part * D + PAIR * (p + 1)] = v.astype(jnp.bfloat16)
    d_joined[:, 2 * D :] = d_pairs[:, D:].astype(jnp.bfloat16)
    d_first = nn_dot(d_joined[...], weight[...])
    normed, factor = norm_parts(tokens[...].astype(jnp.float32))
    gain_grad = jnp.sum(normed * d_first, axis=0, keepdims=True)
    d_stream = d_after[...] + norm_back(d_first * gain[...], normed, factor)
    tokens_grad[...] = jnp.where(live, d_stream, 0.0)
    everyone = list(range(CHIPS))
    for stream in (0, 1):
        lanes = slice(HALF * stream, HALF * (stream + 1))
        for j in range(2):
            up = tn_dot(d_joined[:, 1152 * j : 1152 * (j + 1)], first[:, lanes])
            put_rows(place, send, keep, stream, 0, up, everyone[8 * j : 8 * j + 8])
        for chip in everyone:
            put_rows(place, send, keep, stream, 144, gain_rows(gain_grad, chip), [chip])


def swap_halves(shard, core, sibling):
    low, high = shard[:, :HALF], shard[:, HALF:]
    own = jnp.where(core == 0, low, high)
    return own, permute(jnp.where(core == 0, high, low), sibling)


def interleave(own, got, core, cuts):
    parts, start = [], 0
    for count in cuts:
        mine, theirs = own[start : start + count], got[start : start + count]
        parts += [jnp.where(core == 0, mine, theirs), jnp.where(core == 0, theirs, mine)]
        start += count
    return parts


def spread_line(block, line):
    return jnp.stack([block] + [permute(block, line[k]) for k in (1, 2, 3)])


def widen(held, pairs):
    return jnp.concatenate([held, permute(held, pairs)])


def reduce_near(send, keep, links_of):
    return keep + permute(send, links_of[0])


def sum_shares(own, others):
    share = own.astype(jnp.float32)
    for other in others:
        share = share + other.astype(jnp.float32)
    return share


def place_table(live_rows):
    z, y, x, core = chip_place()
    chips = jnp.arange(CHIPS, dtype=jnp.int32)
    zz, yy, xx = chips // 4, (chips // 2) % 2, chips % 2
    yr, xr = y ^ yy, x ^ xx
    take, put = [], []
    for near, far in ((yr, xr), (xr, yr)):
        take.append(far * 8 + near * 4 + (z - zz) % 4)
        put.append((1 - near) * 8 + (1 - far) * 4 + (zz - z + 3) % 4)
    head = jnp.stack([live_rows, core]).astype(jnp.int32)
    return jnp.concatenate([head] + take + put).astype(jnp.int32)


def fused_body(
    tokens, w_qkv, w_out, w_up, w_down, gain_attn, gain_mlp, cotangent, block_counts, seq_lengths
):
    bf16, f32 = jnp.bfloat16, jnp.float32
    device_index = lax.axis_index("fsdp")
    core = device_index % 2
    wires = links()
    sibling, near, far, line = wires
    gains = jnp.zeros((8, D), bf16)
    gain_pair = jnp.pad(jnp.stack([gain_attn, gain_mlp]), ((0, 6), (0, HALF - 24)))
    gains = jnp.concatenate([gain_pair, gain_pair], axis=1)
    own, got = swap_halves(jnp.concatenate([w_qkv.T, gains]), core, sibling)
    block = jnp.concatenate(interleave(own, got, core, (72, 8)))
    lined_one = spread_line(block, line)
    mine_one = widen(lined_one, near)
    other_one = permute(mine_one, sibling)
    far_one = permute(mine_one, far)
    other_far_one = permute(far_one, sibling)
    block_counts, seq_lengths, _ = lax.optimization_barrier((block_counts, seq_lengths, lined_one))
    block_count = lax.dynamic_index_in_dim(block_counts, device_index, keepdims=False)
    device_ids = jnp.arange(block_counts.shape[0], dtype=jnp.int32)
    first_place = jnp.sum(jnp.where(device_ids < device_index, block_counts, 0)) * BLK
    live_rows = block_count * BLK
    stream_total = jnp.sum(block_counts) * BLK
    place = place_table(live_rows)
    slot_index = jnp.arange(SLOTS, dtype=jnp.int32)
    live_slots = slot_index < live_rows
    query_place = first_place + slot_index
    query_seg, query_pos = sequence_places(query_place, seq_lengths)
    key_slot = (slot_index // BLK * BLK)[:, None] + jnp.arange(256, dtype=jnp.int32)[None, :] - WIN
    key_place = first_place + key_slot
    ends = jnp.cumsum(seq_lengths)
    key_seg = jnp.sum((key_place[:, :, None] >= ends).astype(jnp.int32), axis=2)
    allowed = (
        live_slots[:, None]
        & (key_place >= 0)
        & (key_place < stream_total)
        & (query_seg[:, None] == key_seg)
        & (jnp.abs(query_place[:, None] - key_place) <= WIN)
    ) | (jnp.logical_not(live_slots)[:, None] & (key_slot == slot_index[:, None]))
    bias = jnp.where(allowed, 0.0, MASKED).astype(f32)
    cosine, sine = rotary_tables(query_pos)
    cosine, sine = (jnp.concatenate([t[:, 0], t[:, 0]], axis=1) for t in (cosine, sine))
    front = (jnp.arange(PAIR) % HD < HD // 2)[None, :]
    sin_a, sin_b = jnp.where(front, -sine, 0.0), jnp.where(front, 0.0, sine)
    zz, yy, xx = (jnp.arange(CHIPS, dtype=jnp.int32) // 4, jnp.arange(CHIPS) // 2 % 2, jnp.arange(CHIPS) % 2)
    taken = jnp.where(core == 0, place[AT_TAKE : AT_TAKE + 16], place[AT_TAKE + 16 : AT_TAKE + 32])
    chosen = (taken[:, None] == jnp.arange(CHIPS)[None, :]).astype(f32)
    flat = jnp.concatenate(
        [held[:, row, :24] for held in (mine_one, far_one) for row in (144, 152, 145, 153)], axis=1
    ).astype(f32)
    flat = jnp.concatenate([flat[:, :96], flat[:, 96:]], axis=0)
    flat = jnp.sum(chosen[:, :, None] * flat[None], axis=1)
    gain_a, gain_m = flat[:, :48].reshape(1, D), flat[:, 48:].reshape(1, D)
    query, pairs, first, weight = call(
        project_kernel,
        [((SLOTS, D), bf16), ((SLOTS, 2 * D), bf16), ((SLOTS, D), bf16), ((3 * D, D), bf16)],
        [],
        [place, tokens, gain_a, mine_one, far_one, other_one, other_far_one, cosine, sin_a, sin_b],
        6,
    )
    shard = jnp.concatenate([w_up.T, w_out.T, w_down.T[:, :D]])
    rest = w_down.T[:, D:]
    low, high = shard[:, :HALF], shard[:, HALF:]
    own = jnp.concatenate([jnp.where(core == 0, low, high), rest[:8]])
    got = permute(jnp.concatenate([jnp.where(core == 0, high, low), rest[:8]]), sibling)
    tail = jnp.where(
        core == 0,
        jnp.concatenate([rest, got[120:128]]),
        jnp.concatenate([rest[8:], jnp.zeros((16, HALF), bf16)]),
    )
    block = jnp.concatenate(interleave(own, got, core, (72, 24, 24)) + [tail])
    block, _ = lax.optimization_barrier((block, lined_one))
    lined_two, _ = lax.optimization_barrier((spread_line(block, line), far_one))
    near_two = permute(lined_two, near)
    lined_two, pairs = lax.optimization_barrier((lined_two, pairs))
    mine_two = jnp.concatenate([lined_two, near_two])
    far_two = permute(mine_two, far)
    up = [(i, i + 1) for i in range(31)]
    down = [(i + 1, i) for i in range(31)]
    before = permute(lax.dynamic_slice_in_dim(pairs, live_rows - WIN, WIN, 0), up)
    after = permute(pairs[:WIN], down)
    (mixed,) = call(
        attend_kernel,
        [((SLOTS, D), bf16)],
        [((SPAN, 2 * D), bf16)],
        [place, query, pairs, before, after, bias],
        3,
    )
    other_two = permute(mine_two, sibling)
    far_two, other_two, mixed = lax.optimization_barrier((far_two, other_two, mixed))
    other_far_two = permute(far_two, sibling)
    block_out, d_after, d_mixed, send, keep = call(
        middle_kernel,
        [((SLOTS, D), bf16), ((SLOTS, D), f32), ((SLOTS, D), bf16), ((CHIPS, ROWS2, HALF), bf16), ((CHIPS, ROWS2, HALF), bf16)],
        [((2 * FF, D), bf16), ((D, D), bf16), ((D, FF), bf16), ((SLOTS, 2 * FF), bf16), ((SLOTS, FF), bf16)],
        [place, tokens, mixed, mine_two, far_two, other_two, other_far_two, gain_m, cotangent],
        18,
    )
    d_query, d_own, rim_before, rim_after = call(
        attend_back_kernel,
        [((SLOTS, D), f32), ((SLOTS, 2 * D), f32), ((WIN, 2 * D), bf16), ((WIN, 2 * D), bf16)],
        [((SPAN, 2 * D), bf16), ((SPAN, 2 * D), f32)],
        [place, query, pairs, before, after, bias, d_mixed],
        8,
    )
    from_after = permute(rim_before, down)
    from_before = permute(rim_after, up)
    total = reduce_near(send, keep, wires)
    leaving, staying = total[:8], total[8:]
    leaving, from_after, from_before = lax.optimization_barrier((leaving, from_after, from_before))
    arrived = permute(leaving, near)
    tokens_grad, send_qkv, keep_qkv = call(
        finish_kernel,
        [((SLOTS, D), f32), ((CHIPS, ROWS1, HALF), bf16), ((CHIPS, ROWS1, HALF), bf16)],
        [((SLOTS, 3 * D), bf16), ((SLOTS, 2 * D), f32)],
        [place, tokens, first, gain_a, weight, d_query, d_own, from_before, from_after, cosine, sin_a, sin_b, d_after],
        9,
    )
    total = staying + arrived
    total, send_qkv, keep_qkv = lax.optimization_barrier((total, send_qkv, keep_qkv))
    leaving, staying = total[:4], total[4:]
    arrived = permute(leaving, far)
    total_qkv = reduce_near(send_qkv, keep_qkv, wires)
    leave_qkv, stay_qkv = total_qkv[:8], total_qkv[8:]
    arrived_qkv = permute(leave_qkv, near)
    staying, stay_qkv = lax.optimization_barrier((staying, stay_qkv))
    total = staying + arrived
    last = [permute(total[k], line[k + 1]) for k in range(3)]
    total_qkv = stay_qkv + arrived_qkv
    share, total_qkv = lax.optimization_barrier((total[3], total_qkv))
    share = sum_shares(share, last)
    arrived_qkv = permute(total_qkv[:4], far)
    stay_qkv, share = lax.optimization_barrier((total_qkv[4:], share))
    total_qkv = stay_qkv + arrived_qkv
    last_qkv = [permute(total_qkv[k], line[k + 1]) for k in range(3)]
    chip = device_index // 2
    lane = 48 * chip - jnp.minimum(48 * chip // 128 * 128, D - HALF) + 24 * core

    def part(block, start, count, whose):
        return lax.dynamic_slice_in_dim(block, start + count * whose, count, 0)

    gain_row = lax.dynamic_slice_in_dim(share[256:264], lane - 24 * core, 48, 1)
    gain_row = jnp.pad(gain_row, ((0, 0), (0, HALF - 48)))
    cuts = ((0, 72), (144, 24), (192, 24))
    theirs = jnp.concatenate(
        [part(share, s, n, 1 - core) for s, n in cuts] + [jnp.where(core == 0, share[264:272], gain_row)]
    )
    own = jnp.concatenate([part(share, s, n, core) for s, n in cuts])
    got = permute(theirs, sibling)
    both = jnp.concatenate(
        [jnp.where(core == 0, own, got[:120]), jnp.where(core == 0, got[:120], own)], axis=1
    )
    last = jnp.where(
        core == 0, share[240:264], jnp.concatenate([got[120:128], share[240:256]])
    )
    up_sum, out_sum = both[:72].T, both[72:96].T
    down_sum = jnp.concatenate([both[96:], last], axis=1).T
    gain_m_sum = jnp.where(core == 0, got[120, :24], gain_row[0, 24:48])
    share = sum_shares(total_qkv[3], last_qkv)
    got = permute(part(share, 0, 72, 1 - core), sibling)
    own = part(share, 0, 72, core)
    qkv_sum = jnp.concatenate([jnp.where(core == 0, own, got), jnp.where(core == 0, got, own)], axis=1).T
    gain_a_sum = lax.dynamic_slice(share, (144, lane), (1, 24))[0]
    return (block_out, tokens_grad, qkv_sum, out_sum, up_sum, down_sum, gain_a_sum, gain_m_sum)


def solution(mesh):
    plan = fused_body if mesh.shape["fsdp"] == 32 else body
    placed = (
        P("fsdp", None),
        P(None, "fsdp"),
        P(None, "fsdp"),
        P(None, "fsdp"),
        P(None, "fsdp"),
        P("fsdp"),
        P("fsdp"),
        P("fsdp", None),
        P(),
        P(),
    )
    return jax.shard_map(
        plan,
        mesh=mesh,
        in_specs=placed,
        out_specs=(
            P("fsdp", None),
            P("fsdp", None),
            P(None, "fsdp"),
            P(None, "fsdp"),
            P(None, "fsdp"),
            P(None, "fsdp"),
            P("fsdp"),
            P("fsdp"),
        ),
        check_vma=False,
    )
```

```python
import math

import jax
import jax.numpy as jnp
from jax import lax
from jax.experimental import pallas as pl
from jax.experimental.pallas import tpu as pltpu
from jax.sharding import PartitionSpec as P

D = 768
HEADS = 12
HD = 64
FF = 1152
BLK = 128
WIN = 64


EPSILON = 1e-05
MASKED = -1e30


def with_halo(shard, sides, width):
    for axis, dim in sides:
        peers, length = (lax.axis_size(axis), shard.shape[dim])
        up = [(i, (i + 1) % peers) for i in range(peers - 1)]
        down = [(j, i) for i, j in up]
        last = lax.slice_in_dim(shard, length - width, length, axis=dim)
        initial = lax.slice_in_dim(shard, 0, width, axis=dim)
        before = lax.ppermute(last, axis, up)
        after = lax.ppermute(initial, axis, down)
        shard = jnp.concatenate([before, shard, after], axis=dim)
    return shard


def norm_parts(values):
    center = values - jnp.mean(values, axis=-1, keepdims=True)
    factor = lax.rsqrt(jnp.mean(center * center, axis=-1, keepdims=True) + EPSILON)
    return (center * factor, factor)


def norm_back(grad_normed, normed, factor):
    return factor * (
        grad_normed
        - jnp.mean(grad_normed, axis=-1, keepdims=True)
        - normed * jnp.mean(grad_normed * normed, axis=-1, keepdims=True)
    )


def sequence_places(places, lengths):
    ends = jnp.cumsum(lengths)
    starts = ends - lengths
    segment = jnp.sum((places[:, None] >= ends[None, :]).astype(jnp.int32), axis=1)
    picked = segment[:, None] == jnp.arange(lengths.shape[0], dtype=jnp.int32)[None, :]
    start = jnp.sum(jnp.where(picked, starts[None, :], 0), axis=1)
    return (segment, places - start)


def rotary_tables(position):
    half = HD // 2
    freq = jnp.power(10000.0, -(jnp.arange(half, dtype=jnp.float32) * (2.0 / HD)))
    angle = position.astype(jnp.float32)[:, None] * freq[None, :]
    angle = jnp.concatenate([angle, angle], axis=1)[:, None, :]
    return (jnp.cos(angle), jnp.sin(angle))


def rotate_heads(values, cosine, sine):
    half = HD // 2
    turned = jnp.concatenate([-values[..., half:], values[..., :half]], axis=-1)
    return values * cosine + turned * sine


def rotate_back(grads, cosine, sine):
    half = HD // 2
    spun = grads * sine
    return grads * cosine + jnp.concatenate([spun[..., half:], -spun[..., :half]], axis=-1)


def rows_product(left, right):
    return lax.dot_general(
        left, right, (((0,), (0,)), ((), ())), preferred_element_type=jnp.float32
    )


def cols_product(left, right):
    return lax.dot_general(
        left, right, (((1,), (1,)), ((), ())), preferred_element_type=jnp.float32
    )


def exact_gelu(values):
    return jax.nn.gelu(values, approximate=False)


def masked_scores(query, key_heads, allowed, score_scale):
    raw_scores = (
        jnp.einsum("qhd,khd->hqk", query, key_heads, preferred_element_type=jnp.float32)
        * score_scale
    )
    return jnp.where(allowed[None], raw_scores, MASKED)


def column_term(grad_side, data_side):
    return rows_product(grad_side, data_side)


def permute(values, pairs):
    return lax.ppermute(values, "fsdp", pairs)


def links():
    sibling = [(i, i ^ 1) for i in range(32)]
    near = [(i, i ^ (2 if i & 1 else 4)) for i in range(32)]
    far = [(i, i ^ (4 if i & 1 else 2)) for i in range(32)]
    line = [[(i, (i + 8 * k) % 32) for i in range(32)] for k in range(4)]
    return (sibling, near, far, line)


def chip_place():
    me = lax.axis_index("fsdp")
    return (me // 8, (me // 4) % 2, (me // 2) % 2, me % 2)


def gather_rows(rows):
    return lax.all_gather(rows, "fsdp", axis=0, tiled=False)


def scatter_rows(terms):
    return lax.psum_scatter(terms, "fsdp", scatter_dimension=0, tiled=False).astype(jnp.float32)


def fold_pad(shard):
    count = shard.shape[-2]
    rest = shard[..., D:]
    half = (count + 1) // 2
    left, right = rest[..., :half, :], rest[..., half:, :]
    spare = [(0, 0)] * (shard.ndim - 2) + [(0, 2 * half - count), (0, 0)]
    rest = jnp.concatenate([left, jnp.pad(right, spare)], axis=-1)
    return jnp.concatenate([shard[..., :D], rest], axis=-2)


def unfold_pad(packed, count):
    half, lanes = (count + 1) // 2, FF - D
    rest = packed[..., count : count + half, :]
    rest = jnp.concatenate([rest[..., :lanes], rest[..., lanes:]], axis=-2)[..., :count, :]
    return jnp.concatenate([packed[..., :count, :], rest], axis=-1)


def body(
    tokens, w_qkv, w_out, w_up, w_down, gain_attn, gain_mlp, cotangent, block_counts, seq_lengths
):
    slot_total = tokens.shape[0]
    score_scale = 1.0 / math.sqrt(HD)
    device_index = lax.axis_index("fsdp")
    block_count = lax.dynamic_index_in_dim(block_counts, device_index, keepdims=False)
    device_ids = jnp.arange(block_counts.shape[0], dtype=jnp.int32)
    first_place = jnp.sum(jnp.where(device_ids < device_index, block_counts, 0)) * BLK
    live_rows = block_count * BLK
    stream_total = jnp.sum(block_counts) * BLK
    slot_index = jnp.arange(slot_total, dtype=jnp.int32)
    live_slots = slot_index < live_rows
    rim_offsets = jnp.arange(WIN, dtype=jnp.int32)
    query_place = first_place + slot_index
    before_place = first_place - WIN + rim_offsets
    after_place = first_place + live_rows + rim_offsets
    key_place = jnp.concatenate([before_place, query_place, after_place])
    key_live = jnp.concatenate([before_place >= 0, live_slots, after_place < stream_total])
    key_slot = jnp.concatenate([rim_offsets * 0 - 1, slot_index, rim_offsets * 0 - 1])
    query_seg, query_pos = sequence_places(query_place, seq_lengths)
    key_seg, unused = sequence_places(key_place, seq_lengths)
    in_window = jnp.abs(query_place[:, None] - key_place[None, :]) <= WIN
    allowed = live_slots[:, None] & key_live[None, :] & (
        query_seg[:, None] == key_seg[None, :]
    ) & in_window | jnp.logical_not(live_slots)[:, None] & (
        key_slot[None, :] == slot_index[:, None]
    )
    cosine, sine = rotary_tables(query_pos)
    peers = lax.axis_size("fsdp")
    columns = D // peers
    gains = jnp.zeros((8, D), jnp.bfloat16)
    gains = gains.at[0, :columns].set(gain_attn).at[1, :columns].set(gain_mlp)
    first_rows = gather_rows(jnp.concatenate([w_qkv.T, gains]))
    qkv_full = first_rows[:, : 3 * columns].reshape(3 * D, D)
    gain_a_full = first_rows[:, 3 * columns, :columns].reshape(D)
    gain_m_full = first_rows[:, 3 * columns + 1, :columns].reshape(D)
    up_columns = w_up.shape[1]
    later = jnp.concatenate([w_up.T, w_out.T, fold_pad(w_down.T)])
    later_rows = gather_rows(later)
    up_full = later_rows[:, :up_columns].reshape(2 * FF, D)
    out_full = later_rows[:, up_columns : up_columns + columns].reshape(D, D)
    down_full = unfold_pad(later_rows[:, up_columns + columns :], columns).reshape(D, FF)
    stream = tokens.astype(jnp.float32)
    normed_one, factor_one = norm_parts(stream)
    first_in = (normed_one * gain_a_full.astype(jnp.float32)).astype(jnp.bfloat16)
    joined = cols_product(first_in, qkv_full)
    query = rotate_heads(joined[:, :D].reshape(slot_total, HEADS, HD), cosine, sine).astype(
        jnp.bfloat16
    )
    keys_own = rotate_heads(
        joined[:, D : 2 * D].reshape(slot_total, HEADS, HD), cosine, sine
    ).astype(jnp.bfloat16)
    values_own = joined[:, 2 * D :].astype(jnp.bfloat16)
    pairs = jnp.concatenate([keys_own.reshape(slot_total, D), values_own], axis=1)
    edges = jnp.concatenate(
        [pairs[:WIN], lax.dynamic_slice_in_dim(pairs, live_rows - WIN, WIN, 0)], axis=0
    )
    framed = with_halo(edges, (("fsdp", 0),), WIN)
    all_pairs = jnp.concatenate([framed[:WIN], pairs, framed[3 * WIN :]], axis=0)
    key_heads = all_pairs[:, :D].reshape(-1, HEADS, HD)
    value_heads = all_pairs[:, D:].reshape(-1, HEADS, HD)
    scores = masked_scores(query, key_heads, allowed, score_scale)
    row_top = jnp.max(scores, axis=-1, keepdims=True)
    log_total = row_top + jnp.log(jnp.sum(jnp.exp(scores - row_top), axis=-1, keepdims=True))
    probs_low = jnp.exp(scores - log_total).astype(jnp.bfloat16)
    mixed = (
        jnp.einsum("hqk,khd->qhd", probs_low, value_heads, preferred_element_type=jnp.float32)
        .reshape(slot_total, D)
        .astype(jnp.bfloat16)
    )
    after_attn = stream + cols_product(mixed, out_full)
    normed_two, factor_two = norm_parts(after_attn)
    second_in = (normed_two * gain_m_full.astype(jnp.float32)).astype(jnp.bfloat16)
    projected = cols_product(second_in, up_full)
    gate_half = projected[:, FF:]
    activated, gelu_pull = jax.vjp(exact_gelu, projected[:, :FF])
    hidden = (activated * gate_half).astype(jnp.bfloat16)
    down_out = cols_product(hidden, down_full)
    block_out = jnp.where(live_slots[:, None], after_attn + down_out, 0.0).astype(jnp.bfloat16)
    out_grad = jnp.where(live_slots[:, None], cotangent, jnp.zeros_like(cotangent))
    d_hidden = jnp.dot(out_grad, down_full, preferred_element_type=jnp.float32)
    d_inputs = gelu_pull(d_hidden * gate_half)[0]
    d_projected = jnp.concatenate([d_inputs, d_hidden * activated], axis=1).astype(jnp.bfloat16)
    d_second = jnp.dot(d_projected, up_full, preferred_element_type=jnp.float32)
    grad_gain_m = jnp.sum(normed_two * d_second, axis=0)
    d_after = out_grad.astype(jnp.float32) + norm_back(
        d_second * gain_m_full.astype(jnp.float32), normed_two, factor_two
    )
    d_attn = d_after.astype(jnp.bfloat16)
    d_mixed = jnp.dot(d_attn, out_full, preferred_element_type=jnp.float32).astype(jnp.bfloat16).reshape(slot_total, HEADS, HD)
    scores = masked_scores(query, key_heads, allowed, score_scale)
    probs = jnp.exp(scores - log_total)
    d_probs = jnp.einsum("qhd,khd->hqk", d_mixed, value_heads, preferred_element_type=jnp.float32)
    d_scores = (probs * (d_probs - jnp.sum(probs * d_probs, axis=-1, keepdims=True))).astype(
        jnp.bfloat16
    )
    d_query = (
        jnp.einsum("hqk,khd->qhd", d_scores, key_heads, preferred_element_type=jnp.float32)
        * score_scale
    )
    d_keys = (
        jnp.einsum("hqk,qhd->khd", d_scores, query, preferred_element_type=jnp.float32)
        * score_scale
    )
    d_values = jnp.einsum(
        "hqk,qhd->khd", probs.astype(jnp.bfloat16), d_mixed, preferred_element_type=jnp.float32
    )
    d_pairs = jnp.concatenate([d_keys.reshape(-1, D), d_values.reshape(-1, D)], axis=1)
    grad_edges = jnp.concatenate([d_pairs[:WIN], d_pairs[WIN + slot_total :]], axis=0)
    returned = with_halo(grad_edges.astype(jnp.bfloat16), (("fsdp", 0),), WIN).astype(
        grad_edges.dtype
    )
    own_pairs = d_pairs[WIN : WIN + slot_total]
    own_pairs = own_pairs.at[:WIN].add(returned[:WIN])
    tail_rows = lax.dynamic_slice_in_dim(own_pairs, live_rows - WIN, WIN, 0) + returned[3 * WIN :]
    own_pairs = lax.dynamic_update_slice_in_dim(own_pairs, tail_rows, live_rows - WIN, 0)
    d_query_raw = rotate_back(d_query, cosine, sine).reshape(slot_total, D)
    d_keys_raw = rotate_back(own_pairs[:, :D].reshape(slot_total, HEADS, HD), cosine, sine).reshape(
        slot_total, D
    )
    d_joined = jnp.concatenate([d_query_raw, d_keys_raw, own_pairs[:, D:]], axis=1).astype(
        jnp.bfloat16
    )
    d_first = jnp.dot(d_joined, qkv_full, preferred_element_type=jnp.float32)
    grad_gain_a = jnp.sum(normed_one * d_first, axis=0)
    d_stream = d_after + norm_back(
        d_first * gain_a_full.astype(jnp.float32), normed_one, factor_one
    )
    tokens_grad = jnp.where(live_slots[:, None], d_stream, 0.0)
    down_terms = column_term(out_grad, hidden).astype(jnp.bfloat16).reshape(peers, columns, FF)
    up_terms = column_term(d_projected, second_in).astype(jnp.bfloat16)
    mlp_sum = scatter_rows(
        jnp.concatenate([up_terms.reshape(peers, up_columns, D), fold_pad(down_terms)], axis=1)
    )
    up_sum = mlp_sum[:up_columns].T
    down_sum = unfold_pad(mlp_sum[up_columns:], columns).T
    qkv_terms = column_term(d_joined, first_in).astype(jnp.bfloat16).reshape(peers, 3 * columns, D)
    out_terms = column_term(d_attn, mixed).astype(jnp.bfloat16).reshape(peers, columns, D)
    gain_terms = jnp.stack([grad_gain_a.reshape(peers, columns), grad_gain_m.reshape(peers, columns)], axis=1)
    gain_terms = jnp.pad(gain_terms.astype(jnp.bfloat16), ((0, 0), (0, 6), (0, D - columns)))
    attn_sum = scatter_rows(jnp.concatenate([qkv_terms, out_terms, gain_terms], axis=1))
    qkv_sum = attn_sum[: 3 * columns].T
    out_sum = attn_sum[3 * columns : 4 * columns].T
    gain_a_sum = attn_sum[4 * columns, :columns]
    gain_m_sum = attn_sum[4 * columns + 1, :columns]
    return (block_out, tokens_grad, qkv_sum, out_sum, up_sum, down_sum, gain_a_sum, gain_m_sum)


CHIPS = 16
HALF = 384
ROWS1 = 160
ROWS2 = 272
SLOTS = 256
SPAN = SLOTS + 2 * WIN
PAIR = 2 * HD
PAIRS = HEADS // 2
LIMIT = 48 * 1024 * 1024
AT_LIVE, AT_CORE, AT_CHIP, AT_PUT = 0, 1, 2, 34
VMEM = pltpu.MemorySpace.VMEM
SMEM = pltpu.MemorySpace.SMEM


def nt_dot(left, right):
    return lax.dot_general(left, right, (((1,), (1,)), ((), ())), preferred_element_type=jnp.float32)


def nn_dot(left, right):
    return jnp.dot(left, right, preferred_element_type=jnp.float32)


def tn_dot(left, right):
    return lax.dot_general(left, right, (((0,), (0,)), ((), ())), preferred_element_type=jnp.float32)


def call(kernel, outs, scratch, args, micros, blocks=0):
    whole = len(args) - blocks - 1
    spaces = [pl.BlockSpec(memory_space=SMEM)] + [pl.BlockSpec(memory_space=VMEM)] * whole
    spaces += [pl.BlockSpec(memory_space=pl.ANY)] * blocks
    semaphores = [pltpu.SemaphoreType.DMA((2 * CHIPS, 4))] if blocks else []
    return pl.pallas_call(
        kernel,
        out_shape=[jax.ShapeDtypeStruct(shape, kind) for shape, kind in outs],
        in_specs=spaces,
        out_specs=[pl.BlockSpec(memory_space=VMEM)] * len(outs),
        scratch_shapes=[pltpu.VMEM(shape, kind) for shape, kind in scratch] + semaphores,
        compiler_params=pltpu.CompilerParams(vmem_limit_bytes=LIMIT),
        cost_estimate=pl.CostEstimate(flops=0, bytes_accessed=3_690_000 * micros, transcendentals=0),
    )(*args)


def block_copies(place, refs, weight, done, kind, start, count):
    copies = []
    for slot in range(2 * CHIPS):
        chip = place[AT_CHIP + slot]
        core = place[AT_CORE] if slot < CHIPS else 1 - place[AT_CORE]
        rows = pl.ds(pl.multiple_of(chip * count, 16), count)
        lanes = pl.ds(pl.multiple_of(core * HALF, 128), HALF)
        source = refs[slot // 4].at[slot % 4, start : start + count, :]
        copies.append(pltpu.make_async_copy(source, weight.at[rows, lanes], done.at[slot, kind]))
    return copies


def rest_copies(place, refs, weight, done, core):
    copies = []
    for slot in range(2 * CHIPS):
        stream = core if slot < CHIPS else 1 - core
        count = 32 if stream == 0 else 16
        first = pl.multiple_of(place[AT_CHIP + slot] * 48 + (0 if stream == 0 else 32), 16)
        source = refs[slot // 4].at[slot % 4, 240 : 240 + count, :]
        copies.append(
            pltpu.make_async_copy(source, weight.at[pl.ds(first, count), 2 * HALF :], done.at[slot, 3])
        )
    return copies


def go(copies):
    for copy in copies:
        copy.start()


def land(copies):
    for copy in copies:
        copy.wait()


def put_rows(place, send, keep, stream, start, value, chips):
    count = value.shape[0] // len(chips)
    value = value.astype(jnp.bfloat16)

    def store(ref):
        for i, chip in enumerate(chips):
            slot = place[AT_PUT + 16 * stream + chip]
            ref[slot, start : start + count, :] = value[i * count : (i + 1) * count]

    pl.when(place[AT_CORE] == stream)(lambda: store(keep))
    pl.when(place[AT_CORE] != stream)(lambda: store(send))


def put_both(place, send, keep, start, value, chips):
    for stream in (0, 1):
        put_rows(place, send, keep, stream, start, value[:, HALF * stream : HALF * (stream + 1)], chips)


def gain_rows(vector, chip):
    start = min(48 * chip // 128 * 128, D - HALF)
    return jnp.broadcast_to(vector[:, start : start + HALF], (16, HALF))


def project_kernel(place, tokens, gain, cos, sin_a, sin_b, *rest):
    refs, (query, pairs, first, weight, done) = rest[:8], rest[8:]
    copies = block_copies(place, refs, weight, done, 0, 0, 144)
    go(copies)
    normed, _ = norm_parts(tokens[...].astype(jnp.float32))
    a1 = (normed * gain[...]).astype(jnp.bfloat16)
    first[...] = a1
    c, sa, sb = cos[...], sin_a[...], sin_b[...]
    land(copies)
    for part in range(3):
        for j in range(2):
            base = part * D + HALF * j
            joined = nt_dot(a1, weight[base : base + HALF, :])
            for p in range(3):
                lanes = slice(HALF * j + PAIR * p, HALF * j + PAIR * (p + 1))
                v = joined[:, PAIR * p : PAIR * (p + 1)]
                if part < 2:
                    v = v * c + pltpu.roll(v, 96, 1) * sa + pltpu.roll(v, 32, 1) * sb
                if part == 0:
                    query[:, lanes] = v.astype(jnp.bfloat16)
                else:
                    where = slice((part - 1) * D + lanes.start, (part - 1) * D + lanes.stop)
                    pairs[:, where] = v.astype(jnp.bfloat16)


def frame_pairs(place, pairs, before, after, framed):
    framed[0:WIN, :] = before[...]
    framed[WIN : WIN + SLOTS, :] = pairs[...]
    framed[WIN + SLOTS : SPAN, :] = jnp.zeros((WIN, 2 * D), jnp.bfloat16)
    framed[pl.ds(pl.multiple_of(WIN + place[AT_LIVE], 64), WIN), :] = after[...]


def stack_heads(values, low, high):
    return jnp.concatenate([values * low, values * high], axis=0)


def head_masks():
    lane = lax.broadcasted_iota(jnp.int32, (1, PAIR), 1)
    low = jnp.where(lane < HD, 1.0, 0.0).astype(jnp.bfloat16)
    return (lane < HD, low, 1.0 - low)


def probabilities(query, keys, bias):
    scores = nt_dot(query, keys) * (1.0 / math.sqrt(HD)) + bias
    expos = jnp.exp(scores - jnp.max(scores, axis=-1, keepdims=True))
    return expos * (1.0 / jnp.sum(expos, axis=-1, keepdims=True))


def attend_kernel(place, query, pairs, before, after, bias, mixed, framed):
    frame_pairs(place, pairs, before, after, framed)
    is_low, low, high = head_masks()
    for block in range(2):
        rows, keys = slice(128 * block, 128 * block + 128), slice(128 * block, 128 * block + 256)
        both = jnp.concatenate([bias[rows, :], bias[rows, :]], axis=0)
        for p in range(PAIRS):
            lanes, vlanes = slice(PAIR * p, PAIR * (p + 1)), slice(D + PAIR * p, D + PAIR * (p + 1))
            probs = probabilities(stack_heads(query[rows, lanes], low, high), framed[keys, lanes], both)
            out = nn_dot(probs.astype(jnp.bfloat16), framed[keys, vlanes])
            mixed[rows, lanes] = jnp.where(is_low, out[:128], out[128:]).astype(jnp.bfloat16)


def middle_kernel(place, tokens, mixed, gain, cotangent, *rest):
    refs = rest[:8]
    block_out, d_after_out, d_mixed, send, keep, w_up, w_out, w_down, d_proj, hidden, done = rest[8:]
    out_copies = block_copies(place, refs, w_out, done, 0, 144, 48)
    up_copies = block_copies(place, refs, w_up, done, 1, 0, 144)
    down_copies = block_copies(place, refs, w_down, done, 2, 192, 48)
    go(out_copies)
    go(up_copies)
    go(down_copies)
    for core in (0, 1):
        pl.when(place[AT_CORE] == core)(lambda: go(rest_copies(place, refs, w_down, done, core)))
    land(out_copies)
    after_attn = tokens[...].astype(jnp.float32) + nt_dot(mixed[...], w_out[...])
    normed, factor = norm_parts(after_attn)
    gains = gain[...]
    a2 = (normed * gains).astype(jnp.bfloat16)
    live = lax.broadcasted_iota(jnp.int32, (SLOTS, 1), 0) < place[AT_LIVE]
    grad = jnp.where(live, cotangent[...].astype(jnp.float32), 0.0)
    out_grad = grad.astype(jnp.bfloat16)
    down = jnp.zeros((SLOTS, D), jnp.float32)
    land(up_copies)
    land(down_copies)
    for core in (0, 1):
        pl.when(place[AT_CORE] == core)(lambda: land(rest_copies(place, refs, w_down, done, core)))
    for j in range(3):
        lanes = slice(HALF * j, HALF * (j + 1))
        inputs = nt_dot(a2, w_up[lanes, :])
        gate = nt_dot(a2, w_up[FF + HALF * j : FF + HALF * (j + 1), :])
        cdf = 0.5 * (1.0 + lax.erf(inputs * (1.0 / math.sqrt(2.0))))
        slope = cdf + inputs * (jnp.exp(-0.5 * inputs * inputs) * (1.0 / math.sqrt(2.0 * math.pi)))
        active = inputs * cdf
        low_hidden = (active * gate).astype(jnp.bfloat16)
        hidden[:, lanes] = low_hidden
        down = down + nt_dot(low_hidden, w_down[:, lanes])
        d_hidden = nn_dot(out_grad, w_down[:, lanes])
        d_proj[:, lanes] = (d_hidden * gate * slope).astype(jnp.bfloat16)
        d_proj[:, FF + HALF * j : FF + HALF * (j + 1)] = (d_hidden * active).astype(jnp.bfloat16)
    block_out[...] = jnp.where(live, after_attn + down, 0.0).astype(jnp.bfloat16)
    everyone = list(range(CHIPS))
    d_second = nn_dot(d_proj[...], w_up[...])
    gain_grad = jnp.sum(normed * d_second, axis=0, keepdims=True)
    d_after = grad + norm_back(d_second * gains, normed, factor)
    d_after_out[...] = d_after
    d_attn = d_after.astype(jnp.bfloat16)
    d_mixed[...] = nn_dot(d_attn, w_out[...]).astype(jnp.bfloat16)
    for j in range(2):
        up = tn_dot(d_proj[:, FF * j : FF * (j + 1)], a2)
        put_both(place, send, keep, 0, up, everyone[8 * j : 8 * j + 8])
    put_both(place, send, keep, 144, tn_dot(d_attn, mixed[...]), everyone)
    down_grad = tn_dot(out_grad, hidden[...])
    put_both(place, send, keep, 192, down_grad, everyone)
    rest = down_grad[:, 2 * HALF :]
    for chip in everyone:
        put_rows(place, send, keep, 0, 240, rest[48 * chip : 48 * chip + 32], [chip])
        put_rows(place, send, keep, 1, 240, rest[48 * chip + 32 : 48 * chip + 48], [chip])
        put_rows(place, send, keep, 1, 256, gain_rows(gain_grad, chip), [chip])


def attend_back_kernel(
    place, query, pairs, before, after, bias, d_mixed,
    d_query, d_own, rim_before, rim_after, framed, d_framed,
):
    frame_pairs(place, pairs, before, after, framed)
    is_low, low, high = head_masks()
    d_framed[256:SPAN, :] = jnp.zeros((SPAN - 256, 2 * D), jnp.float32)
    scale = 1.0 / math.sqrt(HD)
    for block in range(2):
        rows, keys = slice(128 * block, 128 * block + 128), slice(128 * block, 128 * block + 256)
        both = jnp.concatenate([bias[rows, :], bias[rows, :]], axis=0)
        for p in range(PAIRS):
            lanes, vlanes = slice(PAIR * p, PAIR * (p + 1)), slice(D + PAIR * p, D + PAIR * (p + 1))
            q2 = stack_heads(query[rows, lanes], low, high)
            o2 = stack_heads(d_mixed[rows, lanes], low, high)
            k2 = framed[keys, lanes]
            probs = probabilities(q2, k2, both)
            d_probs = nt_dot(o2, framed[keys, vlanes])
            spread = jnp.sum(probs * d_probs, axis=-1, keepdims=True)
            d_scores = (probs * (d_probs - spread)).astype(jnp.bfloat16)
            d_q = nn_dot(d_scores, k2) * scale
            d_query[rows, lanes] = jnp.where(is_low, d_q[:128], d_q[128:])
            d_k = tn_dot(d_scores, q2) * scale
            d_v = tn_dot(probs.astype(jnp.bfloat16), o2)
            if block == 0:
                d_framed[keys, lanes] = d_k
                d_framed[keys, vlanes] = d_v
            else:
                d_framed[keys, lanes] += d_k
                d_framed[keys, vlanes] += d_v
    rim_before[...] = d_framed[0:WIN, :].astype(jnp.bfloat16)
    tail = pl.ds(pl.multiple_of(WIN + place[AT_LIVE], 64), WIN)
    rim_after[...] = d_framed[tail, :].astype(jnp.bfloat16)
    d_own[...] = d_framed[WIN : WIN + SLOTS, :]


def finish_kernel(
    place, tokens, first, gain, weight, d_query, d_own, from_before, from_after, cos, sin_a, sin_b, d_after,
    tokens_grad, send, keep, d_joined, d_pairs,
):
    live = lax.broadcasted_iota(jnp.int32, (SLOTS, 1), 0) < place[AT_LIVE]
    d_pairs[...] = jnp.where(live, d_own[...], 0.0)
    d_pairs[0:WIN, :] += from_before[...].astype(jnp.float32)
    tail = pl.ds(pl.multiple_of(place[AT_LIVE] - WIN, 64), WIN)
    d_pairs[tail, :] += from_after[...].astype(jnp.float32)
    c, sa, sb = cos[...], sin_a[...], sin_b[...]
    for part in range(2):
        source = d_query if part == 0 else d_pairs
        for p in range(PAIRS):
            v = source[:, PAIR * p : PAIR * (p + 1)]
            v = v * c - pltpu.roll(v, 96, 1) * sa - pltpu.roll(v, 32, 1) * sb
            d_joined[:, part * D + PAIR * p : part * D + PAIR * (p + 1)] = v.astype(jnp.bfloat16)
    d_joined[:, 2 * D :] = d_pairs[:, D:].astype(jnp.bfloat16)
    d_first = nn_dot(d_joined[...], weight[...])
    normed, factor = norm_parts(tokens[...].astype(jnp.float32))
    gain_grad = jnp.sum(normed * d_first, axis=0, keepdims=True)
    d_stream = d_after[...] + norm_back(d_first * gain[...], normed, factor)
    tokens_grad[...] = jnp.where(live, d_stream, 0.0)
    everyone = list(range(CHIPS))
    for j in range(2):
        up = tn_dot(d_joined[:, 1152 * j : 1152 * (j + 1)], first[...])
        put_both(place, send, keep, 0, up, everyone[8 * j : 8 * j + 8])
    for chip in everyone:
        for stream in (0, 1):
            put_rows(place, send, keep, stream, 144, gain_rows(gain_grad, chip), [chip])


def swap_halves(shard, core, sibling):
    low, high = shard[:, :HALF], shard[:, HALF:]
    own = jnp.where(core == 0, low, high)
    return own, permute(jnp.where(core == 0, high, low), sibling)


def interleave(own, got, core, cuts):
    parts, start = [], 0
    for count in cuts:
        mine, theirs = own[start : start + count], got[start : start + count]
        parts += [jnp.where(core == 0, mine, theirs), jnp.where(core == 0, theirs, mine)]
        start += count
    return parts


def spread_line(block, line):
    return jnp.stack([block] + [permute(block, line[k]) for k in (1, 2, 3)])


def reduce_near(send, keep, links_of):
    return keep + permute(send, links_of[0])


def sum_shares(own, others):
    share = own.astype(jnp.float32)
    for other in others:
        share = share + other.astype(jnp.float32)
    return share


def place_table(live_rows):
    z, y, x, core = chip_place()
    slots = jnp.arange(CHIPS, dtype=jnp.int32)
    zr, nr, fr = slots % 4, slots // 4 % 2, slots // 8
    held = []
    for own in (True, False):
        along_y = (core == 0) if own else (core == 1)
        yr, xr = jnp.where(along_y, nr, fr), jnp.where(along_y, fr, nr)
        held.append((z - zr) % 4 * 4 + (y ^ yr) * 2 + (x ^ xr))
    zz, yy, xx = slots // 4, slots // 2 % 2, slots % 2
    yr, xr = y ^ yy, x ^ xx
    put = []
    for n, f in ((yr, xr), (xr, yr)):
        put.append((1 - n) * 8 + (1 - f) * 4 + (zz - z + 3) % 4)
    head = jnp.stack([live_rows, core]).astype(jnp.int32)
    return jnp.concatenate([head] + held + put).astype(jnp.int32)


def fused_body(
    tokens, w_qkv, w_out, w_up, w_down, gain_attn, gain_mlp, cotangent, block_counts, seq_lengths
):
    bf16, f32 = jnp.bfloat16, jnp.float32
    device_index = lax.axis_index("fsdp")
    core = device_index % 2
    wires = links()
    sibling, near, far, line = wires
    gains = jnp.zeros((8, D), bf16)
    gain_pair = jnp.pad(jnp.stack([gain_attn, gain_mlp]), ((0, 6), (0, HALF - 24)))
    gains = jnp.concatenate([gain_pair, gain_pair], axis=1)
    own, got = swap_halves(jnp.concatenate([w_qkv.T, gains]), core, sibling)
    block = jnp.concatenate(interleave(own, got, core, (72, 8)))
    lined_one = spread_line(block, line)
    near_one, far_one = permute(lined_one, near), permute(lined_one, far)
    both_one = permute(near_one, far)
    mine_one = [lined_one, near_one, far_one, both_one]
    blocks_one = mine_one + [permute(piece, sibling) for piece in mine_one]
    block_counts, seq_lengths, _ = lax.optimization_barrier((block_counts, seq_lengths, lined_one))
    block_count = lax.dynamic_index_in_dim(block_counts, device_index, keepdims=False)
    device_ids = jnp.arange(block_counts.shape[0], dtype=jnp.int32)
    first_place = jnp.sum(jnp.where(device_ids < device_index, block_counts, 0)) * BLK
    live_rows = block_count * BLK
    stream_total = jnp.sum(block_counts) * BLK
    place = place_table(live_rows)
    slot_index = jnp.arange(SLOTS, dtype=jnp.int32)
    live_slots = slot_index < live_rows
    query_place = first_place + slot_index
    query_seg, query_pos = sequence_places(query_place, seq_lengths)
    key_slot = (slot_index // BLK * BLK)[:, None] + jnp.arange(256, dtype=jnp.int32)[None, :] - WIN
    key_place = first_place + key_slot
    ends = jnp.cumsum(seq_lengths)
    key_seg = jnp.sum((key_place[:, :, None] >= ends).astype(jnp.int32), axis=2)
    allowed = (
        live_slots[:, None]
        & (key_place >= 0)
        & (key_place < stream_total)
        & (query_seg[:, None] == key_seg)
        & (jnp.abs(query_place[:, None] - key_place) <= WIN)
    ) | (jnp.logical_not(live_slots)[:, None] & (key_slot == slot_index[:, None]))
    bias = jnp.where(allowed, 0.0, MASKED).astype(f32)
    cosine, sine = rotary_tables(query_pos)
    cosine, sine = (jnp.concatenate([t[:, 0], t[:, 0]], axis=1) for t in (cosine, sine))
    front = (jnp.arange(PAIR) % HD < HD // 2)[None, :]
    sin_a, sin_b = jnp.where(front, -sine, 0.0), jnp.where(front, 0.0, sine)
    chosen = (place[AT_CHIP : AT_CHIP + 16][None, :] == jnp.arange(CHIPS)[:, None]).astype(f32)
    flat = jnp.concatenate([piece[:, 144:, :24] for piece in mine_one]).astype(f32)
    flat = jnp.concatenate([flat[:, row] for row in (0, 8, 1, 9)], axis=1)
    flat = jnp.sum(chosen[:, :, None] * flat[None], axis=1)
    gain_a, gain_m = flat[:, :48].reshape(1, D), flat[:, 48:].reshape(1, D)
    query, pairs, first, weight = call(
        project_kernel,
        [((SLOTS, D), bf16), ((SLOTS, 2 * D), bf16), ((SLOTS, D), bf16), ((3 * D, D), bf16)],
        [],
        [place, tokens, gain_a, cosine, sin_a, sin_b] + blocks_one,
        6,
        8,
    )
    shard = jnp.concatenate([w_up.T, w_out.T, w_down.T[:, :D]])
    rest = w_down.T[:, D:]
    low, high = shard[:, :HALF], shard[:, HALF:]
    own = jnp.concatenate([jnp.where(core == 0, low, high), rest[:8]])
    got = permute(jnp.concatenate([jnp.where(core == 0, high, low), rest[:8]]), sibling)
    tail = jnp.where(
        core == 0,
        jnp.concatenate([rest, got[120:128]]),
        jnp.concatenate([rest[8:], jnp.zeros((16, HALF), bf16)]),
    )
    block = jnp.concatenate(interleave(own, got, core, (72, 24, 24)) + [tail])
    block, _ = lax.optimization_barrier((block, lined_one))
    lined_two, _ = lax.optimization_barrier((spread_line(block, line), both_one))
    near_two, far_two = permute(lined_two, near), permute(lined_two, far)
    up = [(i, i + 1) for i in range(31)]
    down = [(i + 1, i) for i in range(31)]
    before = permute(lax.dynamic_slice_in_dim(pairs, live_rows - WIN, WIN, 0), up)
    after = permute(pairs[:WIN], down)
    near_two, pairs = lax.optimization_barrier((near_two, pairs))
    both_two = permute(near_two, far)
    (mixed,) = call(
        attend_kernel,
        [((SLOTS, D), bf16)],
        [((SPAN, 2 * D), bf16)],
        [place, query, pairs, before, after, bias],
        3,
    )
    mine_two = [lined_two, near_two, far_two]
    other_two = [permute(piece, sibling) for piece in mine_two]
    both_two, mixed = lax.optimization_barrier((both_two, mixed))
    blocks_two = mine_two + [both_two] + other_two + [permute(both_two, sibling)]
    block_out, d_after, d_mixed, send, keep = call(
        middle_kernel,
        [((SLOTS, D), bf16), ((SLOTS, D), f32), ((SLOTS, D), bf16), ((CHIPS, ROWS2, HALF), bf16), ((CHIPS, ROWS2, HALF), bf16)],
        [((2 * FF, D), bf16), ((D, D), bf16), ((D, FF), bf16), ((SLOTS, 2 * FF), bf16), ((SLOTS, FF), bf16)],
        [place, tokens, mixed, gain_m, cotangent] + blocks_two,
        14,
        8,
    )
    d_query, d_own, rim_before, rim_after = call(
        attend_back_kernel,
        [((SLOTS, D), f32), ((SLOTS, 2 * D), f32), ((WIN, 2 * D), bf16), ((WIN, 2 * D), bf16)],
        [((SPAN, 2 * D), bf16), ((SPAN, 2 * D), f32)],
        [place, query, pairs, before, after, bias, d_mixed],
        8,
    )
    from_after = permute(rim_before, down)
    from_before = permute(rim_after, up)
    total = reduce_near(send, keep, wires)
    leaving, staying = total[:8], total[8:]
    leaving, from_after, from_before = lax.optimization_barrier((leaving, from_after, from_before))
    arrived = permute(leaving, near)
    tokens_grad, send_qkv, keep_qkv = call(
        finish_kernel,
        [((SLOTS, D), f32), ((CHIPS, ROWS1, HALF), bf16), ((CHIPS, ROWS1, HALF), bf16)],
        [((SLOTS, 3 * D), bf16), ((SLOTS, 2 * D), f32)],
        [place, tokens, first, gain_a, weight, d_query, d_own, from_before, from_after, cosine, sin_a, sin_b, d_after],
        9,
    )
    total = staying + arrived
    total, send_qkv, keep_qkv = lax.optimization_barrier((total, send_qkv, keep_qkv))
    leaving, staying = total[:4], total[4:]
    arrived = permute(leaving, far)
    total_qkv = reduce_near(send_qkv, keep_qkv, wires)
    leave_qkv, stay_qkv = total_qkv[:8], total_qkv[8:]
    arrived_qkv = permute(leave_qkv, near)
    staying, stay_qkv = lax.optimization_barrier((staying, stay_qkv))
    total = staying + arrived
    last = [permute(total[k], line[k + 1]) for k in range(3)]
    stay_qkv, last[0] = lax.optimization_barrier((stay_qkv, last[0]))
    total_qkv = stay_qkv + arrived_qkv
    arrived_qkv = permute(total_qkv[:4], far)
    total_qkv = total_qkv[4:] + arrived_qkv
    share, total_qkv = lax.optimization_barrier((total[3], total_qkv))
    share = sum_shares(share, last)
    last_qkv = [permute(total_qkv[k], line[k + 1]) for k in range(3)]
    chip = device_index // 2
    lane = 48 * chip - jnp.minimum(48 * chip // 128 * 128, D - HALF) + 24 * core

    def part(block, start, count, whose):
        return lax.dynamic_slice_in_dim(block, start + count * whose, count, 0)

    gain_row = lax.dynamic_slice_in_dim(share[256:264], lane - 24 * core, 48, 1)
    gain_row = jnp.pad(gain_row, ((0, 0), (0, HALF - 48)))
    cuts = ((0, 72), (144, 24), (192, 24))
    theirs = jnp.concatenate(
        [part(share, s, n, 1 - core) for s, n in cuts] + [jnp.where(core == 0, share[264:272], gain_row)]
    )
    own = jnp.concatenate([part(share, s, n, core) for s, n in cuts])
    got = permute(theirs, sibling)
    both = jnp.concatenate(
        [jnp.where(core == 0, own, got[:120]), jnp.where(core == 0, got[:120], own)], axis=1
    )
    last = jnp.where(
        core == 0, share[240:264], jnp.concatenate([got[120:128], share[240:256]])
    )
    up_sum, out_sum = both[:72].T, both[72:96].T
    down_sum = jnp.concatenate([both[96:], last], axis=1).T
    gain_m_sum = jnp.where(core == 0, got[120, :24], gain_row[0, 24:48])
    share = sum_shares(total_qkv[3], last_qkv)
    got = permute(part(share, 0, 72, 1 - core), sibling)
    own = part(share, 0, 72, core)
    qkv_sum = jnp.concatenate([jnp.where(core == 0, own, got), jnp.where(core == 0, got, own)], axis=1).T
    gain_a_sum = lax.dynamic_slice(share, (144, lane), (1, 24))[0]
    return (block_out, tokens_grad, qkv_sum, out_sum, up_sum, down_sum, gain_a_sum, gain_m_sum)


def solution(mesh):
    plan = fused_body if mesh.shape["fsdp"] == 32 else body
    placed = (
        P("fsdp", None),
        P(None, "fsdp"),
        P(None, "fsdp"),
        P(None, "fsdp"),
        P(None, "fsdp"),
        P("fsdp"),
        P("fsdp"),
        P("fsdp", None),
        P(),
        P(),
    )
    return jax.shard_map(
        plan,
        mesh=mesh,
        in_specs=placed,
        out_specs=(
            P("fsdp", None),
            P("fsdp", None),
            P(None, "fsdp"),
            P(None, "fsdp"),
            P(None, "fsdp"),
            P(None, "fsdp"),
            P("fsdp"),
            P("fsdp"),
        ),
        check_vma=False,
    )
```

```python
import functools
import math

import jax
import jax.numpy as jnp
from jax import lax
from jax.experimental import pallas as pl
from jax.experimental.pallas import tpu as pltpu
from jax.sharding import PartitionSpec as P

D = 768
HEADS = 12
HD = 64
FF = 1152
BLK = 128
WIN = 64


EPSILON = 1e-05
MASKED = -1e30


def with_halo(shard, sides, width):
    for axis, dim in sides:
        peers, length = (lax.axis_size(axis), shard.shape[dim])
        up = [(i, (i + 1) % peers) for i in range(peers - 1)]
        down = [(j, i) for i, j in up]
        last = lax.slice_in_dim(shard, length - width, length, axis=dim)
        initial = lax.slice_in_dim(shard, 0, width, axis=dim)
        before = lax.ppermute(last, axis, up)
        after = lax.ppermute(initial, axis, down)
        shard = jnp.concatenate([before, shard, after], axis=dim)
    return shard


def norm_parts(values):
    center = values - jnp.mean(values, axis=-1, keepdims=True)
    factor = lax.rsqrt(jnp.mean(center * center, axis=-1, keepdims=True) + EPSILON)
    return (center * factor, factor)


def norm_back(grad_normed, normed, factor):
    return factor * (
        grad_normed
        - jnp.mean(grad_normed, axis=-1, keepdims=True)
        - normed * jnp.mean(grad_normed * normed, axis=-1, keepdims=True)
    )


def sequence_places(places, lengths):
    ends = jnp.cumsum(lengths)
    starts = ends - lengths
    segment = jnp.sum((places[:, None] >= ends[None, :]).astype(jnp.int32), axis=1)
    picked = segment[:, None] == jnp.arange(lengths.shape[0], dtype=jnp.int32)[None, :]
    start = jnp.sum(jnp.where(picked, starts[None, :], 0), axis=1)
    return (segment, places - start)


def rotary_tables(position):
    half = HD // 2
    freq = jnp.power(10000.0, -(jnp.arange(half, dtype=jnp.float32) * (2.0 / HD)))
    angle = position.astype(jnp.float32)[:, None] * freq[None, :]
    angle = jnp.concatenate([angle, angle], axis=1)[:, None, :]
    return (jnp.cos(angle), jnp.sin(angle))


def rotate_heads(values, cosine, sine):
    half = HD // 2
    turned = jnp.concatenate([-values[..., half:], values[..., :half]], axis=-1)
    return values * cosine + turned * sine


def rotate_back(grads, cosine, sine):
    half = HD // 2
    spun = grads * sine
    return grads * cosine + jnp.concatenate([spun[..., half:], -spun[..., :half]], axis=-1)


def rows_product(left, right):
    return lax.dot_general(
        left, right, (((0,), (0,)), ((), ())), preferred_element_type=jnp.float32
    )


def cols_product(left, right):
    return lax.dot_general(
        left, right, (((1,), (1,)), ((), ())), preferred_element_type=jnp.float32
    )


def exact_gelu(values):
    return jax.nn.gelu(values, approximate=False)


def masked_scores(query, key_heads, allowed, score_scale):
    raw_scores = (
        jnp.einsum("qhd,khd->hqk", query, key_heads, preferred_element_type=jnp.float32)
        * score_scale
    )
    return jnp.where(allowed[None], raw_scores, MASKED)


def column_term(grad_side, data_side):
    return rows_product(grad_side, data_side)


def permute(values, pairs):
    return lax.ppermute(values, "fsdp", pairs)


def links():
    sibling = [(i, i ^ 1) for i in range(32)]
    near = [(i, i ^ (2 if i & 1 else 4)) for i in range(32)]
    far = [(i, i ^ (4 if i & 1 else 2)) for i in range(32)]
    line = [[(i, (i + 8 * k) % 32) for i in range(32)] for k in range(4)]
    return (sibling, near, far, line)


def chip_place():
    me = lax.axis_index("fsdp")
    return (me // 8, (me // 4) % 2, (me // 2) % 2, me % 2)


def gather_rows(rows):
    return lax.all_gather(rows, "fsdp", axis=0, tiled=False)


def scatter_rows(terms):
    return lax.psum_scatter(terms, "fsdp", scatter_dimension=0, tiled=False).astype(jnp.float32)


def fold_pad(shard):
    count = shard.shape[-2]
    rest = shard[..., D:]
    half = (count + 1) // 2
    left, right = rest[..., :half, :], rest[..., half:, :]
    spare = [(0, 0)] * (shard.ndim - 2) + [(0, 2 * half - count), (0, 0)]
    rest = jnp.concatenate([left, jnp.pad(right, spare)], axis=-1)
    return jnp.concatenate([shard[..., :D], rest], axis=-2)


def unfold_pad(packed, count):
    half, lanes = (count + 1) // 2, FF - D
    rest = packed[..., count : count + half, :]
    rest = jnp.concatenate([rest[..., :lanes], rest[..., lanes:]], axis=-2)[..., :count, :]
    return jnp.concatenate([packed[..., :count, :], rest], axis=-1)


def body(
    tokens, w_qkv, w_out, w_up, w_down, gain_attn, gain_mlp, cotangent, block_counts, seq_lengths
):
    slot_total = tokens.shape[0]
    score_scale = 1.0 / math.sqrt(HD)
    device_index = lax.axis_index("fsdp")
    block_count = lax.dynamic_index_in_dim(block_counts, device_index, keepdims=False)
    device_ids = jnp.arange(block_counts.shape[0], dtype=jnp.int32)
    first_place = jnp.sum(jnp.where(device_ids < device_index, block_counts, 0)) * BLK
    live_rows = block_count * BLK
    stream_total = jnp.sum(block_counts) * BLK
    slot_index = jnp.arange(slot_total, dtype=jnp.int32)
    live_slots = slot_index < live_rows
    rim_offsets = jnp.arange(WIN, dtype=jnp.int32)
    query_place = first_place + slot_index
    before_place = first_place - WIN + rim_offsets
    after_place = first_place + live_rows + rim_offsets
    key_place = jnp.concatenate([before_place, query_place, after_place])
    key_live = jnp.concatenate([before_place >= 0, live_slots, after_place < stream_total])
    key_slot = jnp.concatenate([rim_offsets * 0 - 1, slot_index, rim_offsets * 0 - 1])
    query_seg, query_pos = sequence_places(query_place, seq_lengths)
    key_seg, unused = sequence_places(key_place, seq_lengths)
    in_window = jnp.abs(query_place[:, None] - key_place[None, :]) <= WIN
    allowed = live_slots[:, None] & key_live[None, :] & (
        query_seg[:, None] == key_seg[None, :]
    ) & in_window | jnp.logical_not(live_slots)[:, None] & (
        key_slot[None, :] == slot_index[:, None]
    )
    cosine, sine = rotary_tables(query_pos)
    peers = lax.axis_size("fsdp")
    columns = D // peers
    gains = jnp.zeros((8, D), jnp.bfloat16)
    gains = gains.at[0, :columns].set(gain_attn).at[1, :columns].set(gain_mlp)
    first_rows = gather_rows(jnp.concatenate([w_qkv.T, gains]))
    qkv_full = first_rows[:, : 3 * columns].reshape(3 * D, D)
    gain_a_full = first_rows[:, 3 * columns, :columns].reshape(D)
    gain_m_full = first_rows[:, 3 * columns + 1, :columns].reshape(D)
    up_columns = w_up.shape[1]
    later = jnp.concatenate([w_up.T, w_out.T, fold_pad(w_down.T)])
    later_rows = gather_rows(later)
    up_full = later_rows[:, :up_columns].reshape(2 * FF, D)
    out_full = later_rows[:, up_columns : up_columns + columns].reshape(D, D)
    down_full = unfold_pad(later_rows[:, up_columns + columns :], columns).reshape(D, FF)
    stream = tokens.astype(jnp.float32)
    normed_one, factor_one = norm_parts(stream)
    first_in = (normed_one * gain_a_full.astype(jnp.float32)).astype(jnp.bfloat16)
    joined = cols_product(first_in, qkv_full)
    query = rotate_heads(joined[:, :D].reshape(slot_total, HEADS, HD), cosine, sine).astype(
        jnp.bfloat16
    )
    keys_own = rotate_heads(
        joined[:, D : 2 * D].reshape(slot_total, HEADS, HD), cosine, sine
    ).astype(jnp.bfloat16)
    values_own = joined[:, 2 * D :].astype(jnp.bfloat16)
    pairs = jnp.concatenate([keys_own.reshape(slot_total, D), values_own], axis=1)
    edges = jnp.concatenate(
        [pairs[:WIN], lax.dynamic_slice_in_dim(pairs, live_rows - WIN, WIN, 0)], axis=0
    )
    framed = with_halo(edges, (("fsdp", 0),), WIN)
    all_pairs = jnp.concatenate([framed[:WIN], pairs, framed[3 * WIN :]], axis=0)
    key_heads = all_pairs[:, :D].reshape(-1, HEADS, HD)
    value_heads = all_pairs[:, D:].reshape(-1, HEADS, HD)
    scores = masked_scores(query, key_heads, allowed, score_scale)
    row_top = jnp.max(scores, axis=-1, keepdims=True)
    log_total = row_top + jnp.log(jnp.sum(jnp.exp(scores - row_top), axis=-1, keepdims=True))
    probs_low = jnp.exp(scores - log_total).astype(jnp.bfloat16)
    mixed = (
        jnp.einsum("hqk,khd->qhd", probs_low, value_heads, preferred_element_type=jnp.float32)
        .reshape(slot_total, D)
        .astype(jnp.bfloat16)
    )
    after_attn = stream + cols_product(mixed, out_full)
    normed_two, factor_two = norm_parts(after_attn)
    second_in = (normed_two * gain_m_full.astype(jnp.float32)).astype(jnp.bfloat16)
    projected = cols_product(second_in, up_full)
    gate_half = projected[:, FF:]
    activated, gelu_pull = jax.vjp(exact_gelu, projected[:, :FF])
    hidden = (activated * gate_half).astype(jnp.bfloat16)
    down_out = cols_product(hidden, down_full)
    block_out = jnp.where(live_slots[:, None], after_attn + down_out, 0.0).astype(jnp.bfloat16)
    out_grad = jnp.where(live_slots[:, None], cotangent, jnp.zeros_like(cotangent))
    d_hidden = jnp.dot(out_grad, down_full, preferred_element_type=jnp.float32)
    d_inputs = gelu_pull(d_hidden * gate_half)[0]
    d_projected = jnp.concatenate([d_inputs, d_hidden * activated], axis=1).astype(jnp.bfloat16)
    d_second = jnp.dot(d_projected, up_full, preferred_element_type=jnp.float32)
    grad_gain_m = jnp.sum(normed_two * d_second, axis=0)
    d_after = out_grad.astype(jnp.float32) + norm_back(
        d_second * gain_m_full.astype(jnp.float32), normed_two, factor_two
    )
    d_attn = d_after.astype(jnp.bfloat16)
    d_mixed = jnp.dot(d_attn, out_full, preferred_element_type=jnp.float32).astype(jnp.bfloat16).reshape(slot_total, HEADS, HD)
    scores = masked_scores(query, key_heads, allowed, score_scale)
    probs = jnp.exp(scores - log_total)
    d_probs = jnp.einsum("qhd,khd->hqk", d_mixed, value_heads, preferred_element_type=jnp.float32)
    d_scores = (probs * (d_probs - jnp.sum(probs * d_probs, axis=-1, keepdims=True))).astype(
        jnp.bfloat16
    )
    d_query = (
        jnp.einsum("hqk,khd->qhd", d_scores, key_heads, preferred_element_type=jnp.float32)
        * score_scale
    )
    d_keys = (
        jnp.einsum("hqk,qhd->khd", d_scores, query, preferred_element_type=jnp.float32)
        * score_scale
    )
    d_values = jnp.einsum(
        "hqk,qhd->khd", probs.astype(jnp.bfloat16), d_mixed, preferred_element_type=jnp.float32
    )
    d_pairs = jnp.concatenate([d_keys.reshape(-1, D), d_values.reshape(-1, D)], axis=1)
    grad_edges = jnp.concatenate([d_pairs[:WIN], d_pairs[WIN + slot_total :]], axis=0)
    returned = with_halo(grad_edges.astype(jnp.bfloat16), (("fsdp", 0),), WIN).astype(
        grad_edges.dtype
    )
    own_pairs = d_pairs[WIN : WIN + slot_total]
    own_pairs = own_pairs.at[:WIN].add(returned[:WIN])
    tail_rows = lax.dynamic_slice_in_dim(own_pairs, live_rows - WIN, WIN, 0) + returned[3 * WIN :]
    own_pairs = lax.dynamic_update_slice_in_dim(own_pairs, tail_rows, live_rows - WIN, 0)
    d_query_raw = rotate_back(d_query, cosine, sine).reshape(slot_total, D)
    d_keys_raw = rotate_back(own_pairs[:, :D].reshape(slot_total, HEADS, HD), cosine, sine).reshape(
        slot_total, D
    )
    d_joined = jnp.concatenate([d_query_raw, d_keys_raw, own_pairs[:, D:]], axis=1).astype(
        jnp.bfloat16
    )
    d_first = jnp.dot(d_joined, qkv_full, preferred_element_type=jnp.float32)
    grad_gain_a = jnp.sum(normed_one * d_first, axis=0)
    d_stream = d_after + norm_back(
        d_first * gain_a_full.astype(jnp.float32), normed_one, factor_one
    )
    tokens_grad = jnp.where(live_slots[:, None], d_stream, 0.0)
    down_terms = column_term(out_grad, hidden).astype(jnp.bfloat16).reshape(peers, columns, FF)
    up_terms = column_term(d_projected, second_in).astype(jnp.bfloat16)
    mlp_sum = scatter_rows(
        jnp.concatenate([up_terms.reshape(peers, up_columns, D), fold_pad(down_terms)], axis=1)
    )
    up_sum = mlp_sum[:up_columns].T
    down_sum = unfold_pad(mlp_sum[up_columns:], columns).T
    qkv_terms = column_term(d_joined, first_in).astype(jnp.bfloat16).reshape(peers, 3 * columns, D)
    out_terms = column_term(d_attn, mixed).astype(jnp.bfloat16).reshape(peers, columns, D)
    gain_terms = jnp.stack([grad_gain_a.reshape(peers, columns), grad_gain_m.reshape(peers, columns)], axis=1)
    gain_terms = jnp.pad(gain_terms.astype(jnp.bfloat16), ((0, 0), (0, 6), (0, D - columns)))
    attn_sum = scatter_rows(jnp.concatenate([qkv_terms, out_terms, gain_terms], axis=1))
    qkv_sum = attn_sum[: 3 * columns].T
    out_sum = attn_sum[3 * columns : 4 * columns].T
    gain_a_sum = attn_sum[4 * columns, :columns]
    gain_m_sum = attn_sum[4 * columns + 1, :columns]
    return (block_out, tokens_grad, qkv_sum, out_sum, up_sum, down_sum, gain_a_sum, gain_m_sum)


CHIPS = 16
HALF = 384
ROWS1 = 160
ROWS2 = 272
SLOTS = 256
SPAN = SLOTS + 2 * WIN
PAIR = 2 * HD
PAIRS = HEADS // 2
LIMIT = 48 * 1024 * 1024
AT_LIVE, AT_CORE, AT_CHIP, AT_PUT = 0, 1, 2, 34
VMEM = pltpu.MemorySpace.VMEM
SMEM = pltpu.MemorySpace.SMEM


def nt_dot(left, right):
    return lax.dot_general(left, right, (((1,), (1,)), ((), ())), preferred_element_type=jnp.float32)


def nn_dot(left, right):
    return jnp.dot(left, right, preferred_element_type=jnp.float32)


def tn_dot(left, right):
    return lax.dot_general(left, right, (((0,), (0,)), ((), ())), preferred_element_type=jnp.float32)


def call(kernel, outs, scratch, args, micros, blocks=0, away=0):
    whole = len(args) - blocks - 1
    spaces = [pl.BlockSpec(memory_space=SMEM)] + [pl.BlockSpec(memory_space=VMEM)] * whole
    spaces += [pl.BlockSpec(memory_space=pl.ANY)] * blocks
    semaphores = [pltpu.SemaphoreType.DMA((2 * CHIPS, 4))] if blocks else []
    semaphores += [pltpu.SemaphoreType.DMA((8,))] if away else []
    near_outs = len(outs) - away
    return pl.pallas_call(
        kernel,
        out_shape=[jax.ShapeDtypeStruct(shape, kind) for shape, kind in outs],
        in_specs=spaces,
        out_specs=[pl.BlockSpec(memory_space=VMEM)] * near_outs + [pl.BlockSpec(memory_space=pl.ANY)] * away,
        scratch_shapes=[pltpu.VMEM(shape, kind) for shape, kind in scratch] + semaphores,
        compiler_params=pltpu.CompilerParams(vmem_limit_bytes=LIMIT),
        cost_estimate=pl.CostEstimate(flops=0, bytes_accessed=3_690_000 * micros, transcendentals=0),
    )(*args)


def block_copies(place, refs, weight, done, kind, start, count):
    copies = []
    for slot in range(2 * CHIPS):
        chip = place[AT_CHIP + slot]
        core = place[AT_CORE] if slot < CHIPS else 1 - place[AT_CORE]
        rows = pl.ds(pl.multiple_of(chip * count, 16), count)
        lanes = pl.ds(pl.multiple_of(core * HALF, 128), HALF)
        source = refs[slot // 4].at[slot % 4, start : start + count, :]
        copies.append(pltpu.make_async_copy(source, weight.at[rows, lanes], done.at[slot, kind]))
    return copies


def rest_copies(place, refs, weight, done, core):
    copies = []
    for slot in range(2 * CHIPS):
        stream = core if slot < CHIPS else 1 - core
        count = 32 if stream == 0 else 16
        first = pl.multiple_of(place[AT_CHIP + slot] * 48 + (0 if stream == 0 else 32), 16)
        source = refs[slot // 4].at[slot % 4, 240 : 240 + count, :]
        copies.append(
            pltpu.make_async_copy(source, weight.at[pl.ds(first, count), 2 * HALF :], done.at[slot, 3])
        )
    return copies


def go(copies):
    for copy in copies:
        copy.start()


def land(copies):
    for copy in copies:
        copy.wait()


def put_rows(place, send, keep, stream, start, value, chips):
    count = value.shape[0] // len(chips)
    value = value.astype(jnp.bfloat16)

    def store(ref):
        for i, chip in enumerate(chips):
            slot = place[AT_PUT + 16 * stream + chip]
            ref[slot, start : start + count, :] = value[i * count : (i + 1) * count]

    pl.when(place[AT_CORE] == stream)(lambda: store(keep))
    pl.when(place[AT_CORE] != stream)(lambda: store(send))


def put_both(place, send, keep, start, value, chips):
    for stream in (0, 1):
        put_rows(place, send, keep, stream, start, value[:, HALF * stream : HALF * (stream + 1)], chips)


def gain_rows(vector, chip):
    start = min(48 * chip // 128 * 128, D - HALF)
    return jnp.broadcast_to(vector[:, start : start + HALF], (16, HALF))


def project_kernel(place, tokens, gain, cos, sin_a, sin_b, *rest):
    refs, (query, pairs, first, weight, done) = rest[:8], rest[8:]
    copies = block_copies(place, refs, weight, done, 0, 0, 144)
    go(copies)
    normed, _ = norm_parts(tokens[...].astype(jnp.float32))
    a1 = (normed * gain[...]).astype(jnp.bfloat16)
    first[...] = a1
    c, sa, sb = cos[...], sin_a[...], sin_b[...]
    land(copies)
    for part in range(3):
        for j in range(2):
            base = part * D + HALF * j
            joined = nt_dot(a1, weight[base : base + HALF, :])
            for p in range(3):
                lanes = slice(HALF * j + PAIR * p, HALF * j + PAIR * (p + 1))
                v = joined[:, PAIR * p : PAIR * (p + 1)]
                if part < 2:
                    v = v * c + pltpu.roll(v, 96, 1) * sa + pltpu.roll(v, 32, 1) * sb
                if part == 0:
                    query[:, lanes] = v.astype(jnp.bfloat16)
                else:
                    where = slice((part - 1) * D + lanes.start, (part - 1) * D + lanes.stop)
                    pairs[:, where] = v.astype(jnp.bfloat16)


def frame_pairs(place, pairs, before, after, framed):
    framed[0:WIN, :] = before[...]
    framed[WIN : WIN + SLOTS, :] = pairs[...]
    framed[WIN + SLOTS : SPAN, :] = jnp.zeros((WIN, 2 * D), jnp.bfloat16)
    framed[pl.ds(pl.multiple_of(WIN + place[AT_LIVE], 64), WIN), :] = after[...]


def stack_heads(values, low, high):
    return jnp.concatenate([values * low, values * high], axis=0)


def head_masks():
    lane = lax.broadcasted_iota(jnp.int32, (1, PAIR), 1)
    low = jnp.where(lane < HD, 1.0, 0.0).astype(jnp.bfloat16)
    return (lane < HD, low, 1.0 - low)


def probabilities(query, keys, bias):
    scores = nt_dot(query, keys) * (1.0 / math.sqrt(HD)) + bias
    expos = jnp.exp(scores - jnp.max(scores, axis=-1, keepdims=True))
    return expos * (1.0 / jnp.sum(expos, axis=-1, keepdims=True))


def attend_kernel(place, query, pairs, before, after, bias, mixed, framed):
    frame_pairs(place, pairs, before, after, framed)
    is_low, low, high = head_masks()
    for block in range(2):
        rows, keys = slice(128 * block, 128 * block + 128), slice(128 * block, 128 * block + 256)
        both = jnp.concatenate([bias[rows, :], bias[rows, :]], axis=0)
        for p in range(PAIRS):
            lanes, vlanes = slice(PAIR * p, PAIR * (p + 1)), slice(D + PAIR * p, D + PAIR * (p + 1))
            probs = probabilities(stack_heads(query[rows, lanes], low, high), framed[keys, lanes], both)
            out = nn_dot(probs.astype(jnp.bfloat16), framed[keys, vlanes])
            mixed[rows, lanes] = jnp.where(is_low, out[:128], out[128:]).astype(jnp.bfloat16)


def middle_kernel(place, tokens, mixed, gain, cotangent, *rest):
    refs = rest[:8]
    (block_out, d_after_out, d_mixed, send_out, keep_out, w_up, w_out, w_down, d_proj, hidden, send, keep, done, sent) = rest[8:]

    def leave(start, count, kind):
        rows = (slice(None), slice(start, start + count), slice(None))
        pairs = ((send, send_out), (keep, keep_out))
        return [pltpu.make_async_copy(a.at[rows], b.at[rows], sent.at[kind + i]) for i, (a, b) in enumerate(pairs)]

    out_copies = block_copies(place, refs, w_out, done, 0, 144, 48)
    up_copies = block_copies(place, refs, w_up, done, 1, 0, 144)
    down_copies = block_copies(place, refs, w_down, done, 2, 192, 48)
    go(out_copies)
    go(up_copies)
    go(down_copies)
    for core in (0, 1):
        pl.when(place[AT_CORE] == core)(lambda: go(rest_copies(place, refs, w_down, done, core)))
    land(out_copies)
    after_attn = tokens[...].astype(jnp.float32) + nt_dot(mixed[...], w_out[...])
    normed, factor = norm_parts(after_attn)
    gains = gain[...]
    a2 = (normed * gains).astype(jnp.bfloat16)
    live = lax.broadcasted_iota(jnp.int32, (SLOTS, 1), 0) < place[AT_LIVE]
    grad = jnp.where(live, cotangent[...].astype(jnp.float32), 0.0)
    out_grad = grad.astype(jnp.bfloat16)
    down = jnp.zeros((SLOTS, D), jnp.float32)
    land(up_copies)
    land(down_copies)
    for core in (0, 1):
        pl.when(place[AT_CORE] == core)(lambda: land(rest_copies(place, refs, w_down, done, core)))
    for j in range(3):
        lanes = slice(HALF * j, HALF * (j + 1))
        inputs = nt_dot(a2, w_up[lanes, :])
        gate = nt_dot(a2, w_up[FF + HALF * j : FF + HALF * (j + 1), :])
        cdf = 0.5 * (1.0 + lax.erf(inputs * (1.0 / math.sqrt(2.0))))
        slope = cdf + inputs * (jnp.exp(-0.5 * inputs * inputs) * (1.0 / math.sqrt(2.0 * math.pi)))
        active = inputs * cdf
        low_hidden = (active * gate).astype(jnp.bfloat16)
        hidden[:, lanes] = low_hidden
        down = down + nt_dot(low_hidden, w_down[:, lanes])
        d_hidden = nn_dot(out_grad, w_down[:, lanes])
        d_proj[:, lanes] = (d_hidden * gate * slope).astype(jnp.bfloat16)
        d_proj[:, FF + HALF * j : FF + HALF * (j + 1)] = (d_hidden * active).astype(jnp.bfloat16)
    block_out[...] = jnp.where(live, after_attn + down, 0.0).astype(jnp.bfloat16)
    everyone = list(range(CHIPS))
    for j in range(2):
        up = tn_dot(d_proj[:, FF * j : FF * (j + 1)], a2)
        put_both(place, send, keep, 0, up, everyone[8 * j : 8 * j + 8])
    up_leave = leave(0, 144, 0)
    go(up_leave)
    down_grad = tn_dot(out_grad, hidden[...])
    put_both(place, send, keep, 192, down_grad, everyone)
    rest = down_grad[:, 2 * HALF :]
    for chip in everyone:
        put_rows(place, send, keep, 0, 240, rest[48 * chip : 48 * chip + 32], [chip])
        put_rows(place, send, keep, 1, 240, rest[48 * chip + 32 : 48 * chip + 48], [chip])
    down_leave = leave(192, 64, 2)
    go(down_leave)
    d_second = nn_dot(d_proj[...], w_up[...])
    gain_grad = jnp.sum(normed * d_second, axis=0, keepdims=True)
    d_after = grad + norm_back(d_second * gains, normed, factor)
    d_after_out[...] = d_after
    d_attn = d_after.astype(jnp.bfloat16)
    d_mixed[...] = nn_dot(d_attn, w_out[...]).astype(jnp.bfloat16)
    put_both(place, send, keep, 144, tn_dot(d_attn, mixed[...]), everyone)
    for chip in everyone:
        put_rows(place, send, keep, 1, 256, gain_rows(gain_grad, chip), [chip])
    out_leave, gain_leave = leave(144, 48, 4), leave(256, 16, 6)
    go(out_leave + gain_leave)
    land(up_leave + down_leave + out_leave + gain_leave)


def attend_back_kernel(
    place, query, pairs, before, after, bias, d_mixed,
    d_query, d_own, rim_before, rim_after, framed, d_framed,
):
    frame_pairs(place, pairs, before, after, framed)
    is_low, low, high = head_masks()
    d_framed[256:SPAN, :] = jnp.zeros((SPAN - 256, 2 * D), jnp.float32)
    scale = 1.0 / math.sqrt(HD)
    for block in range(2):
        rows, keys = slice(128 * block, 128 * block + 128), slice(128 * block, 128 * block + 256)
        both = jnp.concatenate([bias[rows, :], bias[rows, :]], axis=0)
        for p in range(PAIRS):
            lanes, vlanes = slice(PAIR * p, PAIR * (p + 1)), slice(D + PAIR * p, D + PAIR * (p + 1))
            q2 = stack_heads(query[rows, lanes], low, high)
            o2 = stack_heads(d_mixed[rows, lanes], low, high)
            k2 = framed[keys, lanes]
            probs = probabilities(q2, k2, both)
            d_probs = nt_dot(o2, framed[keys, vlanes])
            spread = jnp.sum(probs * d_probs, axis=-1, keepdims=True)
            d_scores = (probs * (d_probs - spread)).astype(jnp.bfloat16)
            d_q = nn_dot(d_scores, k2) * scale
            d_query[rows, lanes] = jnp.where(is_low, d_q[:128], d_q[128:])
            d_k = tn_dot(d_scores, q2) * scale
            d_v = tn_dot(probs.astype(jnp.bfloat16), o2)
            if block == 0:
                d_framed[keys, lanes] = d_k
                d_framed[keys, vlanes] = d_v
            else:
                d_framed[keys, lanes] += d_k
                d_framed[keys, vlanes] += d_v
    rim_before[...] = d_framed[0:WIN, :].astype(jnp.bfloat16)
    tail = pl.ds(pl.multiple_of(WIN + place[AT_LIVE], 64), WIN)
    rim_after[...] = d_framed[tail, :].astype(jnp.bfloat16)
    d_own[...] = d_framed[WIN : WIN + SLOTS, :]


def finish_kernel(
    place, tokens, first, gain, weight, d_query, d_own, from_before, from_after, cos, sin_a, sin_b, d_after,
    tokens_grad, send, keep, d_joined, d_pairs,
):
    live = lax.broadcasted_iota(jnp.int32, (SLOTS, 1), 0) < place[AT_LIVE]
    d_pairs[...] = jnp.where(live, d_own[...], 0.0)
    d_pairs[0:WIN, :] += from_before[...].astype(jnp.float32)
    tail = pl.ds(pl.multiple_of(place[AT_LIVE] - WIN, 64), WIN)
    d_pairs[tail, :] += from_after[...].astype(jnp.float32)
    c, sa, sb = cos[...], sin_a[...], sin_b[...]
    for part in range(2):
        source = d_query if part == 0 else d_pairs
        for p in range(PAIRS):
            v = source[:, PAIR * p : PAIR * (p + 1)]
            v = v * c - pltpu.roll(v, 96, 1) * sa - pltpu.roll(v, 32, 1) * sb
            d_joined[:, part * D + PAIR * p : part * D + PAIR * (p + 1)] = v.astype(jnp.bfloat16)
    d_joined[:, 2 * D :] = d_pairs[:, D:].astype(jnp.bfloat16)
    d_first = nn_dot(d_joined[...], weight[...])
    normed, factor = norm_parts(tokens[...].astype(jnp.float32))
    gain_grad = jnp.sum(normed * d_first, axis=0, keepdims=True)
    d_stream = d_after[...] + norm_back(d_first * gain[...], normed, factor)
    tokens_grad[...] = jnp.where(live, d_stream, 0.0)
    everyone = list(range(CHIPS))
    for j in range(2):
        up = tn_dot(d_joined[:, 1152 * j : 1152 * (j + 1)], first[...])
        put_both(place, send, keep, 0, up, everyone[8 * j : 8 * j + 8])
    for chip in everyone:
        for stream in (0, 1):
            put_rows(place, send, keep, stream, 144, gain_rows(gain_grad, chip), [chip])


def swap_halves(shard, core, sibling):
    low, high = shard[:, :HALF], shard[:, HALF:]
    own = jnp.where(core == 0, low, high)
    return own, permute(jnp.where(core == 0, high, low), sibling)


def interleave(own, got, core, cuts):
    parts, start = [], 0
    for count in cuts:
        mine, theirs = own[start : start + count], got[start : start + count]
        parts += [jnp.where(core == 0, mine, theirs), jnp.where(core == 0, theirs, mine)]
        start += count
    return parts


def spread_line(block, line):
    return jnp.stack([block] + [permute(block, line[k]) for k in (1, 2, 3)])


def reduce_near(send, keep, links_of):
    return keep + permute(send, links_of[0])


def sum_shares(own, others):
    share = own.astype(jnp.float32)
    for other in others:
        share = share + other.astype(jnp.float32)
    return share


def place_table(live_rows):
    z, y, x, core = chip_place()
    slots = jnp.arange(CHIPS, dtype=jnp.int32)
    zr, nr, fr = slots % 4, slots // 4 % 2, slots // 8
    held = []
    for own in (True, False):
        along_y = (core == 0) if own else (core == 1)
        yr, xr = jnp.where(along_y, nr, fr), jnp.where(along_y, fr, nr)
        held.append((z - zr) % 4 * 4 + (y ^ yr) * 2 + (x ^ xr))
    zz, yy, xx = slots // 4, slots // 2 % 2, slots % 2
    yr, xr = y ^ yy, x ^ xx
    put = []
    for n, f in ((yr, xr), (xr, yr)):
        put.append((1 - n) * 8 + (1 - f) * 4 + (zz - z + 3) % 4)
    head = jnp.stack([live_rows, core]).astype(jnp.int32)
    return jnp.concatenate([head] + held + put).astype(jnp.int32)


def fused_body(
    tokens, w_qkv, w_out, w_up, w_down, gain_attn, gain_mlp, cotangent, block_counts, seq_lengths
):
    bf16, f32 = jnp.bfloat16, jnp.float32
    device_index = lax.axis_index("fsdp")
    core = device_index % 2
    wires = links()
    sibling, near, far, line = wires
    gains = jnp.zeros((8, D), bf16)
    gain_pair = jnp.pad(jnp.stack([gain_attn, gain_mlp]), ((0, 6), (0, HALF - 24)))
    gains = jnp.concatenate([gain_pair, gain_pair], axis=1)
    own, got = swap_halves(jnp.concatenate([w_qkv.T, gains]), core, sibling)
    block = jnp.concatenate(interleave(own, got, core, (72, 8)))
    lined_one = spread_line(block, line)
    near_one, far_one = permute(lined_one, near), permute(lined_one, far)
    both_one = permute(near_one, far)
    mine_one = [lined_one, near_one, far_one, both_one]
    blocks_one = mine_one + [permute(piece, sibling) for piece in mine_one]
    block_counts, seq_lengths, _ = lax.optimization_barrier((block_counts, seq_lengths, lined_one))
    block_count = lax.dynamic_index_in_dim(block_counts, device_index, keepdims=False)
    device_ids = jnp.arange(block_counts.shape[0], dtype=jnp.int32)
    first_place = jnp.sum(jnp.where(device_ids < device_index, block_counts, 0)) * BLK
    live_rows = block_count * BLK
    stream_total = jnp.sum(block_counts) * BLK
    place = place_table(live_rows)
    slot_index = jnp.arange(SLOTS, dtype=jnp.int32)
    live_slots = slot_index < live_rows
    query_place = first_place + slot_index
    query_seg, query_pos = sequence_places(query_place, seq_lengths)
    key_slot = (slot_index // BLK * BLK)[:, None] + jnp.arange(256, dtype=jnp.int32)[None, :] - WIN
    key_place = first_place + key_slot
    ends = jnp.cumsum(seq_lengths)
    key_seg = jnp.sum((key_place[:, :, None] >= ends).astype(jnp.int32), axis=2)
    allowed = (
        live_slots[:, None]
        & (key_place >= 0)
        & (key_place < stream_total)
        & (query_seg[:, None] == key_seg)
        & (jnp.abs(query_place[:, None] - key_place) <= WIN)
    ) | (jnp.logical_not(live_slots)[:, None] & (key_slot == slot_index[:, None]))
    bias = jnp.where(allowed, 0.0, MASKED).astype(f32)
    cosine, sine = rotary_tables(query_pos)
    cosine, sine = (jnp.concatenate([t[:, 0], t[:, 0]], axis=1) for t in (cosine, sine))
    front = (jnp.arange(PAIR) % HD < HD // 2)[None, :]
    sin_a, sin_b = jnp.where(front, -sine, 0.0), jnp.where(front, 0.0, sine)
    chosen = (place[AT_CHIP : AT_CHIP + 16][None, :] == jnp.arange(CHIPS)[:, None]).astype(f32)
    flat = jnp.concatenate([piece[:, 144:, :24] for piece in mine_one]).astype(f32)
    flat = jnp.concatenate([flat[:, row] for row in (0, 8, 1, 9)], axis=1)
    flat = jnp.sum(chosen[:, :, None] * flat[None], axis=1)
    gain_a, gain_m = flat[:, :48].reshape(1, D), flat[:, 48:].reshape(1, D)
    query, pairs, first, weight = call(
        project_kernel,
        [((SLOTS, D), bf16), ((SLOTS, 2 * D), bf16), ((SLOTS, D), bf16), ((3 * D, D), bf16)],
        [],
        [place, tokens, gain_a, cosine, sin_a, sin_b] + blocks_one,
        6,
        8,
    )
    shard = jnp.concatenate([w_up.T, w_out.T, w_down.T[:, :D]])
    rest = w_down.T[:, D:]
    low, high = shard[:, :HALF], shard[:, HALF:]
    own = jnp.concatenate([jnp.where(core == 0, low, high), rest[:8]])
    got = permute(jnp.concatenate([jnp.where(core == 0, high, low), rest[:8]]), sibling)
    tail = jnp.where(
        core == 0,
        jnp.concatenate([rest, got[120:128]]),
        jnp.concatenate([rest[8:], jnp.zeros((16, HALF), bf16)]),
    )
    block = jnp.concatenate(interleave(own, got, core, (72, 24, 24)) + [tail])
    block, _ = lax.optimization_barrier((block, lined_one))
    lined_two, _ = lax.optimization_barrier((spread_line(block, line), both_one))
    near_two, far_two = permute(lined_two, near), permute(lined_two, far)
    up = [(i, i + 1) for i in range(31)]
    down = [(i + 1, i) for i in range(31)]
    before = permute(lax.dynamic_slice_in_dim(pairs, live_rows - WIN, WIN, 0), up)
    after = permute(pairs[:WIN], down)
    near_two, pairs = lax.optimization_barrier((near_two, pairs))
    both_two = permute(near_two, far)
    (mixed,) = call(
        attend_kernel,
        [((SLOTS, D), bf16)],
        [((SPAN, 2 * D), bf16)],
        [place, query, pairs, before, after, bias],
        3,
    )
    mine_two = [lined_two, near_two, far_two]
    other_two = [permute(piece, sibling) for piece in mine_two]
    both_two, mixed = lax.optimization_barrier((both_two, mixed))
    blocks_two = mine_two + [both_two] + other_two + [permute(both_two, sibling)]
    block_out, d_after, d_mixed, send, keep = call(
        middle_kernel,
        [((SLOTS, D), bf16), ((SLOTS, D), f32), ((SLOTS, D), bf16), ((CHIPS, ROWS2, HALF), bf16), ((CHIPS, ROWS2, HALF), bf16)],
        [((2 * FF, D), bf16), ((D, D), bf16), ((D, FF), bf16), ((SLOTS, 2 * FF), bf16), ((SLOTS, FF), bf16)]
        + [((CHIPS, ROWS2, HALF), bf16)] * 2,
        [place, tokens, mixed, gain_m, cotangent] + blocks_two,
        14,
        8,
        2,
    )
    d_query, d_own, rim_before, rim_after = call(
        attend_back_kernel,
        [((SLOTS, D), f32), ((SLOTS, 2 * D), f32), ((WIN, 2 * D), bf16), ((WIN, 2 * D), bf16)],
        [((SPAN, 2 * D), bf16), ((SPAN, 2 * D), f32)],
        [place, query, pairs, before, after, bias, d_mixed],
        8,
    )
    from_after = permute(rim_before, down)
    from_before = permute(rim_after, up)
    total = reduce_near(send, keep, wires)
    leaving, staying = total[:8], total[8:]
    leaving, from_after, from_before = lax.optimization_barrier((leaving, from_after, from_before))
    arrived = permute(leaving, near)
    tokens_grad, send_qkv, keep_qkv = call(
        finish_kernel,
        [((SLOTS, D), f32), ((CHIPS, ROWS1, HALF), bf16), ((CHIPS, ROWS1, HALF), bf16)],
        [((SLOTS, 3 * D), bf16), ((SLOTS, 2 * D), f32)],
        [place, tokens, first, gain_a, weight, d_query, d_own, from_before, from_after, cosine, sin_a, sin_b, d_after],
        9,
    )
    total = staying + arrived
    total, send_qkv, keep_qkv = lax.optimization_barrier((total, send_qkv, keep_qkv))
    leaving, staying = total[:4], total[4:]
    arrived = permute(leaving, far)
    total_qkv = reduce_near(send_qkv, keep_qkv, wires)
    leave_qkv, stay_qkv = total_qkv[:8], total_qkv[8:]
    arrived_qkv = permute(leave_qkv, near)
    staying, stay_qkv = lax.optimization_barrier((staying, stay_qkv))
    total = staying + arrived
    last = [permute(total[k], line[k + 1]) for k in range(3)]
    stay_qkv, last[0] = lax.optimization_barrier((stay_qkv, last[0]))
    total_qkv = stay_qkv + arrived_qkv
    arrived_qkv = permute(total_qkv[:4], far)
    total_qkv = total_qkv[4:] + arrived_qkv
    share, total_qkv = lax.optimization_barrier((total[3], total_qkv))
    share = sum_shares(share, last)
    last_qkv = [permute(total_qkv[k], line[k + 1]) for k in range(3)]
    chip = device_index // 2
    lane = 48 * chip - jnp.minimum(48 * chip // 128 * 128, D - HALF) + 24 * core

    def part(block, start, count, whose):
        return lax.dynamic_slice_in_dim(block, start + count * whose, count, 0)

    gain_row = lax.dynamic_slice_in_dim(share[256:264], lane - 24 * core, 48, 1)
    gain_row = jnp.pad(gain_row, ((0, 0), (0, HALF - 48)))
    cuts = ((0, 72), (144, 24), (192, 24))
    theirs = jnp.concatenate(
        [part(share, s, n, 1 - core) for s, n in cuts] + [jnp.where(core == 0, share[264:272], gain_row)]
    )
    own = jnp.concatenate([part(share, s, n, core) for s, n in cuts])
    got = permute(theirs, sibling)
    both = jnp.concatenate(
        [jnp.where(core == 0, own, got[:120]), jnp.where(core == 0, got[:120], own)], axis=1
    )
    last = jnp.where(
        core == 0, share[240:264], jnp.concatenate([got[120:128], share[240:256]])
    )
    up_sum, out_sum = both[:72].T, both[72:96].T
    down_sum = jnp.concatenate([both[96:], last], axis=1).T
    gain_m_sum = jnp.where(core == 0, got[120, :24], gain_row[0, 24:48])
    done = (total_qkv[3], up_sum, out_sum, down_sum, gain_m_sum)
    share, up_sum, out_sum, down_sum, gain_m_sum = lax.optimization_barrier(done)
    share = sum_shares(share, last_qkv)
    got = permute(part(share, 0, 72, 1 - core), sibling)
    own = part(share, 0, 72, core)
    qkv_sum = jnp.concatenate([jnp.where(core == 0, own, got), jnp.where(core == 0, got, own)], axis=1).T
    gain_a_sum = lax.dynamic_slice(share, (144, lane), (1, 24))[0]
    return (block_out, tokens_grad, qkv_sum, out_sum, up_sum, down_sum, gain_a_sum, gain_m_sum)


def solution(mesh):
    plan = fused_body if mesh.shape["fsdp"] == 32 else body
    placed = (
        P("fsdp", None),
        P(None, "fsdp"),
        P(None, "fsdp"),
        P(None, "fsdp"),
        P(None, "fsdp"),
        P("fsdp"),
        P("fsdp"),
        P("fsdp", None),
        P(),
        P(),
    )
    return jax.shard_map(
        plan,
        mesh=mesh,
        in_specs=placed,
        out_specs=(
            P("fsdp", None),
            P("fsdp", None),
            P(None, "fsdp"),
            P(None, "fsdp"),
            P(None, "fsdp"),
            P(None, "fsdp"),
            P("fsdp"),
            P("fsdp"),
        ),
        check_vma=False,
    )
```

```python
import functools
import math

import jax
import jax.numpy as jnp
from jax import lax
from jax.experimental import pallas as pl
from jax.experimental.pallas import tpu as pltpu
from jax.sharding import PartitionSpec as P

D = 768
HEADS = 12
HD = 64
FF = 1152
BLK = 128
WIN = 64


EPSILON = 1e-05
MASKED = -1e30


def with_halo(shard, sides, width):
    for axis, dim in sides:
        peers, length = (lax.axis_size(axis), shard.shape[dim])
        up = [(i, (i + 1) % peers) for i in range(peers - 1)]
        down = [(j, i) for i, j in up]
        last = lax.slice_in_dim(shard, length - width, length, axis=dim)
        initial = lax.slice_in_dim(shard, 0, width, axis=dim)
        before = lax.ppermute(last, axis, up)
        after = lax.ppermute(initial, axis, down)
        shard = jnp.concatenate([before, shard, after], axis=dim)
    return shard


def norm_parts(values):
    center = values - jnp.mean(values, axis=-1, keepdims=True)
    factor = lax.rsqrt(jnp.mean(center * center, axis=-1, keepdims=True) + EPSILON)
    return (center * factor, factor)


def norm_back(grad_normed, normed, factor):
    return factor * (
        grad_normed
        - jnp.mean(grad_normed, axis=-1, keepdims=True)
        - normed * jnp.mean(grad_normed * normed, axis=-1, keepdims=True)
    )


def sequence_places(places, lengths):
    ends = jnp.cumsum(lengths)
    starts = ends - lengths
    segment = jnp.sum((places[:, None] >= ends[None, :]).astype(jnp.int32), axis=1)
    picked = segment[:, None] == jnp.arange(lengths.shape[0], dtype=jnp.int32)[None, :]
    start = jnp.sum(jnp.where(picked, starts[None, :], 0), axis=1)
    return (segment, places - start)


def rotary_tables(position):
    half = HD // 2
    freq = jnp.power(10000.0, -(jnp.arange(half, dtype=jnp.float32) * (2.0 / HD)))
    angle = position.astype(jnp.float32)[:, None] * freq[None, :]
    angle = jnp.concatenate([angle, angle], axis=1)[:, None, :]
    return (jnp.cos(angle), jnp.sin(angle))


def rotate_heads(values, cosine, sine):
    half = HD // 2
    turned = jnp.concatenate([-values[..., half:], values[..., :half]], axis=-1)
    return values * cosine + turned * sine


def rotate_back(grads, cosine, sine):
    half = HD // 2
    spun = grads * sine
    return grads * cosine + jnp.concatenate([spun[..., half:], -spun[..., :half]], axis=-1)


def rows_product(left, right):
    return lax.dot_general(
        left, right, (((0,), (0,)), ((), ())), preferred_element_type=jnp.float32
    )


def cols_product(left, right):
    return lax.dot_general(
        left, right, (((1,), (1,)), ((), ())), preferred_element_type=jnp.float32
    )


def exact_gelu(values):
    return jax.nn.gelu(values, approximate=False)


def masked_scores(query, key_heads, allowed, score_scale):
    raw_scores = (
        jnp.einsum("qhd,khd->hqk", query, key_heads, preferred_element_type=jnp.float32)
        * score_scale
    )
    return jnp.where(allowed[None], raw_scores, MASKED)


def column_term(grad_side, data_side):
    return rows_product(grad_side, data_side)


def permute(values, pairs):
    return lax.ppermute(values, "fsdp", pairs)


def links():
    sibling = [(i, i ^ 1) for i in range(32)]
    near = [(i, i ^ (2 if i & 1 else 4)) for i in range(32)]
    far = [(i, i ^ (4 if i & 1 else 2)) for i in range(32)]
    line = [[(i, (i + 8 * k) % 32) for i in range(32)] for k in range(4)]
    return (sibling, near, far, line)


def chip_place():
    me = lax.axis_index("fsdp")
    return (me // 8, (me // 4) % 2, (me // 2) % 2, me % 2)


def gather_rows(rows):
    return lax.all_gather(rows, "fsdp", axis=0, tiled=False)


def scatter_rows(terms):
    return lax.psum_scatter(terms, "fsdp", scatter_dimension=0, tiled=False).astype(jnp.float32)


def fold_pad(shard):
    count = shard.shape[-2]
    rest = shard[..., D:]
    half = (count + 1) // 2
    left, right = rest[..., :half, :], rest[..., half:, :]
    spare = [(0, 0)] * (shard.ndim - 2) + [(0, 2 * half - count), (0, 0)]
    rest = jnp.concatenate([left, jnp.pad(right, spare)], axis=-1)
    return jnp.concatenate([shard[..., :D], rest], axis=-2)


def unfold_pad(packed, count):
    half, lanes = (count + 1) // 2, FF - D
    rest = packed[..., count : count + half, :]
    rest = jnp.concatenate([rest[..., :lanes], rest[..., lanes:]], axis=-2)[..., :count, :]
    return jnp.concatenate([packed[..., :count, :], rest], axis=-1)


def body(
    tokens, w_qkv, w_out, w_up, w_down, gain_attn, gain_mlp, cotangent, block_counts, seq_lengths
):
    slot_total = tokens.shape[0]
    score_scale = 1.0 / math.sqrt(HD)
    device_index = lax.axis_index("fsdp")
    block_count = lax.dynamic_index_in_dim(block_counts, device_index, keepdims=False)
    device_ids = jnp.arange(block_counts.shape[0], dtype=jnp.int32)
    first_place = jnp.sum(jnp.where(device_ids < device_index, block_counts, 0)) * BLK
    live_rows = block_count * BLK
    stream_total = jnp.sum(block_counts) * BLK
    slot_index = jnp.arange(slot_total, dtype=jnp.int32)
    live_slots = slot_index < live_rows
    rim_offsets = jnp.arange(WIN, dtype=jnp.int32)
    query_place = first_place + slot_index
    before_place = first_place - WIN + rim_offsets
    after_place = first_place + live_rows + rim_offsets
    key_place = jnp.concatenate([before_place, query_place, after_place])
    key_live = jnp.concatenate([before_place >= 0, live_slots, after_place < stream_total])
    key_slot = jnp.concatenate([rim_offsets * 0 - 1, slot_index, rim_offsets * 0 - 1])
    query_seg, query_pos = sequence_places(query_place, seq_lengths)
    key_seg, unused = sequence_places(key_place, seq_lengths)
    in_window = jnp.abs(query_place[:, None] - key_place[None, :]) <= WIN
    allowed = live_slots[:, None] & key_live[None, :] & (
        query_seg[:, None] == key_seg[None, :]
    ) & in_window | jnp.logical_not(live_slots)[:, None] & (
        key_slot[None, :] == slot_index[:, None]
    )
    cosine, sine = rotary_tables(query_pos)
    peers = lax.axis_size("fsdp")
    columns = D // peers
    gains = jnp.zeros((8, D), jnp.bfloat16)
    gains = gains.at[0, :columns].set(gain_attn).at[1, :columns].set(gain_mlp)
    first_rows = gather_rows(jnp.concatenate([w_qkv.T, gains]))
    qkv_full = first_rows[:, : 3 * columns].reshape(3 * D, D)
    gain_a_full = first_rows[:, 3 * columns, :columns].reshape(D)
    gain_m_full = first_rows[:, 3 * columns + 1, :columns].reshape(D)
    up_columns = w_up.shape[1]
    later = jnp.concatenate([w_up.T, w_out.T, fold_pad(w_down.T)])
    later_rows = gather_rows(later)
    up_full = later_rows[:, :up_columns].reshape(2 * FF, D)
    out_full = later_rows[:, up_columns : up_columns + columns].reshape(D, D)
    down_full = unfold_pad(later_rows[:, up_columns + columns :], columns).reshape(D, FF)
    stream = tokens.astype(jnp.float32)
    normed_one, factor_one = norm_parts(stream)
    first_in = (normed_one * gain_a_full.astype(jnp.float32)).astype(jnp.bfloat16)
    joined = cols_product(first_in, qkv_full)
    query = rotate_heads(joined[:, :D].reshape(slot_total, HEADS, HD), cosine, sine).astype(
        jnp.bfloat16
    )
    keys_own = rotate_heads(
        joined[:, D : 2 * D].reshape(slot_total, HEADS, HD), cosine, sine
    ).astype(jnp.bfloat16)
    values_own = joined[:, 2 * D :].astype(jnp.bfloat16)
    pairs = jnp.concatenate([keys_own.reshape(slot_total, D), values_own], axis=1)
    edges = jnp.concatenate(
        [pairs[:WIN], lax.dynamic_slice_in_dim(pairs, live_rows - WIN, WIN, 0)], axis=0
    )
    framed = with_halo(edges, (("fsdp", 0),), WIN)
    all_pairs = jnp.concatenate([framed[:WIN], pairs, framed[3 * WIN :]], axis=0)
    key_heads = all_pairs[:, :D].reshape(-1, HEADS, HD)
    value_heads = all_pairs[:, D:].reshape(-1, HEADS, HD)
    scores = masked_scores(query, key_heads, allowed, score_scale)
    row_top = jnp.max(scores, axis=-1, keepdims=True)
    log_total = row_top + jnp.log(jnp.sum(jnp.exp(scores - row_top), axis=-1, keepdims=True))
    probs_low = jnp.exp(scores - log_total).astype(jnp.bfloat16)
    mixed = (
        jnp.einsum("hqk,khd->qhd", probs_low, value_heads, preferred_element_type=jnp.float32)
        .reshape(slot_total, D)
        .astype(jnp.bfloat16)
    )
    after_attn = stream + cols_product(mixed, out_full)
    normed_two, factor_two = norm_parts(after_attn)
    second_in = (normed_two * gain_m_full.astype(jnp.float32)).astype(jnp.bfloat16)
    projected = cols_product(second_in, up_full)
    gate_half = projected[:, FF:]
    activated, gelu_pull = jax.vjp(exact_gelu, projected[:, :FF])
    hidden = (activated * gate_half).astype(jnp.bfloat16)
    down_out = cols_product(hidden, down_full)
    block_out = jnp.where(live_slots[:, None], after_attn + down_out, 0.0).astype(jnp.bfloat16)
    out_grad = jnp.where(live_slots[:, None], cotangent, jnp.zeros_like(cotangent))
    d_hidden = jnp.dot(out_grad, down_full, preferred_element_type=jnp.float32)
    d_inputs = gelu_pull(d_hidden * gate_half)[0]
    d_projected = jnp.concatenate([d_inputs, d_hidden * activated], axis=1).astype(jnp.bfloat16)
    d_second = jnp.dot(d_projected, up_full, preferred_element_type=jnp.float32)
    grad_gain_m = jnp.sum(normed_two * d_second, axis=0)
    d_after = out_grad.astype(jnp.float32) + norm_back(
        d_second * gain_m_full.astype(jnp.float32), normed_two, factor_two
    )
    d_attn = d_after.astype(jnp.bfloat16)
    d_mixed = jnp.dot(d_attn, out_full, preferred_element_type=jnp.float32).astype(jnp.bfloat16).reshape(slot_total, HEADS, HD)
    scores = masked_scores(query, key_heads, allowed, score_scale)
    probs = jnp.exp(scores - log_total)
    d_probs = jnp.einsum("qhd,khd->hqk", d_mixed, value_heads, preferred_element_type=jnp.float32)
    d_scores = (probs * (d_probs - jnp.sum(probs * d_probs, axis=-1, keepdims=True))).astype(
        jnp.bfloat16
    )
    d_query = (
        jnp.einsum("hqk,khd->qhd", d_scores, key_heads, preferred_element_type=jnp.float32)
        * score_scale
    )
    d_keys = (
        jnp.einsum("hqk,qhd->khd", d_scores, query, preferred_element_type=jnp.float32)
        * score_scale
    )
    d_values = jnp.einsum(
        "hqk,qhd->khd", probs.astype(jnp.bfloat16), d_mixed, preferred_element_type=jnp.float32
    )
    d_pairs = jnp.concatenate([d_keys.reshape(-1, D), d_values.reshape(-1, D)], axis=1)
    grad_edges = jnp.concatenate([d_pairs[:WIN], d_pairs[WIN + slot_total :]], axis=0)
    returned = with_halo(grad_edges.astype(jnp.bfloat16), (("fsdp", 0),), WIN).astype(
        grad_edges.dtype
    )
    own_pairs = d_pairs[WIN : WIN + slot_total]
    own_pairs = own_pairs.at[:WIN].add(returned[:WIN])
    tail_rows = lax.dynamic_slice_in_dim(own_pairs, live_rows - WIN, WIN, 0) + returned[3 * WIN :]
    own_pairs = lax.dynamic_update_slice_in_dim(own_pairs, tail_rows, live_rows - WIN, 0)
    d_query_raw = rotate_back(d_query, cosine, sine).reshape(slot_total, D)
    d_keys_raw = rotate_back(own_pairs[:, :D].reshape(slot_total, HEADS, HD), cosine, sine).reshape(
        slot_total, D
    )
    d_joined = jnp.concatenate([d_query_raw, d_keys_raw, own_pairs[:, D:]], axis=1).astype(
        jnp.bfloat16
    )
    d_first = jnp.dot(d_joined, qkv_full, preferred_element_type=jnp.float32)
    grad_gain_a = jnp.sum(normed_one * d_first, axis=0)
    d_stream = d_after + norm_back(
        d_first * gain_a_full.astype(jnp.float32), normed_one, factor_one
    )
    tokens_grad = jnp.where(live_slots[:, None], d_stream, 0.0)
    down_terms = column_term(out_grad, hidden).astype(jnp.bfloat16).reshape(peers, columns, FF)
    up_terms = column_term(d_projected, second_in).astype(jnp.bfloat16)
    mlp_sum = scatter_rows(
        jnp.concatenate([up_terms.reshape(peers, up_columns, D), fold_pad(down_terms)], axis=1)
    )
    up_sum = mlp_sum[:up_columns].T
    down_sum = unfold_pad(mlp_sum[up_columns:], columns).T
    qkv_terms = column_term(d_joined, first_in).astype(jnp.bfloat16).reshape(peers, 3 * columns, D)
    out_terms = column_term(d_attn, mixed).astype(jnp.bfloat16).reshape(peers, columns, D)
    gain_terms = jnp.stack([grad_gain_a.reshape(peers, columns), grad_gain_m.reshape(peers, columns)], axis=1)
    gain_terms = jnp.pad(gain_terms.astype(jnp.bfloat16), ((0, 0), (0, 6), (0, D - columns)))
    attn_sum = scatter_rows(jnp.concatenate([qkv_terms, out_terms, gain_terms], axis=1))
    qkv_sum = attn_sum[: 3 * columns].T
    out_sum = attn_sum[3 * columns : 4 * columns].T
    gain_a_sum = attn_sum[4 * columns, :columns]
    gain_m_sum = attn_sum[4 * columns + 1, :columns]
    return (block_out, tokens_grad, qkv_sum, out_sum, up_sum, down_sum, gain_a_sum, gain_m_sum)


CHIPS = 16
HALF = 384
ROWS1 = 160
ROWS2 = 272
SLOTS = 256
SPAN = SLOTS + 2 * WIN
PAIR = 2 * HD
PAIRS = HEADS // 2
LIMIT = 48 * 1024 * 1024
AT_LIVE, AT_CORE, AT_CHIP, AT_PUT = 0, 1, 2, 34
VMEM = pltpu.MemorySpace.VMEM
SMEM = pltpu.MemorySpace.SMEM


def nt_dot(left, right):
    return lax.dot_general(left, right, (((1,), (1,)), ((), ())), preferred_element_type=jnp.float32)


def nn_dot(left, right):
    return jnp.dot(left, right, preferred_element_type=jnp.float32)


def tn_dot(left, right):
    return lax.dot_general(left, right, (((0,), (0,)), ((), ())), preferred_element_type=jnp.float32)


def call(kernel, outs, scratch, args, micros, blocks=0, away=0):
    whole = len(args) - blocks - 1
    spaces = [pl.BlockSpec(memory_space=SMEM)] + [pl.BlockSpec(memory_space=VMEM)] * whole
    spaces += [pl.BlockSpec(memory_space=pl.ANY)] * blocks
    semaphores = [pltpu.SemaphoreType.DMA((2 * CHIPS, 4))] if blocks else []
    semaphores += [pltpu.SemaphoreType.DMA((8,))] if away else []
    near_outs = len(outs) - away
    return pl.pallas_call(
        kernel,
        out_shape=[jax.ShapeDtypeStruct(shape, kind) for shape, kind in outs],
        in_specs=spaces,
        out_specs=[pl.BlockSpec(memory_space=VMEM)] * near_outs + [pl.BlockSpec(memory_space=pl.ANY)] * away,
        scratch_shapes=[pltpu.VMEM(shape, kind) for shape, kind in scratch] + semaphores,
        compiler_params=pltpu.CompilerParams(vmem_limit_bytes=LIMIT),
        cost_estimate=pl.CostEstimate(flops=0, bytes_accessed=3_690_000 * micros, transcendentals=0),
    )(*args)


def block_copies(place, refs, weight, done, kind, start, count):
    copies = []
    for slot in range(2 * CHIPS):
        chip = place[AT_CHIP + slot]
        core = place[AT_CORE] if slot < CHIPS else 1 - place[AT_CORE]
        rows = pl.ds(pl.multiple_of(chip * count, 16), count)
        lanes = pl.ds(pl.multiple_of(core * HALF, 128), HALF)
        source = refs[slot // 4].at[slot % 4, start : start + count, :]
        copies.append(pltpu.make_async_copy(source, weight.at[rows, lanes], done.at[slot, kind]))
    return copies


def rest_copies(place, refs, weight, done, core):
    copies = []
    for slot in range(2 * CHIPS):
        stream = core if slot < CHIPS else 1 - core
        count = 32 if stream == 0 else 16
        first = pl.multiple_of(place[AT_CHIP + slot] * 48 + (0 if stream == 0 else 32), 16)
        source = refs[slot // 4].at[slot % 4, 240 : 240 + count, :]
        copies.append(
            pltpu.make_async_copy(source, weight.at[pl.ds(first, count), 2 * HALF :], done.at[slot, 3])
        )
    return copies


def go(copies):
    for copy in copies:
        copy.start()


def land(copies):
    for copy in copies:
        copy.wait()


def put_rows(place, send, keep, stream, start, value, chips):
    count = value.shape[0] // len(chips)
    value = value.astype(jnp.bfloat16)

    def store(ref):
        for i, chip in enumerate(chips):
            slot = place[AT_PUT + 16 * stream + chip]
            ref[slot, start : start + count, :] = value[i * count : (i + 1) * count]

    pl.when(place[AT_CORE] == stream)(lambda: store(keep))
    pl.when(place[AT_CORE] != stream)(lambda: store(send))


def put_both(place, send, keep, start, value, chips):
    for stream in (0, 1):
        put_rows(place, send, keep, stream, start, value[:, HALF * stream : HALF * (stream + 1)], chips)


def gain_rows(vector, chip):
    start = min(48 * chip // 128 * 128, D - HALF)
    return jnp.broadcast_to(vector[:, start : start + HALF], (16, HALF))


def project_kernel(place, tokens, gain, cos, sin_a, sin_b, *rest):
    refs, (query, pairs, first, weight, done) = rest[:8], rest[8:]
    copies = block_copies(place, refs, weight, done, 0, 0, 144)
    go(copies)
    normed, _ = norm_parts(tokens[...].astype(jnp.float32))
    a1 = (normed * gain[...]).astype(jnp.bfloat16)
    first[...] = a1
    c, sa, sb = cos[...], sin_a[...], sin_b[...]
    land(copies)
    for part in range(3):
        for j in range(1):
            joined = nt_dot(a1, weight[part * D : (part + 1) * D, :])
            for p in range(PAIRS):
                lanes = slice(PAIR * p, PAIR * (p + 1))
                v = joined[:, lanes]
                if part < 2:
                    v = v * c + pltpu.roll(v, 96, 1) * sa + pltpu.roll(v, 32, 1) * sb
                if part == 0:
                    query[:, lanes] = v.astype(jnp.bfloat16)
                else:
                    where = slice((part - 1) * D + lanes.start, (part - 1) * D + lanes.stop)
                    pairs[:, where] = v.astype(jnp.bfloat16)


def frame_pairs(place, pairs, before, after, framed):
    framed[0:WIN, :] = before[...]
    framed[WIN : WIN + SLOTS, :] = pairs[...]
    framed[WIN + SLOTS : SPAN, :] = jnp.zeros((WIN, 2 * D), jnp.bfloat16)
    framed[pl.ds(pl.multiple_of(WIN + place[AT_LIVE], 64), WIN), :] = after[...]


def stack_heads(values, low, high):
    return jnp.concatenate([values * low, values * high], axis=0)


def head_masks():
    lane = lax.broadcasted_iota(jnp.int32, (1, PAIR), 1)
    low = jnp.where(lane < HD, 1.0, 0.0).astype(jnp.bfloat16)
    return (lane < HD, low, 1.0 - low)


def probabilities(query, keys, bias):
    scores = nt_dot(query, keys) * (1.0 / math.sqrt(HD)) + bias
    expos = jnp.exp(scores - jnp.max(scores, axis=-1, keepdims=True))
    return expos * (1.0 / jnp.sum(expos, axis=-1, keepdims=True))


def attend_kernel(place, query, pairs, before, after, bias, mixed, framed):
    frame_pairs(place, pairs, before, after, framed)
    is_low, low, high = head_masks()
    for block in range(2):
        rows, keys = slice(128 * block, 128 * block + 128), slice(128 * block, 128 * block + 256)
        both = jnp.concatenate([bias[rows, :], bias[rows, :]], axis=0)
        for p in range(PAIRS):
            lanes, vlanes = slice(PAIR * p, PAIR * (p + 1)), slice(D + PAIR * p, D + PAIR * (p + 1))
            probs = probabilities(stack_heads(query[rows, lanes], low, high), framed[keys, lanes], both)
            out = nn_dot(probs.astype(jnp.bfloat16), framed[keys, vlanes])
            mixed[rows, lanes] = jnp.where(is_low, out[:128], out[128:]).astype(jnp.bfloat16)


def middle_kernel(place, tokens, mixed, gain, cotangent, *rest):
    refs = rest[:8]
    (block_out, d_after_out, d_mixed, send_out, keep_out, w_up, w_out, w_down, d_proj, hidden, send, keep, done, sent) = rest[8:]

    def leave(start, count, kind):
        rows = (slice(None), slice(start, start + count), slice(None))
        pairs = ((send, send_out), (keep, keep_out))
        return [pltpu.make_async_copy(a.at[rows], b.at[rows], sent.at[kind + i]) for i, (a, b) in enumerate(pairs)]

    out_copies = block_copies(place, refs, w_out, done, 0, 144, 48)
    up_copies = block_copies(place, refs, w_up, done, 1, 0, 144)
    down_copies = block_copies(place, refs, w_down, done, 2, 192, 48)
    go(out_copies)
    go(up_copies)
    go(down_copies)
    for core in (0, 1):
        pl.when(place[AT_CORE] == core)(lambda: go(rest_copies(place, refs, w_down, done, core)))
    land(out_copies)
    after_attn = tokens[...].astype(jnp.float32) + nt_dot(mixed[...], w_out[...])
    normed, factor = norm_parts(after_attn)
    gains = gain[...]
    a2 = (normed * gains).astype(jnp.bfloat16)
    live = lax.broadcasted_iota(jnp.int32, (SLOTS, 1), 0) < place[AT_LIVE]
    grad = jnp.where(live, cotangent[...].astype(jnp.float32), 0.0)
    out_grad = grad.astype(jnp.bfloat16)
    down = jnp.zeros((SLOTS, D), jnp.float32)
    land(up_copies)
    land(down_copies)
    for core in (0, 1):
        pl.when(place[AT_CORE] == core)(lambda: land(rest_copies(place, refs, w_down, done, core)))
    for j in range(3):
        lanes = slice(HALF * j, HALF * (j + 1))
        inputs = nt_dot(a2, w_up[lanes, :])
        gate = nt_dot(a2, w_up[FF + HALF * j : FF + HALF * (j + 1), :])
        cdf = 0.5 * (1.0 + lax.erf(inputs * (1.0 / math.sqrt(2.0))))
        slope = cdf + inputs * (jnp.exp(-0.5 * inputs * inputs) * (1.0 / math.sqrt(2.0 * math.pi)))
        active = inputs * cdf
        low_hidden = (active * gate).astype(jnp.bfloat16)
        hidden[:, lanes] = low_hidden
        down = down + nt_dot(low_hidden, w_down[:, lanes])
        d_hidden = nn_dot(out_grad, w_down[:, lanes])
        d_proj[:, lanes] = (d_hidden * gate * slope).astype(jnp.bfloat16)
        d_proj[:, FF + HALF * j : FF + HALF * (j + 1)] = (d_hidden * active).astype(jnp.bfloat16)
    block_out[...] = jnp.where(live, after_attn + down, 0.0).astype(jnp.bfloat16)
    everyone = list(range(CHIPS))
    for j in range(2):
        up = tn_dot(d_proj[:, FF * j : FF * (j + 1)], a2)
        put_both(place, send, keep, 0, up, everyone[8 * j : 8 * j + 8])
    up_leave = leave(0, 144, 0)
    go(up_leave)
    down_grad = tn_dot(out_grad, hidden[...])
    put_both(place, send, keep, 192, down_grad, everyone)
    rest = down_grad[:, 2 * HALF :]
    for chip in everyone:
        put_rows(place, send, keep, 0, 240, rest[48 * chip : 48 * chip + 32], [chip])
        put_rows(place, send, keep, 1, 240, rest[48 * chip + 32 : 48 * chip + 48], [chip])
    down_leave = leave(192, 64, 2)
    go(down_leave)
    d_second = nn_dot(d_proj[...], w_up[...])
    gain_grad = jnp.sum(normed * d_second, axis=0, keepdims=True)
    d_after = grad + norm_back(d_second * gains, normed, factor)
    d_after_out[...] = d_after
    d_attn = d_after.astype(jnp.bfloat16)
    d_mixed[...] = nn_dot(d_attn, w_out[...]).astype(jnp.bfloat16)
    put_both(place, send, keep, 144, tn_dot(d_attn, mixed[...]), everyone)
    for chip in everyone:
        put_rows(place, send, keep, 1, 256, gain_rows(gain_grad, chip), [chip])
    out_leave, gain_leave = leave(144, 48, 4), leave(256, 16, 6)
    go(out_leave + gain_leave)
    land(up_leave + down_leave + out_leave + gain_leave)


def attend_back_kernel(
    place, query, pairs, before, after, bias, d_mixed,
    d_query, d_own, rim_before, rim_after, framed, d_framed,
):
    frame_pairs(place, pairs, before, after, framed)
    is_low, low, high = head_masks()
    d_framed[256:SPAN, :] = jnp.zeros((SPAN - 256, 2 * D), jnp.float32)
    scale = 1.0 / math.sqrt(HD)
    for block in range(2):
        rows, keys = slice(128 * block, 128 * block + 128), slice(128 * block, 128 * block + 256)
        both = jnp.concatenate([bias[rows, :], bias[rows, :]], axis=0)
        for p in range(PAIRS):
            lanes, vlanes = slice(PAIR * p, PAIR * (p + 1)), slice(D + PAIR * p, D + PAIR * (p + 1))
            q2 = stack_heads(query[rows, lanes], low, high)
            o2 = stack_heads(d_mixed[rows, lanes], low, high)
            k2 = framed[keys, lanes]
            probs = probabilities(q2, k2, both)
            d_probs = nt_dot(o2, framed[keys, vlanes])
            spread = jnp.sum(probs * d_probs, axis=-1, keepdims=True)
            d_scores = (probs * (d_probs - spread)).astype(jnp.bfloat16)
            d_q = nn_dot(d_scores, k2) * scale
            d_query[rows, lanes] = jnp.where(is_low, d_q[:128], d_q[128:])
            d_k = tn_dot(d_scores, q2) * scale
            d_v = tn_dot(probs.astype(jnp.bfloat16), o2)
            if block == 0:
                d_framed[keys, lanes] = d_k
                d_framed[keys, vlanes] = d_v
            else:
                d_framed[keys, lanes] += d_k
                d_framed[keys, vlanes] += d_v
    rim_before[...] = d_framed[0:WIN, :].astype(jnp.bfloat16)
    tail = pl.ds(pl.multiple_of(WIN + place[AT_LIVE], 64), WIN)
    rim_after[...] = d_framed[tail, :].astype(jnp.bfloat16)
    d_own[...] = d_framed[WIN : WIN + SLOTS, :]


def finish_kernel(
    place, tokens, first, gain, weight, d_query, d_own, from_before, from_after, cos, sin_a, sin_b, d_after,
    tokens_grad, send, keep, d_joined, d_pairs,
):
    live = lax.broadcasted_iota(jnp.int32, (SLOTS, 1), 0) < place[AT_LIVE]
    d_pairs[...] = jnp.where(live, d_own[...], 0.0)
    d_pairs[0:WIN, :] += from_before[...].astype(jnp.float32)
    tail = pl.ds(pl.multiple_of(place[AT_LIVE] - WIN, 64), WIN)
    d_pairs[tail, :] += from_after[...].astype(jnp.float32)
    c, sa, sb = cos[...], sin_a[...], sin_b[...]
    for part in range(2):
        source = d_query if part == 0 else d_pairs
        for p in range(PAIRS):
            v = source[:, PAIR * p : PAIR * (p + 1)]
            v = v * c - pltpu.roll(v, 96, 1) * sa - pltpu.roll(v, 32, 1) * sb
            d_joined[:, part * D + PAIR * p : part * D + PAIR * (p + 1)] = v.astype(jnp.bfloat16)
    d_joined[:, 2 * D :] = d_pairs[:, D:].astype(jnp.bfloat16)
    d_first = nn_dot(d_joined[...], weight[...])
    normed, factor = norm_parts(tokens[...].astype(jnp.float32))
    gain_grad = jnp.sum(normed * d_first, axis=0, keepdims=True)
    d_stream = d_after[...] + norm_back(d_first * gain[...], normed, factor)
    tokens_grad[...] = jnp.where(live, d_stream, 0.0)
    everyone = list(range(CHIPS))
    for j in range(2):
        up = tn_dot(d_joined[:, 1152 * j : 1152 * (j + 1)], first[...])
        put_both(place, send, keep, 0, up, everyone[8 * j : 8 * j + 8])
    for chip in everyone:
        for stream in (0, 1):
            put_rows(place, send, keep, stream, 144, gain_rows(gain_grad, chip), [chip])


def swap_halves(shard, core, sibling):
    low, high = shard[:, :HALF], shard[:, HALF:]
    own = jnp.where(core == 0, low, high)
    return own, permute(jnp.where(core == 0, high, low), sibling)


def interleave(own, got, core, cuts):
    parts, start = [], 0
    for count in cuts:
        mine, theirs = own[start : start + count], got[start : start + count]
        parts += [jnp.where(core == 0, mine, theirs), jnp.where(core == 0, theirs, mine)]
        start += count
    return parts


def spread_line(block, line):
    return jnp.stack([block] + [permute(block, line[k]) for k in (1, 2, 3)])


def reduce_near(send, keep, links_of):
    return keep + permute(send, links_of[0])


def sum_shares(own, others):
    share = own.astype(jnp.float32)
    for other in others:
        share = share + other.astype(jnp.float32)
    return share


def place_table(live_rows):
    z, y, x, core = chip_place()
    slots = jnp.arange(CHIPS, dtype=jnp.int32)
    zr, nr, fr = slots % 4, slots // 4 % 2, slots // 8
    held = []
    for own in (True, False):
        along_y = (core == 0) if own else (core == 1)
        yr, xr = jnp.where(along_y, nr, fr), jnp.where(along_y, fr, nr)
        held.append((z - zr) % 4 * 4 + (y ^ yr) * 2 + (x ^ xr))
    zz, yy, xx = slots // 4, slots // 2 % 2, slots % 2
    yr, xr = y ^ yy, x ^ xx
    put = []
    for n, f in ((yr, xr), (xr, yr)):
        put.append((1 - n) * 8 + (1 - f) * 4 + (zz - z + 3) % 4)
    head = jnp.stack([live_rows, core]).astype(jnp.int32)
    return jnp.concatenate([head] + held + put).astype(jnp.int32)


def fused_body(
    tokens, w_qkv, w_out, w_up, w_down, gain_attn, gain_mlp, cotangent, block_counts, seq_lengths
):
    bf16, f32 = jnp.bfloat16, jnp.float32
    device_index = lax.axis_index("fsdp")
    core = device_index % 2
    wires = links()
    sibling, near, far, line = wires
    gains = jnp.zeros((8, D), bf16)
    gain_pair = jnp.pad(jnp.stack([gain_attn, gain_mlp]), ((0, 6), (0, HALF - 24)))
    gains = jnp.concatenate([gain_pair, gain_pair], axis=1)
    own, got = swap_halves(jnp.concatenate([w_qkv.T, gains]), core, sibling)
    block = jnp.concatenate(interleave(own, got, core, (72, 8)))
    lined_one = spread_line(block, line)
    near_one, far_one = permute(lined_one, near), permute(lined_one, far)
    both_one = permute(near_one, far)
    mine_one = [lined_one, near_one, far_one, both_one]
    blocks_one = mine_one + [permute(piece, sibling) for piece in mine_one]
    block_counts, seq_lengths, _ = lax.optimization_barrier((block_counts, seq_lengths, lined_one))
    block_count = lax.dynamic_index_in_dim(block_counts, device_index, keepdims=False)
    device_ids = jnp.arange(block_counts.shape[0], dtype=jnp.int32)
    first_place = jnp.sum(jnp.where(device_ids < device_index, block_counts, 0)) * BLK
    live_rows = block_count * BLK
    stream_total = jnp.sum(block_counts) * BLK
    place = place_table(live_rows)
    slot_index = jnp.arange(SLOTS, dtype=jnp.int32)
    live_slots = slot_index < live_rows
    query_place = first_place + slot_index
    query_seg, query_pos = sequence_places(query_place, seq_lengths)
    key_slot = (slot_index // BLK * BLK)[:, None] + jnp.arange(256, dtype=jnp.int32)[None, :] - WIN
    key_place = first_place + key_slot
    ends = jnp.cumsum(seq_lengths)
    key_seg = jnp.sum((key_place[:, :, None] >= ends).astype(jnp.int32), axis=2)
    allowed = (
        live_slots[:, None]
        & (key_place >= 0)
        & (key_place < stream_total)
        & (query_seg[:, None] == key_seg)
        & (jnp.abs(query_place[:, None] - key_place) <= WIN)
    ) | (jnp.logical_not(live_slots)[:, None] & (key_slot == slot_index[:, None]))
    bias = jnp.where(allowed, 0.0, MASKED).astype(f32)
    cosine, sine = rotary_tables(query_pos)
    cosine, sine = (jnp.concatenate([t[:, 0], t[:, 0]], axis=1) for t in (cosine, sine))
    front = (jnp.arange(PAIR) % HD < HD // 2)[None, :]
    sin_a, sin_b = jnp.where(front, -sine, 0.0), jnp.where(front, 0.0, sine)
    chosen = (place[AT_CHIP : AT_CHIP + 16][None, :] == jnp.arange(CHIPS)[:, None]).astype(f32)
    flat = jnp.concatenate([piece[:, 144:, :24] for piece in mine_one]).astype(f32)
    flat = jnp.concatenate([flat[:, row] for row in (0, 8, 1, 9)], axis=1)
    flat = jnp.sum(chosen[:, :, None] * flat[None], axis=1)
    gain_a, gain_m = flat[:, :48].reshape(1, D), flat[:, 48:].reshape(1, D)
    query, pairs, first, weight = call(
        project_kernel,
        [((SLOTS, D), bf16), ((SLOTS, 2 * D), bf16), ((SLOTS, D), bf16), ((3 * D, D), bf16)],
        [],
        [place, tokens, gain_a, cosine, sin_a, sin_b] + blocks_one,
        6,
        8,
    )
    shard = jnp.concatenate([w_up.T, w_out.T, w_down.T[:, :D]])
    rest = w_down.T[:, D:]
    low, high = shard[:, :HALF], shard[:, HALF:]
    own = jnp.concatenate([jnp.where(core == 0, low, high), rest[:8]])
    got = permute(jnp.concatenate([jnp.where(core == 0, high, low), rest[:8]]), sibling)
    tail = jnp.where(
        core == 0,
        jnp.concatenate([rest, got[120:128]]),
        jnp.concatenate([rest[8:], jnp.zeros((16, HALF), bf16)]),
    )
    block = jnp.concatenate(interleave(own, got, core, (72, 24, 24)) + [tail])
    block, _ = lax.optimization_barrier((block, lined_one))
    lined_two, _ = lax.optimization_barrier((spread_line(block, line), both_one))
    near_two, far_two = permute(lined_two, near), permute(lined_two, far)
    up = [(i, i + 1) for i in range(31)]
    down = [(i + 1, i) for i in range(31)]
    before = permute(lax.dynamic_slice_in_dim(pairs, live_rows - WIN, WIN, 0), up)
    after = permute(pairs[:WIN], down)
    near_two, pairs = lax.optimization_barrier((near_two, pairs))
    both_two = permute(near_two, far)
    (mixed,) = call(
        attend_kernel,
        [((SLOTS, D), bf16)],
        [((SPAN, 2 * D), bf16)],
        [place, query, pairs, before, after, bias],
        3,
    )
    mine_two = [lined_two, near_two, far_two]
    other_two = [permute(piece, sibling) for piece in mine_two]
    both_two, mixed = lax.optimization_barrier((both_two, mixed))
    blocks_two = mine_two + [both_two] + other_two + [permute(both_two, sibling)]
    block_out, d_after, d_mixed, send, keep = call(
        middle_kernel,
        [((SLOTS, D), bf16), ((SLOTS, D), f32), ((SLOTS, D), bf16), ((CHIPS, ROWS2, HALF), bf16), ((CHIPS, ROWS2, HALF), bf16)],
        [((2 * FF, D), bf16), ((D, D), bf16), ((D, FF), bf16), ((SLOTS, 2 * FF), bf16), ((SLOTS, FF), bf16)]
        + [((CHIPS, ROWS2, HALF), bf16)] * 2,
        [place, tokens, mixed, gain_m, cotangent] + blocks_two,
        14,
        8,
        2,
    )
    d_query, d_own, rim_before, rim_after = call(
        attend_back_kernel,
        [((SLOTS, D), f32), ((SLOTS, 2 * D), f32), ((WIN, 2 * D), bf16), ((WIN, 2 * D), bf16)],
        [((SPAN, 2 * D), bf16), ((SPAN, 2 * D), f32)],
        [place, query, pairs, before, after, bias, d_mixed],
        8,
    )
    from_after = permute(rim_before, down)
    from_before = permute(rim_after, up)
    total = reduce_near(send, keep, wires)
    leaving, staying = total[:8], total[8:]
    leaving, from_after, from_before = lax.optimization_barrier((leaving, from_after, from_before))
    arrived = permute(leaving, near)
    tokens_grad, send_qkv, keep_qkv = call(
        finish_kernel,
        [((SLOTS, D), f32), ((CHIPS, ROWS1, HALF), bf16), ((CHIPS, ROWS1, HALF), bf16)],
        [((SLOTS, 3 * D), bf16), ((SLOTS, 2 * D), f32)],
        [place, tokens, first, gain_a, weight, d_query, d_own, from_before, from_after, cosine, sin_a, sin_b, d_after],
        9,
    )
    total = staying + arrived
    total, send_qkv, keep_qkv = lax.optimization_barrier((total, send_qkv, keep_qkv))
    leaving, staying = total[:4], total[4:]
    arrived = permute(leaving, far)
    total_qkv = reduce_near(send_qkv, keep_qkv, wires)
    leave_qkv, stay_qkv = total_qkv[:8], total_qkv[8:]
    arrived_qkv = permute(leave_qkv, near)
    staying, stay_qkv = lax.optimization_barrier((staying, stay_qkv))
    total = staying + arrived
    last = [permute(total[k], line[k + 1]) for k in range(3)]
    stay_qkv, last[0] = lax.optimization_barrier((stay_qkv, last[0]))
    total_qkv = stay_qkv + arrived_qkv
    arrived_qkv = permute(total_qkv[:4], far)
    total_qkv = total_qkv[4:] + arrived_qkv
    share, total_qkv = lax.optimization_barrier((total[3], total_qkv))
    share = sum_shares(share, last)
    last_qkv = [permute(total_qkv[k], line[k + 1]) for k in range(3)]
    chip = device_index // 2
    lane = 48 * chip - jnp.minimum(48 * chip // 128 * 128, D - HALF) + 24 * core

    def part(block, start, count, whose):
        return lax.dynamic_slice_in_dim(block, start + count * whose, count, 0)

    gain_row = lax.dynamic_slice_in_dim(share[256:264], lane - 24 * core, 48, 1)
    gain_row = jnp.pad(gain_row, ((0, 0), (0, HALF - 48)))
    cuts = ((0, 72), (144, 24), (192, 24))
    theirs = jnp.concatenate(
        [part(share, s, n, 1 - core) for s, n in cuts] + [jnp.where(core == 0, share[264:272], gain_row)]
    )
    own = jnp.concatenate([part(share, s, n, core) for s, n in cuts])
    got = permute(theirs, sibling)
    both = jnp.concatenate(
        [jnp.where(core == 0, own, got[:120]), jnp.where(core == 0, got[:120], own)], axis=1
    )
    last = jnp.where(
        core == 0, share[240:264], jnp.concatenate([got[120:128], share[240:256]])
    )
    up_sum, out_sum = both[:72].T, both[72:96].T
    down_sum = jnp.concatenate([both[96:], last], axis=1).T
    gain_m_sum = jnp.where(core == 0, got[120, :24], gain_row[0, 24:48])
    done = (total_qkv[3], up_sum, out_sum, down_sum, gain_m_sum)
    share, up_sum, out_sum, down_sum, gain_m_sum = lax.optimization_barrier(done)
    share = sum_shares(share, last_qkv)
    got = permute(part(share, 0, 72, 1 - core), sibling)
    own = part(share, 0, 72, core)
    qkv_sum = jnp.concatenate([jnp.where(core == 0, own, got), jnp.where(core == 0, got, own)], axis=1).T
    gain_a_sum = lax.dynamic_slice(share, (144, lane), (1, 24))[0]
    return (block_out, tokens_grad, qkv_sum, out_sum, up_sum, down_sum, gain_a_sum, gain_m_sum)


def solution(mesh):
    plan = fused_body if mesh.shape["fsdp"] == 32 else body
    placed = (
        P("fsdp", None),
        P(None, "fsdp"),
        P(None, "fsdp"),
        P(None, "fsdp"),
        P(None, "fsdp"),
        P("fsdp"),
        P("fsdp"),
        P("fsdp", None),
        P(),
        P(),
    )
    return jax.shard_map(
        plan,
        mesh=mesh,
        in_specs=placed,
        out_specs=(
            P("fsdp", None),
            P("fsdp", None),
            P(None, "fsdp"),
            P(None, "fsdp"),
            P(None, "fsdp"),
            P(None, "fsdp"),
            P("fsdp"),
            P("fsdp"),
        ),
        check_vma=False,
    )
```
